128 devices in a mesh: inner: 8 (over z_hi, x), outer: 16 (over z_lo, y, core).
Axes of the slice: x: 4, y: 4, z: 4 (z_hi: 2, z_lo: 2; z = z_hi * 2 + z_lo), core: 2. Of those that a mesh axis runs over, the one named last changes fastest.
Arguments:
- image_embed: bfloat16 [16384, 768], P(('inner', 'outer')), may hold values from -80 to 80
- text_embed: bfloat16 [16384, 768], P(('inner', 'outer')), may hold values from -32 to 32
Outputs:
- mean_loss: float32 [], replicated
- image_grad: float32 [16384, 768], P(('inner', 'outer'))
- text_grad: float32 [16384, 768], P(('inner', 'outer'))
The draws below stay inside these ranges and needn't reach their ends.
All inputs are finite; a program needn't handle non-finite values.
Results may differ from the reference program's by a relative error of at most 0.0023.
Values may be sent and summed in bfloat16 or wider, within the bound.
A program may use at most 192 MiB of HBM per device.

```python
import math
import jax
import jax.numpy as jnp
from jax import lax

EMBED = 768
BATCH = 16384


def text_rows(key):
    key_a = jax.random.fold_in(key, 0)
    key_c = jax.random.fold_in(key, 2)
    index = jnp.arange(BATCH)
    spread = jnp.exp(jax.random.uniform(key_c, (BATCH,), minval=math.log(0.5), maxval=math.log(2.0)))
    drift = 1.0 + 2.0 * index.astype(jnp.float32) / BATCH
    factor = spread * drift
    base = jax.random.truncated_normal(key_a, -5.0, 5.0, (BATCH, EMBED))
    values = base * factor[:, None]
    return values


def draw_text_embed(key, part):
    values = text_rows(key)
    return values.astype(jnp.bfloat16)


def draw_image_embed(key, part):
    key = jax.random.fold_in(key, 11)
    key_a = jax.random.fold_in(key, 0)
    key_c = jax.random.fold_in(key, 2)
    index = jnp.arange(BATCH)
    spread = jnp.exp(jax.random.uniform(key_c, (BATCH,), minval=math.log(0.5), maxval=math.log(2.0)))
    factor = spread * (1.0 + 2.0 * index.astype(jnp.float32) / BATCH)
    values = jax.random.truncated_normal(key_a, -5.0, 5.0, (BATCH, EMBED)) * factor[:, None]
    return values.astype(jnp.bfloat16)


def setup_inputs(seed: int = 0) -> dict:
    arg_keys = jax.random.split(jax.random.key(seed), 3)
    return {
        "image_embed": draw_image_embed(jax.random.fold_in(arg_keys[2], 71), 0),
        "text_embed": draw_text_embed(jax.random.fold_in(arg_keys[2], 71), 0),
    }


def reference(image_embed, text_embed):
    score_scale = EMBED ** -0.5
    block_size = math.gcd(BATCH, 512)
    block_count = BATCH // block_size

    def lse_rows(left, right):
        def per_block(portion):
            scores = score_scale * jnp.dot(portion, right.T, preferred_element_type=jnp.float32)
            row_top = jnp.max(scores, 1)
            return row_top + jnp.log(jnp.sum(jnp.exp(scores - row_top[:, None]), 1))
        return lax.map(per_block, left.reshape(block_count, block_size, EMBED)).reshape(BATCH)

    row_lse = lse_rows(image_embed, text_embed)
    col_lse = lse_rows(text_embed, image_embed)
    positive = score_scale * jnp.sum(image_embed.astype(jnp.float32) * text_embed.astype(jnp.float32), 1)
    mean_loss = (jnp.sum(row_lse - positive) + jnp.sum(col_lse - positive)) / (2.0 * BATCH)

    def grads(left, right, own_lse, other_lse):
        def per_block(items):
            portion, partner, lse_part = items
            scores = score_scale * jnp.dot(portion, right.T, preferred_element_type=jnp.float32)
            weights = (jnp.exp(scores - lse_part[:, None]) + jnp.exp(scores - other_lse[None, :])).astype(jnp.bfloat16)
            summed = jnp.dot(weights, right, preferred_element_type=jnp.float32)
            return score_scale * 0.5 * (summed - 2.0 * partner.astype(jnp.float32))
        parts = (left.reshape(block_count, block_size, EMBED), right.reshape(block_count, block_size, EMBED), own_lse.reshape(block_count, block_size))
        return lax.map(per_block, parts).reshape(BATCH, EMBED)

    image_grad = grads(image_embed, text_embed, row_lse, col_lse)
    text_grad = grads(text_embed, image_embed, col_lse, row_lse)
    return mean_loss, image_grad, text_grad
```

```python
import jax
import jax.numpy as jnp
from jax import lax
from jax.sharding import PartitionSpec as P


def on_device(image_embed, text_embed):
    shard_rows, embed_width = image_embed.shape
    score_scale = embed_width ** (-0.5)
    total_rows = shard_rows * lax.axis_size("inner") * lax.axis_size("outer")

    images = lax.all_gather(image_embed, "inner", axis=0, tiled=True)
    texts = lax.all_gather(text_embed, "outer", axis=0, tiled=True)
    scores = score_scale * jnp.einsum(
        "re,ce->rc", images, texts, preferred_element_type=jnp.float32
    )

    def lse(axis, name):
        top = jnp.max(scores, axis)
        total = jnp.sum(jnp.exp(scores - jnp.expand_dims(top, axis)), axis)
        parts = lax.all_gather(jnp.stack([top, total]), name, axis=0)
        tops, totals = parts[:, 0], parts[:, 1]
        top = jnp.max(tops, 0)
        return top + jnp.log(jnp.sum(totals * jnp.exp(tops - top), 0))

    row_lse = lse(1, "inner")
    col_lse = lse(0, "outer")
    weights = (
        jnp.exp(scores - row_lse[:, None]) + jnp.exp(scores - col_lse[None, :])
    ).astype(jnp.bfloat16)
    image_part = jnp.dot(weights, texts, preferred_element_type=jnp.float32)
    text_part = lax.dot_general(
        weights, images, (((0,), (0,)), ((), ())), preferred_element_type=jnp.float32
    )
    image_sum = lax.psum_scatter(image_part, "inner", scatter_dimension=0, tiled=True)
    text_sum = lax.psum_scatter(text_part, "outer", scatter_dimension=0, tiled=True)

    row_own = lax.dynamic_slice_in_dim(
        row_lse, lax.axis_index("inner") * shard_rows, shard_rows
    )
    col_own = lax.dynamic_slice_in_dim(
        col_lse, lax.axis_index("outer") * shard_rows, shard_rows
    )
    positive = score_scale * jnp.sum(
        image_embed.astype(jnp.float32) * text_embed.astype(jnp.float32), 1
    )
    loss_part = jnp.sum(row_own - positive) + jnp.sum(col_own - positive)
    mean_loss = lax.psum(loss_part, ("inner", "outer")) / (2.0 * total_rows)
    image_grad = score_scale * 0.5 * (image_sum - 2.0 * text_embed.astype(jnp.float32))
    text_grad = score_scale * 0.5 * (text_sum - 2.0 * image_embed.astype(jnp.float32))
    return (mean_loss, image_grad, text_grad)


def solution(mesh):
    return jax.shard_map(
        on_device,
        mesh=mesh,
        in_specs=(P(("inner", "outer"), None), P(("inner", "outer"), None)),
        out_specs=(P(), P(("inner", "outer"), None), P(("inner", "outer"), None)),
        check_vma=False,
    )
```

```python
import functools
import math

import jax
import jax.numpy as jnp
from jax import lax
from jax.experimental import pallas as pl
from jax.experimental.pallas import tpu as pltpu
from jax.sharding import PartitionSpec as P

F32, BF16 = jnp.float32, jnp.bfloat16
MESH = pl.DeviceIdType.MESH
OFFSETS = ((0, 0), (0, 1), (0, 3), (0, 2), (1, 0), (1, 1), (1, 3), (1, 2))
RING = 4
SLOTS = 8
LOG2E = math.log2(math.e)


class Group:
    def __init__(self, axis, plane, place, core):
        self.axis, self.plane, self.place, self.core = axis, plane, place, core

    def index(self, plane_step, ring_step, core_step=0):
        chip = lax.rem(self.plane + plane_step, 2) * RING + lax.rem(
            self.place + ring_step, RING
        )
        if self.axis == "inner":
            return chip
        return chip * 2 + lax.rem(self.core + core_step, 2)

    def device(self, plane_step, ring_step, core_step=0):
        return {self.axis: self.index(plane_step, ring_step, core_step)}


def kernel(
    image_ref,
    text_ref,
    loss_ref,
    image_out,
    text_out,
    image_rows,
    text_rows,
    scores,
    row_top,
    row_sum,
    col_top,
    col_sum,
    row_stats,
    col_stats,
    row_lse,
    col_lse,
    row_wide,
    col_wide,
    w_own,
    w_other,
    w_got,
    image_part,
    text_part,
    image_send,
    text_send,
    image_half,
    text_half,
    image_full,
    text_full,
    image_plane,
    text_plane,
    row_loss,
    col_loss,
    gather_send,
    gather_recv,
    fwd_send,
    fwd_recv,
    row_ssem,
    row_rsem,
    col_ssem,
    col_rsem,
    rloss_ssem,
    rloss_rsem,
    closs_ssem,
    closs_rsem,
    w_ssem,
    w_rsem,
    red_ssem,
    red_rsem,
):
    block, width = image_ref.shape
    half = block // 2
    pair = 2 * block
    scale = width ** (-0.5)
    inner, outer = lax.axis_index("inner"), lax.axis_index("outer")
    core = lax.rem(outer, 2)
    out_chip = outer // 2
    groups = (
        Group("inner", inner // RING, lax.rem(inner, RING), core),
        Group("outer", out_chip // RING, lax.rem(out_chip, RING), core),
    )
    sibling = {"outer": groups[1].index(0, 0, 1)}
    own = (image_ref, text_ref)
    rows = (image_rows, text_rows)

    def remote(src, dst, ssem, rsem, device):
        return pltpu.make_async_remote_copy(
            src_ref=src,
            dst_ref=dst,
            send_sem=ssem,
            recv_sem=rsem,
            device_id=device,
            device_id_type=MESH,
        )

    inner_peers = [groups[0].device(*o) for o in OFFSETS[1:]]
    outer_peers = [
        groups[1].device(*o, c) for o in OFFSETS for c in (0, 1) if (o, c) != ((0, 0), 0)
    ]

    barrier = pltpu.get_barrier_semaphore()
    for device in inner_peers + outer_peers:
        pl.semaphore_signal(barrier, inc=1, device_id=device, device_id_type=MESH)
    pl.semaphore_wait(barrier, len(inner_peers) + len(outer_peers))

    def at(kind, core_step, slot, part=None):
        start, size = slot * block, block
        if part is not None:
            start, size = start + part * half, half
        return rows[kind].at[core_step, pl.ds(start, size), :]

    ARRIVE = {1: 0, 2: 1, 4: 2, 5: 3, 6: 4, (3, 0): 5, (3, 1): 6, (7, 0): 7, (7, 1): 8}

    def copy(kind, src, slot, offset, part=None):
        key = slot if part is None else (slot, part)
        n = ARRIVE[key]
        return remote(
            src,
            at(kind, 0, slot, part),
            gather_send.at[kind, n],
            gather_recv.at[kind, n],
            groups[kind].device(*offset),
        )

    RIGHT, LEFT, PARTNER = (0, 1), (0, 3), (1, 0)

    def gather_copies(kind):
        return {
            2: copy(kind, own[kind], 2, RIGHT),
            1: copy(kind, own[kind], 1, LEFT),
            4: copy(kind, own[kind], 4, PARTNER),
            (3, 0): copy(kind, at(kind, 0, 2, 0), 3, RIGHT, 0),
            (3, 1): copy(kind, at(kind, 0, 1, 1), 3, LEFT, 1),
            6: copy(kind, at(kind, 0, 4), 6, RIGHT),
            5: copy(kind, at(kind, 0, 4), 5, LEFT),
            (7, 0): copy(kind, at(kind, 0, 6, 0), 7, RIGHT, 0),
            (7, 1): copy(kind, at(kind, 0, 5, 1), 7, LEFT, 1),
        }

    def fwd(kind, slot):
        return remote(
            own[kind] if slot == 0 else at(kind, 0, slot),
            at(kind, 1, slot),
            fwd_send.at[kind, slot],
            fwd_recv.at[kind, slot],
            sibling,
        )

    copies = [gather_copies(kind) for kind in (0, 1)]
    fwds = [[fwd(kind, slot) for slot in range(SLOTS)] for kind in (0, 1)]

    def start(*keys):
        for key in keys:
            for kind in (0, 1):
                copies[kind][key].start()

    def arrived(*keys):
        for key in keys:
            for kind in (0, 1):
                copies[kind][key].wait_recv()

    def forward(*slots):
        for slot in slots:
            for kind in (0, 1):
                fwds[kind][slot].start()

    start(2, 1, 4)
    forward(0)

    for kind in (0, 1):
        rows[kind][0, pl.ds(0, block), :] = own[kind][...]
    row_top[...] = jnp.full(row_top.shape, -1e30, F32)
    row_sum[...] = jnp.zeros(row_sum.shape, F32)
    col_top[...] = jnp.full(col_top.shape, -1e30, F32)
    col_sum[...] = jnp.zeros(col_sum.shape, F32)
    product = image_ref[...].astype(F32) * text_ref[...].astype(F32)
    positive = scale * jnp.sum(product, 0, keepdims=True)
    positive = sum(positive[:, i : i + 128] for i in range(0, width, 128))

    def unit(a, b):
        image = image_rows[0, pl.ds(pl.multiple_of(a * pair, pair), pair), :]
        here = pl.ds(pl.multiple_of(a * pair, pair), pair)
        for c in (0, 1):
            text = text_rows[c, pl.ds(pl.multiple_of(b * pair, pair), pair), :]
            there = pl.ds(pl.multiple_of((2 * b + c) * pair, pair), pair)
            value = (scale * LOG2E) * lax.dot_general(
                image, text, (((1,), (1,)), ((), ())), preferred_element_type=F32
            )
            scores[a, 2 * b + c] = value
            old = row_top[here, :]
            top = jnp.maximum(old, jnp.max(value, 1, keepdims=True))
            total = jnp.sum(jnp.exp2(value - jnp.concatenate([top, top], 1)), 1, keepdims=True)
            row_sum[here, :] = row_sum[here, :] * jnp.exp2(old - top) + total
            row_top[here, :] = top
            old = col_top[:, there]
            top = jnp.maximum(old, jnp.max(value, 0, keepdims=True))
            total = jnp.sum(jnp.exp2(value - top), 0, keepdims=True)
            col_sum[:, there] = col_sum[:, there] * jnp.exp2(old - top) + total
            col_top[:, there] = top

    def shell(n):
        def body(j, carry):
            a = jnp.where(j <= n, n, j - n - 1)
            b = jnp.where(j <= n, j, n)
            unit(a, b)
            return carry

        lax.fori_loop(0, 2 * n + 1, body, 0)

    def sib_arrived(*slots):
        for slot in slots:
            for kind in (0, 1):
                fwds[kind][slot].wait_recv()

    arrived(1)
    start((3, 1))
    forward(1)
    arrived(2)
    start((3, 0))
    forward(2)
    arrived(4)
    start(6, 5)
    forward(4)
    sib_arrived(0, 1)
    shell(0)
    arrived((3, 0), (3, 1))
    forward(3)
    sib_arrived(2, 3)
    shell(1)
    arrived(5)
    start((7, 1))
    forward(5)
    arrived(6)
    start((7, 0))
    forward(6)
    sib_arrived(4, 5)
    shell(2)
    arrived((7, 0), (7, 1))
    forward(7)
    sib_arrived(6, 7)
    shell(3)

    for slot, offset in enumerate(OFFSETS):
        i = groups[0].index(*offset)
        r = pl.ds(slot * block, block)
        row_stats[inner, pl.ds(i, 1), :] = jnp.transpose(row_top[r, :])[0:1]
        row_stats[inner, pl.ds(i + SLOTS, 1), :] = jnp.transpose(row_sum[r, :])[0:1]
        for c in (0, 1):
            o = groups[1].index(*offset, c)
            k = pl.ds((slot // 2) * 2 * pair + c * pair + (slot % 2) * block, block)
            col_stats[outer, pl.ds(o, 1), :] = col_top[:, k]
            col_stats[outer, pl.ds(o + 2 * SLOTS, 1), :] = col_sum[:, k]
    row_stats[inner, pl.ds(2 * SLOTS, 8), :] = jnp.concatenate(
        [positive, jnp.zeros((7, 128), F32)], 0
    )

    def spread(ref, me, ssem, rsem, peers):
        out = [
            remote(ref.at[me], ref.at[me], ssem.at[n], rsem.at[me], device)
            for n, device in enumerate(peers)
        ]
        for c in out:
            c.start()
        return out

    def collect(ref, rsem, me, count, out):
        def body(n, carry):
            who = lax.rem(me + n, count)
            remote(
                ref.at[who], ref.at[who], out_ssem0(out), rsem.at[who], sibling
            ).wait_recv()
            return carry

        lax.fori_loop(1, count, body, 0)

    def out_ssem0(out):
        return out

    row_out = spread(row_stats, inner, row_ssem, row_rsem, inner_peers)
    col_out = spread(col_stats, outer, col_ssem, col_rsem, outer_peers)
    collect(row_stats, row_rsem, inner, SLOTS, row_ssem.at[0])
    collect(col_stats, col_rsem, outer, 2 * SLOTS, col_ssem.at[0])

    def combine(ref, count):
        tops = [ref[n, 0:count, :] for n in range(count)]
        top = functools.reduce(jnp.maximum, tops)
        total = sum(
            ref[n, count : 2 * count, :] * jnp.exp2(tops[n] - top) for n in range(count)
        )
        return top + LOG2E * jnp.log(total)

    row_value = combine(row_stats, SLOTS)
    col_value = combine(col_stats, 2 * SLOTS)
    row_lse[...] = row_value
    col_lse[...] = col_value
    paired = sum(row_stats[n, 2 * SLOTS : 2 * SLOTS + 8, :] for n in range(SLOTS))
    row_loss[outer] = row_value * (1.0 / LOG2E) - 2.0 * paired
    col_loss[inner] = (col_value[0:8] + col_value[8:16]) * (1.0 / LOG2E)
    rloss_out = spread(row_loss, outer, rloss_ssem, rloss_rsem, outer_peers)
    closs_out = spread(col_loss, inner, closs_ssem, closs_rsem, inner_peers)

    for slot, offset in enumerate(OFFSETS):
        i = groups[0].index(*offset)
        line = row_lse[pl.ds(i, 1), :]
        row_wide[pl.ds(slot * block, block), :] = jnp.transpose(
            jnp.broadcast_to(line, (block, block))
        )
        for c in (0, 1):
            o = groups[1].index(*offset, c)
            k = pl.ds((slot // 2) * 2 * pair + c * pair + (slot % 2) * block, block)
            col_wide[:, k] = col_lse[pl.ds(o, 1), :]

    def w_copy(a):
        r = pl.ds(pl.multiple_of(a * pair, pair), pair)
        return remote(
            w_other.at[r, :], w_got.at[r, :], w_ssem.at[a], w_rsem.at[a], sibling
        )

    def weigh(a, carry):
        r = pl.ds(pl.multiple_of(a * pair, pair), pair)
        line = row_wide[r, :]
        line = jnp.concatenate([line, line], 1)

        def body(b, inner_carry):
            k = pl.ds(pl.multiple_of(b * pair, pair), pair)
            for c, out in ((0, w_own), (1, w_other)):
                value = scores[a, 2 * b + c]
                there = pl.ds(pl.multiple_of((2 * b + c) * pair, pair), pair)
                weight = jnp.exp2(value - line) + jnp.exp2(value - col_wide[:, there])
                out[r, k] = weight.astype(BF16)
            return inner_carry

        lax.fori_loop(0, 4, body, 0)
        w_copy(a).start()
        return carry

    lax.fori_loop(0, 4, weigh, 0)

    parts = (image_part, text_part)
    sends = (image_send, text_send)
    halves = (image_half, text_half)
    fulls = (image_full, text_full)
    planes = (image_plane, text_plane)

    def lines(slot, part=None):
        if part is None:
            return pl.ds(slot * block, block)
        return pl.ds(slot * block + part * half, half)

    def red(kind, n, src, dst, offset):
        return remote(
            src, dst, red_ssem.at[kind, n], red_rsem.at[kind, n], groups[kind].device(*offset)
        )

    def red_copies(kind):
        out = {}
        for p in (0, 1):
            far, right, left = 4 * p + 3, 4 * p + 1, 4 * p + 2
            s, h, f = sends[kind], halves[kind], fulls[kind]
            out["far0", p] = red(kind, 4 * p, s.at[lines(far, 0), :], h.at[p, 0], RIGHT)
            out["far1", p] = red(kind, 4 * p + 1, s.at[lines(far, 1), :], h.at[p, 1], LEFT)
            out["right", p] = red(kind, 4 * p + 2, s.at[lines(right), :], f.at[p, 0], RIGHT)
            out["left", p] = red(kind, 4 * p + 3, s.at[lines(left), :], f.at[p, 1], LEFT)
        out["plane"] = red(kind, 8, parts[kind].at[lines(4), :], planes[kind].at[...], PARTNER)
        return out

    reds = [red_copies(kind) for kind in (0, 1)]

    def far(kind, p):
        sends[kind][lines(4 * p + 3), :] = parts[kind][lines(4 * p + 3), :].astype(BF16)
        reds[kind]["far0", p].start()
        reds[kind]["far1", p].start()

    def near(kind, p):
        right, left = 4 * p + 1, 4 * p + 2
        part, send, got = parts[kind], sends[kind], halves[kind]
        send[lines(right, 1), :] = part[lines(right, 1), :].astype(BF16)
        send[lines(left, 0), :] = part[lines(left, 0), :].astype(BF16)
        reds[kind]["far0", p].wait_recv()
        send[lines(right, 0), :] = (part[lines(right, 0), :] + got[p, 0].astype(F32)).astype(BF16)
        reds[kind]["right", p].start()
        reds[kind]["far1", p].wait_recv()
        send[lines(left, 1), :] = (part[lines(left, 1), :] + got[p, 1].astype(F32)).astype(BF16)
        reds[kind]["left", p].start()

    def ring_sum(kind, p):
        reds[kind]["right", p].wait_recv()
        reds[kind]["left", p].wait_recv()
        return (
            parts[kind][lines(4 * p), :]
            + fulls[kind][p, 0].astype(F32)
            + fulls[kind][p, 1].astype(F32)
        )

    def partial(step, carry):
        g = 3 - step
        r = pl.ds(pl.multiple_of(g * pair, pair), pair)
        image_part[r, :] = jnp.dot(
            w_own[r, :], text_rows[0], preferred_element_type=F32
        ) + jnp.dot(w_other[r, :], text_rows[1], preferred_element_type=F32)

        for s in range(4):

            @pl.when(step == s)
            def _():
                if s % 2 == 0:
                    far(0, 1 - s // 2)
                else:
                    near(0, 1 - s // 2)
                if s == 0:
                    for a in range(4):
                        w_copy(a).wait_recv()

        text_part[r, :] = lax.dot_general(
            w_own[:, r], image_rows[0], (((0,), (0,)), ((), ())), preferred_element_type=F32
        ) + lax.dot_general(
            w_got[:, r], image_rows[1], (((0,), (0,)), ((), ())), preferred_element_type=F32
        )

        for s in range(4):

            @pl.when(step == s)
            def _():
                if s % 2 == 0:
                    far(1, 1 - s // 2)
                else:
                    near(1, 1 - s // 2)

        return carry

    lax.fori_loop(0, 4, partial, 0)

    for kind in (0, 1):
        parts[kind][lines(4), :] = ring_sum(kind, 1)
        reds[kind]["plane"].start()

    collect(row_loss, rloss_rsem, outer, 2 * SLOTS, rloss_ssem.at[0])
    collect(col_loss, closs_rsem, inner, SLOTS, closs_ssem.at[0])
    loss = sum(row_loss[n] for n in range(2 * SLOTS)) + sum(
        col_loss[n] for n in range(SLOTS)
    )
    loss = jnp.sum(jnp.sum(loss, 0, keepdims=True), 1, keepdims=True)
    total_rows = block * 2 * SLOTS * SLOTS
    loss_ref[...] = jnp.broadcast_to(loss / (2.0 * total_rows), loss_ref.shape)

    for kind, out, other in ((0, image_out, text_ref), (1, text_out, image_ref)):
        value = ring_sum(kind, 0)
        reds[kind]["plane"].wait_recv()
        value = value + planes[kind][...]
        out[...] = (scale * 0.5) * (value - 2.0 * other[...].astype(F32))

    for kind in (0, 1):
        for c in copies[kind].values():
            c.wait_send()
        for c in fwds[kind]:
            c.wait_send()
        for c in reds[kind].values():
            c.wait_send()
    for a in range(4):
        w_copy(a).wait_send()
    for c in row_out + col_out + rloss_out + closs_out:
        c.wait_send()


def on_device(image_embed, text_embed):
    block, width = image_embed.shape
    group = SLOTS * block
    dma = pltpu.SemaphoreType.DMA
    shape = jax.ShapeDtypeStruct
    vmem = pl.BlockSpec(memory_space=pltpu.VMEM)
    loss, image_grad, text_grad = pl.pallas_call(
        kernel,
        out_shape=(
            shape((8, 128), F32),
            shape((block, width), F32),
            shape((block, width), F32),
        ),
        in_specs=[vmem, vmem],
        out_specs=(vmem, vmem, vmem),
        scratch_shapes=[
            pltpu.VMEM((2, group, width), BF16),
            pltpu.VMEM((2, group, width), BF16),
            pltpu.VMEM((4, 8, 2 * block, 2 * block), F32),
            pltpu.VMEM((group, 128), F32),
            pltpu.VMEM((group, 128), F32),
            pltpu.VMEM((1, 2 * group), F32),
            pltpu.VMEM((1, 2 * group), F32),
            pltpu.VMEM((SLOTS, 3 * SLOTS, 128), F32),
            pltpu.VMEM((2 * SLOTS, 4 * SLOTS, 128), F32),
            pltpu.VMEM((SLOTS, 128), F32),
            pltpu.VMEM((2 * SLOTS, 128), F32),
            pltpu.VMEM((group, 128), F32),
            pltpu.VMEM((1, 2 * group), F32),
            pltpu.VMEM((group, group), BF16),
            pltpu.VMEM((group, group), BF16),
            pltpu.VMEM((group, group), BF16),
            pltpu.VMEM((group, width), F32),
            pltpu.VMEM((group, width), F32),
            pltpu.VMEM((group, width), BF16),
            pltpu.VMEM((group, width), BF16),
            pltpu.VMEM((2, 2, block // 2, width), BF16),
            pltpu.VMEM((2, 2, block // 2, width), BF16),
            pltpu.VMEM((2, 2, block, width), BF16),
            pltpu.VMEM((2, 2, block, width), BF16),
            pltpu.VMEM((block, width), F32),
            pltpu.VMEM((block, width), F32),
            pltpu.VMEM((2 * SLOTS, 8, 128), F32),
            pltpu.VMEM((SLOTS, 8, 128), F32),
            dma((2, 9)),
            dma((2, 9)),
            dma((2, SLOTS)),
            dma((2, SLOTS)),
            dma((SLOTS,)),
            dma((SLOTS,)),
            dma((2 * SLOTS,)),
            dma((2 * SLOTS,)),
            dma((2 * SLOTS,)),
            dma((2 * SLOTS,)),
            dma((SLOTS,)),
            dma((SLOTS,)),
            dma((4,)),
            dma((4,)),
            dma((2, 9)),
            dma((2, 9)),
        ],
        compiler_params=pltpu.CompilerParams(
            collective_id=0, has_side_effects=True, vmem_limit_bytes=56 * 2**20
        ),
    )(image_embed, text_embed)
    return loss[0, 0], image_grad, text_grad


def solution(mesh):
    return jax.shard_map(
        on_device,
        mesh=mesh,
        in_specs=(P(("inner", "outer"), None), P(("inner", "outer"), None)),
        out_specs=(P(), P(("inner", "outer"), None), P(("inner", "outer"), None)),
        check_vma=False,
    )
```

```python
import functools
import math

import jax
import jax.numpy as jnp
from jax import lax
from jax.experimental import pallas as pl
from jax.experimental.pallas import tpu as pltpu
from jax.sharding import PartitionSpec as P

F32, BF16 = jnp.float32, jnp.bfloat16
MESH = pl.DeviceIdType.MESH
OFFSETS = ((0, 0), (0, 1), (0, 3), (0, 2), (1, 0), (1, 1), (1, 3), (1, 2))
RING = 4
SLOTS = 8
LOG2E = math.log2(math.e)


class Group:
    def __init__(self, axis, plane, place, core):
        self.axis, self.plane, self.place, self.core = axis, plane, place, core

    def index(self, plane_step, ring_step, core_step=0):
        chip = lax.rem(self.plane + plane_step, 2) * RING + lax.rem(
            self.place + ring_step, RING
        )
        if self.axis == "inner":
            return chip
        return chip * 2 + lax.rem(self.core + core_step, 2)

    def device(self, plane_step, ring_step, core_step=0):
        return {self.axis: self.index(plane_step, ring_step, core_step)}


def kernel(
    image_ref,
    text_ref,
    loss_ref,
    image_out,
    text_out,
    image_rows,
    text_rows,
    scores,
    row_top,
    row_sum,
    col_top,
    col_sum,
    row_stats,
    col_stats,
    row_lse,
    col_lse,
    row_wide,
    col_wide,
    w_own,
    w_other,
    w_got,
    image_part,
    text_part,
    image_send,
    text_send,
    image_half,
    text_half,
    image_full,
    text_full,
    image_plane,
    text_plane,
    loss_out,
    loss_in,
    gather_send,
    gather_recv,
    fwd_send,
    fwd_recv,
    row_ssem,
    row_rsem,
    col_ssem,
    col_rsem,
    loss_ssem,
    loss_rsem,
    w_ssem,
    w_rsem,
    red_ssem,
    red_rsem,
):
    block, width = image_ref.shape
    half, quarter = block // 2, block // 4
    pair = 2 * block
    scale = width ** (-0.5)
    inner, outer = lax.axis_index("inner"), lax.axis_index("outer")
    core = lax.rem(outer, 2)
    out_chip = outer // 2
    groups = (
        Group("inner", inner // RING, lax.rem(inner, RING), core),
        Group("outer", out_chip // RING, lax.rem(out_chip, RING), core),
    )
    sibling = {"outer": groups[1].index(0, 0, 1)}
    own = (image_ref, text_ref)
    rows = (image_rows, text_rows)

    def remote(src, dst, ssem, rsem, device):
        return pltpu.make_async_remote_copy(
            src_ref=src,
            dst_ref=dst,
            send_sem=ssem,
            recv_sem=rsem,
            device_id=device,
            device_id_type=MESH,
        )

    inner_peers = [groups[0].device(*o) for o in OFFSETS[1:]]
    outer_peers = [
        groups[1].device(*o, c) for o in OFFSETS for c in (0, 1) if (o, c) != ((0, 0), 0)
    ]

    RIGHT, LEFT, FAR, PARTNER = (0, 1), (0, 3), (0, 2), (1, 0)
    neighbours = [g.device(*o) for g in groups for o in (RIGHT, LEFT, PARTNER)] + [sibling]

    barrier = pltpu.get_barrier_semaphore()
    for device in neighbours:
        pl.semaphore_signal(barrier, inc=1, device_id=device, device_id_type=MESH)

    row_top[...] = jnp.full(row_top.shape, -1e30, F32)
    row_sum[...] = jnp.zeros(row_sum.shape, F32)
    col_top[...] = jnp.full(col_top.shape, -1e30, F32)
    col_sum[...] = jnp.zeros(col_sum.shape, F32)
    for kind in (0, 1):
        rows[kind][0, pl.ds(0, block), :] = own[kind][...]
    pl.semaphore_wait(barrier, len(neighbours))

    def at(kind, core_step, slot, part=None):
        start, size = slot * block, block
        if part is not None:
            start, size = start + part * half, half
        return rows[kind].at[core_step, pl.ds(start, size), :]

    FILLS = (1, 2, (4, 0), (4, 1), (5, 0), (5, 1), (6, 0), (6, 1), (3, 0), (3, 1), (7, 0), (7, 1))

    def copy(kind, src, fills, offset):
        slot, part = fills if isinstance(fills, tuple) else (fills, None)
        n = FILLS.index(fills)
        return remote(
            src,
            at(kind, 0, slot, part),
            gather_send.at[kind, n],
            gather_recv.at[kind, n],
            groups[kind].device(*offset),
        )

    def gather_copies(kind):
        out = {
            2: copy(kind, own[kind], 2, RIGHT),
            1: copy(kind, own[kind], 1, LEFT),
            (3, 0): copy(kind, at(kind, 0, 2, 0), (3, 0), RIGHT),
            (3, 1): copy(kind, at(kind, 0, 1, 1), (3, 1), LEFT),
            (7, 0): copy(kind, at(kind, 0, 6, 0), (7, 0), RIGHT),
            (7, 1): copy(kind, at(kind, 0, 5, 1), (7, 1), LEFT),
        }
        for h in (0, 1):
            out[4, h] = copy(kind, own[kind].at[pl.ds(h * half, half), :], (4, h), PARTNER)
            out[6, h] = copy(kind, at(kind, 0, 4, h), (6, h), RIGHT)
            out[5, h] = copy(kind, at(kind, 0, 4, h), (5, h), LEFT)
        return out

    def fwd(kind, slot):
        return remote(
            own[kind] if slot == 0 else at(kind, 0, slot),
            at(kind, 1, slot),
            fwd_send.at[kind, slot],
            fwd_recv.at[kind, slot],
            sibling,
        )

    copies = [gather_copies(kind) for kind in (0, 1)]
    fwds = [[fwd(kind, slot) for slot in range(SLOTS)] for kind in (0, 1)]

    def start(*keys):
        for key in keys:
            for kind in (0, 1):
                copies[kind][key].start()

    def arrived(*keys):
        for key in keys:
            for kind in (0, 1):
                copies[kind][key].wait_recv()

    def forward(*slots):
        for slot in slots:
            for kind in (0, 1):
                fwds[kind][slot].start()

    start((4, 0), 2, 1, (4, 1))
    forward(0)

    product = image_ref[...].astype(F32) * text_ref[...].astype(F32)
    positive = scale * jnp.sum(product, 0, keepdims=True)
    positive = sum(positive[:, i : i + 128] for i in range(0, width, 128))

    def multiply(a, b):
        image = image_rows[0, pl.ds(a * pair, pair), :]
        for c in (0, 1):
            text = text_rows[c, pl.ds(b * pair, pair), :]
            scores[a, b, :, pl.ds(c * pair, pair)] = (scale * LOG2E) * lax.dot_general(
                image, text, (((1,), (1,)), ((), ())), preferred_element_type=F32
            )

    def count(a, b):
        step = 32
        k = pl.ds(b * 2 * pair, 2 * pair)
        old = col_top[:, k]
        top = old
        for r in range(0, pair, step):
            value = scores[a, b, pl.ds(r, step), :].reshape(step // 8, 8, 2 * pair)
            top = jnp.maximum(top, jnp.max(value, 0))
        total = col_sum[:, k] * jnp.exp2(old - top)
        for r in range(0, pair, step):
            value = scores[a, b, pl.ds(r, step), :]
            here = pl.ds(a * pair + r, step)
            lanes = [value[:, i : i + 128] for i in range(0, 2 * pair, 128)]
            before = row_top[here, :]
            row = functools.reduce(jnp.maximum, lanes, before)
            row_sum[here, :] = row_sum[here, :] * jnp.exp2(before - row) + sum(
                jnp.exp2(lane - row) for lane in lanes
            )
            row_top[here, :] = row
            value = value.reshape(step // 8, 8, 2 * pair)
            total = total + jnp.sum(jnp.exp2(value - top[None]), 0)
        col_top[:, k] = top
        col_sum[:, k] = total

    waiting = []

    def shell(n):
        for a, b in [(n, j) for j in range(n + 1)] + [(j, n) for j in range(n)]:
            multiply(a, b)
            if waiting:
                count(*waiting.pop())
            waiting.append((a, b))

    def sib_arrived(*slots):
        for slot in slots:
            for kind in (0, 1):
                fwds[kind][slot].wait_recv()

    arrived((4, 0))
    start((6, 0), (5, 0))
    arrived(1)
    start((3, 1))
    forward(1)
    arrived(2)
    start((3, 0))
    forward(2)
    sib_arrived(0, 1)
    shell(0)
    arrived((3, 0), (3, 1))
    forward(3)
    sib_arrived(2, 3)
    arrived((4, 1))
    start((6, 1), (5, 1))
    forward(4)
    shell(1)
    arrived((6, 0))
    start((7, 0))
    arrived((5, 0), (5, 1))
    start((7, 1))
    forward(5)
    arrived((6, 1))
    forward(6)
    sib_arrived(4, 5)
    shell(2)
    arrived((7, 0), (7, 1))
    forward(7)
    sib_arrived(6, 7)
    shell(3)
    count(*waiting.pop())

    for slot, offset in enumerate(OFFSETS):
        i = groups[0].index(*offset)
        r = pl.ds(slot * block, block)
        lanes = jnp.transpose(row_top[r, :])
        top = jnp.max(lanes, 0, keepdims=True)
        total = jnp.sum(jnp.transpose(row_sum[r, :]) * jnp.exp2(lanes - top), 0, keepdims=True)
        row_stats[inner, pl.ds(i, 1), :] = top
        row_stats[inner, pl.ds(i + SLOTS, 1), :] = total
        for c in (0, 1):
            o = groups[1].index(*offset, c)
            k = pl.ds((slot // 2) * 2 * pair + c * pair + (slot % 2) * block, block)
            lanes = col_top[:, k]
            top = jnp.max(lanes, 0, keepdims=True)
            total = jnp.sum(col_sum[:, k] * jnp.exp2(lanes - top), 0, keepdims=True)
            col_stats[outer, pl.ds(o, 1), :] = top
            col_stats[outer, pl.ds(o + 2 * SLOTS, 1), :] = total

    def spread(ref, me, ssem, rsem, peers):
        out = [
            remote(ref.at[me], ref.at[me], ssem.at[n], rsem.at[me], device)
            for n, device in enumerate(peers)
        ]
        for c in out:
            c.start()
        return out

    def collect(ref, ssem, rsem, me, count):
        def body(n, carry):
            who = lax.rem(me + n, count)
            remote(ref.at[who], ref.at[who], ssem.at[0], rsem.at[who], sibling).wait_recv()
            return carry

        lax.fori_loop(1, count, body, 0)

    row_out = spread(row_stats, inner, row_ssem, row_rsem, inner_peers)
    col_out = spread(col_stats, outer, col_ssem, col_rsem, outer_peers)
    collect(row_stats, row_ssem, row_rsem, inner, SLOTS)
    collect(col_stats, col_ssem, col_rsem, outer, 2 * SLOTS)

    def combine(ref, count):
        tops = [ref[n, 0:count, :] for n in range(count)]
        top = functools.reduce(jnp.maximum, tops)
        total = sum(
            ref[n, count : 2 * count, :] * jnp.exp2(tops[n] - top) for n in range(count)
        )
        return top + LOG2E * jnp.log(total)

    row_value = combine(row_stats, SLOTS)
    col_value = combine(col_stats, 2 * SLOTS)
    row_lse[...] = row_value
    col_lse[...] = col_value
    for slot, offset in enumerate(OFFSETS):
        i = groups[0].index(*offset)
        line = row_lse[pl.ds(i, 1), :]
        row_wide[pl.ds(slot * block, block), :] = jnp.transpose(
            jnp.broadcast_to(line, (block, block))
        )
        for c in (0, 1):
            o = groups[1].index(*offset, c)
            k = pl.ds((slot // 2) * 2 * pair + c * pair + (slot % 2) * block, block)
            col_wide[:, k] = col_lse[pl.ds(o, 1), :]

    def w_copy(a):
        r = pl.ds(pl.multiple_of(a * pair, pair), pair)
        return remote(
            w_other.at[r, :], w_got.at[r, :], w_ssem.at[a], w_rsem.at[a], sibling
        )

    def weigh(a, carry):
        r = pl.ds(pl.multiple_of(a * pair, pair), pair)
        line = row_wide[r, :]
        line = jnp.concatenate([line, line], 1)

        for b in range(4):
            for c, out in ((0, w_own), (1, w_other)):
                value = scores[a, b, :, pl.ds(c * pair, pair)]
                there = pl.ds((2 * b + c) * pair, pair)
                weight = jnp.exp2(value - line) + jnp.exp2(value - col_wide[:, there])
                out[r, pl.ds(b * pair, pair)] = weight.astype(BF16)
        w_copy(a).start()
        return carry

    lax.fori_loop(0, 4, weigh, 0)

    def flip(group, bit):
        return group.device(0, 2) if bit else group.device(0, 1 + 2 * lax.rem(group.place, 2))

    others = [sibling, groups[1].device(*PARTNER), groups[0].device(*PARTNER)] + [
        flip(group, bit) for group in groups for bit in (0, 1)
    ]
    loss_copies = [
        remote(loss_out.at[n], loss_in.at[n], loss_ssem.at[n], loss_rsem.at[n], device)
        for n, device in enumerate(others)
    ]

    def loss_step(n):
        if n == 0:
            both = row_lse[pl.ds(inner, 1), :] + col_lse[pl.ds(outer, 1), :]
            both = both * (1.0 / LOG2E) - 2.0 * positive
            value = jnp.concatenate([both, jnp.zeros((7, 128), F32)], 0)
        else:
            loss_copies[n - 1].wait_recv()
            value = loss_out[n - 1] + loss_in[n - 1]
        if n < len(others):
            loss_out[n] = value
            loss_copies[n].start()
        return value

    loss_step(0)

    parts = (image_part, text_part)
    sends = (image_send, text_send)
    halves = (image_half, text_half)
    fulls = (image_full, text_full)
    planes = (image_plane, text_plane)

    def lines(slot, start=0, size=block):
        return pl.ds(slot * block + start, size)

    def red(kind, n, src, dst, offset):
        return remote(
            src, dst, red_ssem.at[kind, n], red_rsem.at[kind, n], groups[kind].device(*offset)
        )

    def red_copies(kind):
        out = {}
        s, q, f = sends[kind], halves[kind], fulls[kind]
        for p in (0, 1):
            for h in (0, 1):
                n = 8 * p + 4 * h
                for d, offset in ((0, RIGHT), (1, LEFT)):
                    src = s.at[lines(4 * p + 3, h * half + d * quarter, quarter), :]
                    out["far", p, h, d] = red(kind, n + d, src, q.at[p, h, d], offset)
                    src = s.at[lines(4 * p + 1 + d, h * half, half), :]
                    dst = f.at[p, d, pl.ds(h * half, half), :]
                    out["near", p, h, d] = red(kind, n + 2 + d, src, dst, offset)
        for h in (0, 1):
            src = s.at[lines(4, h * half, half), :]
            dst = planes[kind].at[pl.ds(h * half, half), :]
            out["plane", h] = red(kind, 16 + h, src, dst, PARTNER)
        return out

    reds = [red_copies(kind) for kind in (0, 1)]

    def far(kind, p):
        sends[kind][lines(4 * p + 3), :] = parts[kind][lines(4 * p + 3), :].astype(BF16)
        for h in (0, 1):
            for d in (0, 1):
                reds[kind]["far", p, h, d].start()

    def near(kind, p):
        part, send, got = parts[kind], sends[kind], halves[kind]
        for h in (0, 1):
            for d in (0, 1):
                slot = 4 * p + 1 + d
                plain = lines(slot, h * half + (1 - d) * quarter, quarter)
                mixed = lines(slot, h * half + d * quarter, quarter)
                send[plain, :] = part[plain, :].astype(BF16)
                reds[kind]["far", p, h, d].wait_recv()
                send[mixed, :] = (part[mixed, :] + got[p, h, d].astype(F32)).astype(BF16)
                reds[kind]["near", p, h, d].start()

    def ring_sum(kind, p, h):
        for d in (0, 1):
            reds[kind]["near", p, h, d].wait_recv()
        r = pl.ds(h * half, half)
        return (
            parts[kind][lines(4 * p, h * half, half), :]
            + fulls[kind][p, 0, r, :].astype(F32)
            + fulls[kind][p, 1, r, :].astype(F32)
        )

    def plane(kind, h):
        sends[kind][lines(4, h * half, half), :] = ring_sum(kind, 1, h).astype(BF16)
        reds[kind]["plane", h].start()

    def partial(step, carry):
        g = 3 - step
        r = pl.ds(pl.multiple_of(g * pair, pair), pair)
        image_part[r, :] = jnp.dot(
            w_own[r, :], text_rows[0], preferred_element_type=F32
        ) + jnp.dot(w_other[r, :], text_rows[1], preferred_element_type=F32)

        for s in range(4):

            @pl.when(step == s)
            def _():
                if s == 0:
                    far(0, 1)
                    for a in range(4):
                        w_copy(a).wait_recv()
                elif s == 1:
                    near(0, 1)
                elif s == 2:
                    far(0, 0)

        text_part[r, :] = lax.dot_general(
            w_own[:, r], image_rows[0], (((0,), (0,)), ((), ())), preferred_element_type=F32
        ) + lax.dot_general(
            w_got[:, r], image_rows[1], (((0,), (0,)), ((), ())), preferred_element_type=F32
        )

        for s in range(4):

            @pl.when(step == s)
            def _():
                if s == 0:
                    far(1, 1)
                elif s == 1:
                    near(1, 1)
                elif s == 2:
                    far(1, 0)
                    plane(0, 0)
                    plane(1, 0)
                else:
                    plane(0, 1)
                    plane(1, 1)
                    near(0, 0)
                    near(1, 0)
                loss_step(s + 1)

        return carry

    lax.fori_loop(0, 4, partial, 0)

    for n in (5, 6, 7):
        loss = loss_step(n)
    loss = jnp.sum(jnp.sum(loss, 0, keepdims=True), 1, keepdims=True)
    total_rows = block * 2 * SLOTS * SLOTS
    loss_ref[...] = jnp.broadcast_to(loss / (2.0 * total_rows), loss_ref.shape)

    for h in (0, 1):
        r = pl.ds(h * half, half)
        for kind, out, other in ((0, image_out, text_ref), (1, text_out, image_ref)):
            value = ring_sum(kind, 0, h)
            reds[kind]["plane", h].wait_recv()
            value = value + planes[kind][r, :].astype(F32)
            out[r, :] = (scale * 0.5) * (value - 2.0 * other[r, :].astype(F32))

    for kind in (0, 1):
        for c in copies[kind].values():
            c.wait_send()
        for c in fwds[kind]:
            c.wait_send()
        for c in reds[kind].values():
            c.wait_send()
    for a in range(4):
        w_copy(a).wait_send()
    for c in row_out + col_out + loss_copies:
        c.wait_send()


def on_device(image_embed, text_embed):
    block, width = image_embed.shape
    group = SLOTS * block
    dma = pltpu.SemaphoreType.DMA
    shape = jax.ShapeDtypeStruct
    vmem = pl.BlockSpec(memory_space=pltpu.VMEM)
    loss, image_grad, text_grad = pl.pallas_call(
        kernel,
        out_shape=(
            shape((8, 128), F32),
            shape((block, width), F32),
            shape((block, width), F32),
        ),
        in_specs=[vmem, vmem],
        out_specs=(vmem, vmem, vmem),
        scratch_shapes=[
            pltpu.VMEM((2, group, width), BF16),
            pltpu.VMEM((2, group, width), BF16),
            pltpu.VMEM((4, 4, 2 * block, 4 * block), F32),
            pltpu.VMEM((group, 128), F32),
            pltpu.VMEM((group, 128), F32),
            pltpu.VMEM((8, 2 * group), F32),
            pltpu.VMEM((8, 2 * group), F32),
            pltpu.VMEM((SLOTS, 2 * SLOTS, 128), F32),
            pltpu.VMEM((2 * SLOTS, 4 * SLOTS, 128), F32),
            pltpu.VMEM((SLOTS, 128), F32),
            pltpu.VMEM((2 * SLOTS, 128), F32),
            pltpu.VMEM((group, 128), F32),
            pltpu.VMEM((1, 2 * group), F32),
            pltpu.VMEM((group, group), BF16),
            pltpu.VMEM((group, group), BF16),
            pltpu.VMEM((group, group), BF16),
            pltpu.VMEM((group, width), F32),
            pltpu.VMEM((group, width), F32),
            pltpu.VMEM((group, width), BF16),
            pltpu.VMEM((group, width), BF16),
            pltpu.VMEM((2, 2, 2, block // 4, width), BF16),
            pltpu.VMEM((2, 2, 2, block // 4, width), BF16),
            pltpu.VMEM((2, 2, block, width), BF16),
            pltpu.VMEM((2, 2, block, width), BF16),
            pltpu.VMEM((block, width), BF16),
            pltpu.VMEM((block, width), BF16),
            pltpu.VMEM((7, 8, 128), F32),
            pltpu.VMEM((7, 8, 128), F32),
            dma((2, 12)),
            dma((2, 12)),
            dma((2, SLOTS)),
            dma((2, SLOTS)),
            dma((SLOTS,)),
            dma((SLOTS,)),
            dma((2 * SLOTS,)),
            dma((2 * SLOTS,)),
            dma((7,)),
            dma((7,)),
            dma((4,)),
            dma((4,)),
            dma((2, 18)),
            dma((2, 18)),
        ],
        compiler_params=pltpu.CompilerParams(
            collective_id=0, has_side_effects=True, vmem_limit_bytes=56 * 2**20
        ),
    )(image_embed, text_embed)
    return loss[0, 0], image_grad, text_grad


def solution(mesh):
    return jax.shard_map(
        on_device,
        mesh=mesh,
        in_specs=(P(("inner", "outer"), None), P(("inner", "outer"), None)),
        out_specs=(P(), P(("inner", "outer"), None), P(("inner", "outer"), None)),
        check_vma=False,
    )
```

```python
import functools
import math

import jax
import jax.numpy as jnp
from jax import lax
from jax.experimental import pallas as pl
from jax.experimental.pallas import tpu as pltpu
from jax.sharding import PartitionSpec as P

F32, BF16 = jnp.float32, jnp.bfloat16
MESH = pl.DeviceIdType.MESH
OFFSETS = ((0, 0), (0, 1), (0, 3), (0, 2), (1, 0), (1, 1), (1, 3), (1, 2))
RING = 4
SLOTS = 8
LOG2E = math.log2(math.e)


def add_up(values):
    return functools.reduce(jnp.add, values)


class Group:
    def __init__(self, kind):
        inner, outer = lax.axis_index("inner"), lax.axis_index("outer")
        self.kind, self.core, chip = kind, lax.rem(outer, 2), outer // 2
        self.high, self.x = inner // RING, lax.rem(inner, RING)
        self.low, self.y = chip // RING, lax.rem(chip, RING)
        self.place = self.y if kind else self.x

    def index(self, plane_step, ring_step, core_step=0):
        place = lax.rem(self.place + ring_step, RING)
        if self.kind == 0:
            return lax.rem(self.high + plane_step, 2) * RING + place
        chip = lax.rem(self.low + plane_step, 2) * RING + place
        return chip * 2 + lax.rem(self.core + core_step, 2)

    def device(self, plane_step, ring_step, core_step=0):
        index = self.index(plane_step, ring_step, core_step)
        if self.kind:
            return {"outer": index}
        chip = lax.rem(self.low + plane_step, 2) * RING + self.y
        return {"inner": index, "outer": chip * 2 + self.core}


def kernel(
    image_ref,
    text_ref,
    loss_ref,
    image_out,
    text_out,
    image_rows,
    text_rows,
    scores,
    row_top,
    row_sum,
    col_top,
    col_sum,
    row_stats,
    col_stats,
    row_lse,
    col_lse,
    row_wide,
    col_wide,
    w_own,
    w_other,
    w_got,
    image_part,
    text_part,
    image_send,
    text_send,
    image_got,
    text_got,
    loss_out,
    loss_in,
    gather_send,
    gather_recv,
    fwd_send,
    fwd_recv,
    row_ssem,
    row_rsem,
    col_ssem,
    col_rsem,
    loss_ssem,
    loss_rsem,
    w_ssem,
    w_rsem,
    red_ssem,
    red_rsem,
):
    block, width = image_ref.shape
    half = block // 2
    pair = 2 * block
    scale = width ** (-0.5)
    inner, outer = lax.axis_index("inner"), lax.axis_index("outer")
    groups = (Group(0), Group(1))
    sibling = {"outer": groups[1].index(0, 0, 1)}
    own = (image_ref, text_ref)
    rows = (image_rows, text_rows)

    def remote(src, dst, ssem, rsem, device):
        return pltpu.make_async_remote_copy(
            src_ref=src,
            dst_ref=dst,
            send_sem=ssem,
            recv_sem=rsem,
            device_id=device,
            device_id_type=MESH,
        )

    RIGHT, LEFT, FAR, PARTNER = (0, 1), (0, 3), (0, 2), (1, 0)
    neighbours = [g.device(*o) for g in groups for o in (RIGHT, LEFT, PARTNER)] + [sibling]

    barrier = pltpu.get_barrier_semaphore()
    for device in neighbours:
        pl.semaphore_signal(barrier, inc=1, device_id=device, device_id_type=MESH)

    row_top[...] = jnp.full(row_top.shape, -1e30, F32)
    row_sum[...] = jnp.zeros(row_sum.shape, F32)
    col_top[...] = jnp.full(col_top.shape, -1e30, F32)
    col_sum[...] = jnp.zeros(col_sum.shape, F32)
    for kind in (0, 1):
        rows[kind][0, pl.ds(0, block), :] = own[kind][...]
    pl.semaphore_wait(barrier, len(neighbours))

    away = sorted(OFFSETS[1:], key=lambda o: -(o[0] + min(o[1], RING - o[1])))
    inner_peers = [groups[0].device(*o) for o in away]
    outer_peers = [groups[1].device(*o, c) for o in away for c in (1, 0)] + [sibling]

    def at(kind, core_step, slot, part=None):
        start, size = slot * block, block
        if part is not None:
            start, size = start + part * half, half
        return rows[kind].at[core_step, pl.ds(start, size), :]

    def copy(kind, src, slot, part, offset):
        n = 2 * (slot - 1) + part
        return remote(
            src,
            at(kind, 0, slot, part),
            gather_send.at[kind],
            gather_recv.at[kind, n],
            groups[kind].device(*offset),
        )

    def gather_copies(kind):
        out = {
            (3, 0): copy(kind, at(kind, 0, 2, 0), 3, 0, RIGHT),
            (3, 1): copy(kind, at(kind, 0, 1, 1), 3, 1, LEFT),
            (6, 0): copy(kind, at(kind, 0, 4, 0), 6, 0, RIGHT),
            (5, 0): copy(kind, at(kind, 0, 4, 0), 5, 0, LEFT),
            (7, 0): copy(kind, at(kind, 0, 6, 0), 7, 0, RIGHT),
            (5, 1): copy(kind, at(kind, 0, 1, 1), 5, 1, PARTNER),
            (6, 1): copy(kind, at(kind, 0, 2, 1), 6, 1, PARTNER),
            (7, 1): copy(kind, at(kind, 0, 3, 1), 7, 1, PARTNER),
        }
        for h in (0, 1):
            mine = own[kind].at[pl.ds(h * half, half), :]
            for slot, offset in ((2, RIGHT), (1, LEFT), (4, PARTNER)):
                out[slot, h] = copy(kind, mine, slot, h, offset)
        return out

    def fwd(kind, slot):
        return remote(
            own[kind] if slot == 0 else at(kind, 0, slot),
            at(kind, 1, slot),
            fwd_send.at[kind],
            fwd_recv.at[kind, slot],
            sibling,
        )

    copies = [gather_copies(kind) for kind in (0, 1)]
    fwds = [[fwd(kind, slot) for slot in range(SLOTS)] for kind in (0, 1)]

    def start(*keys):
        for key in keys:
            for kind in (0, 1):
                copies[kind][key].start()

    def arrived(*keys):
        for key in keys:
            for kind in (0, 1):
                copies[kind][key].wait_recv()

    def forward(*slots):
        for slot in slots:
            for kind in (0, 1):
                fwds[kind][slot].start()

    start((4, 0), (2, 1), (1, 1), (4, 1), (2, 0), (1, 0))
    forward(0)

    product = image_ref[...].astype(F32) * text_ref[...].astype(F32)
    positive = scale * jnp.sum(product, 0, keepdims=True)
    positive = add_up(positive[:, i : i + 128] for i in range(0, width, 128))

    def multiply(a, b):
        image = image_rows[0, pl.ds(a * pair, pair), :]
        for c in (0, 1):
            text = text_rows[c, pl.ds(b * pair, pair), :]
            scores[a, b, :, pl.ds(c * pair, pair)] = (scale * LOG2E) * lax.dot_general(
                image, text, (((1,), (1,)), ((), ())), preferred_element_type=F32
            )

    def count(a, b):
        step = 32
        k = pl.ds(b * 2 * pair, 2 * pair)
        old = col_top[:, k]
        top = old
        for r in range(0, pair, step):
            value = scores[a, b, pl.ds(r, step), :].reshape(step // 8, 8, 2 * pair)
            top = jnp.maximum(top, jnp.max(value, 0))
        total = col_sum[:, k] * jnp.exp2(old - top)
        for r in range(0, pair, step):
            value = scores[a, b, pl.ds(r, step), :]
            here = pl.ds(a * pair + r, step)
            lanes = [value[:, i : i + 128] for i in range(0, 2 * pair, 128)]
            before = row_top[here, :]
            row = functools.reduce(jnp.maximum, lanes, before)
            row_sum[here, :] = row_sum[here, :] * jnp.exp2(before - row) + add_up(
                jnp.exp2(lane - row) for lane in lanes
            )
            row_top[here, :] = row
            value = value.reshape(step // 8, 8, 2 * pair)
            total = total + jnp.sum(jnp.exp2(value - top[None]), 0)
        col_top[:, k] = top
        col_sum[:, k] = total

    waiting = []

    def shell(n):
        for a, b in [(n, j) for j in range(n + 1)] + [(j, n) for j in range(n)]:
            multiply(a, b)
            if waiting:
                count(*waiting.pop())
            waiting.append((a, b))

    def sib_arrived(*slots):
        for slot in slots:
            for kind in (0, 1):
                fwds[kind][slot].wait_recv()

    arrived((1, 1))
    start((3, 1), (5, 1))
    arrived((4, 0))
    start((6, 0), (5, 0))
    arrived((2, 1))
    start((6, 1))
    arrived((2, 0))
    start((3, 0))
    arrived((1, 0))
    forward(1, 2)
    arrived((4, 1))
    forward(4)
    sib_arrived(0, 1)
    shell(0)
    arrived((3, 1))
    start((7, 1))
    arrived((6, 0))
    start((7, 0))
    arrived((3, 0))
    forward(3)
    arrived((5, 0), (5, 1))
    forward(5)
    arrived((6, 1))
    forward(6)
    sib_arrived(2, 3)
    shell(1)
    sib_arrived(4, 5)
    shell(2)
    arrived((7, 0), (7, 1))
    forward(7)
    sib_arrived(6, 7)
    shell(3)
    count(*waiting.pop())

    for slot, offset in enumerate(OFFSETS):
        i = groups[0].index(*offset)
        r = pl.ds(slot * block, block)
        lanes = jnp.transpose(row_top[r, :])
        top = jnp.max(lanes, 0, keepdims=True)
        total = jnp.sum(jnp.transpose(row_sum[r, :]) * jnp.exp2(lanes - top), 0, keepdims=True)
        row_stats[inner, pl.ds(i, 1), :] = top
        row_stats[inner, pl.ds(i + SLOTS, 1), :] = total
        for c in (0, 1):
            o = groups[1].index(*offset, c)
            k = pl.ds((slot // 2) * 2 * pair + c * pair + (slot % 2) * block, block)
            lanes = col_top[:, k]
            top = jnp.max(lanes, 0, keepdims=True)
            total = jnp.sum(col_sum[:, k] * jnp.exp2(lanes - top), 0, keepdims=True)
            col_stats[outer, pl.ds(o, 1), :] = top
            col_stats[outer, pl.ds(o + 2 * SLOTS, 1), :] = total

    def spread(ref, me, ssem, rsem, peers):
        for device in peers:
            remote(ref.at[me], ref.at[me], ssem, rsem, device).start()
        every = ref.at[pl.ds(0, len(peers))]
        return remote(every, every, ssem, rsem, sibling)

    col_out = spread(col_stats, outer, col_ssem.at[0], col_rsem.at[0], outer_peers)
    row_out = spread(row_stats, inner, row_ssem.at[0], row_rsem.at[0], inner_peers)
    row_out.wait_recv()
    col_out.wait_recv()

    def combine(ref, count):
        tops = [ref[n, 0:count, :] for n in range(count)]
        top = functools.reduce(jnp.maximum, tops)
        total = add_up(
            ref[n, count : 2 * count, :] * jnp.exp2(tops[n] - top) for n in range(count)
        )
        return top + LOG2E * jnp.log(total)

    row_value = combine(row_stats, SLOTS)
    col_value = combine(col_stats, 2 * SLOTS)
    row_lse[...] = row_value
    col_lse[...] = col_value
    for slot, offset in enumerate(OFFSETS):
        i = groups[0].index(*offset)
        line = row_lse[pl.ds(i, 1), :]
        row_wide[pl.ds(slot * block, block), :] = jnp.transpose(
            jnp.broadcast_to(line, (block, block))
        )
        for c in (0, 1):
            o = groups[1].index(*offset, c)
            k = pl.ds((slot // 2) * 2 * pair + c * pair + (slot % 2) * block, block)
            col_wide[:, k] = col_lse[pl.ds(o, 1), :]

    def weigh(a, b):
        step = 32
        for r in range(0, pair, step):
            here = pl.ds(a * pair + r, step)
            line = jnp.concatenate([row_wide[here, :]] * 2, 1)
            for c, out in ((0, w_own), (1, w_other)):
                value = scores[a, b, pl.ds(r, step), pl.ds(c * pair, pair)]
                there = pl.ds((2 * b + c) * pair, pair)
                weight = jnp.exp2(value - line) + jnp.exp2(value - col_wide[:, there])
                out[b, here, :] = weight.astype(BF16)

    w_copies = [
        remote(w_other.at[b], w_got.at[b], w_ssem.at[b], w_rsem.at[b], sibling) for b in range(4)
    ]
    weighed = set()

    def weigh_pair(g):
        for a, b in [(a, g) for a in range(4)] + [(g, b) for b in range(4)]:
            if (a, b) not in weighed:
                weighed.add((a, b))
                weigh(a, b)
            if len([1 for w in weighed if w[1] == g]) == 4 and (g, "sent") not in weighed:
                weighed.add((g, "sent"))
                w_copies[g].start()

    def flip(group, bit):
        return group.device(0, 2) if bit else group.device(0, 1 + 2 * lax.rem(group.place, 2))

    others = [sibling, groups[1].device(*PARTNER), groups[0].device(*PARTNER)] + [
        flip(group, bit) for group in groups for bit in (0, 1)
    ]
    loss_copies = [
        remote(loss_out.at[n], loss_in.at[n], loss_ssem.at[n], loss_rsem.at[n], device)
        for n, device in enumerate(others)
    ]

    def loss_step(n):
        if n == 0:
            both = row_lse[pl.ds(inner, 1), :] + col_lse[pl.ds(outer, 1), :]
            both = both * (1.0 / LOG2E) - 2.0 * positive
            value = jnp.concatenate([both, jnp.zeros((7, 128), F32)], 0)
        else:
            loss_copies[n - 1].wait_recv()
            value = loss_out[n - 1] + loss_in[n - 1]
        if n < len(others):
            loss_out[n] = value
            loss_copies[n].start()
        return value

    parts = (image_part, text_part)
    sends = (image_send, text_send)
    gots = (image_got, text_got)

    def lines(slot, h):
        return pl.ds(slot * block + h * half, half)

    def red_copies(kind):
        way = {(7, 0): RIGHT, (5, 0): RIGHT, (6, 0): LEFT, (3, 0): RIGHT, (3, 1): LEFT}
        way.update({(1, h): RIGHT for h in (0, 1)})
        way.update({(2, h): LEFT for h in (0, 1)})
        way.update({(slot, 1): PARTNER for slot in (4, 5, 6, 7)})
        way[4, 0] = PARTNER
        return {
            key: remote(
                sends[kind].at[lines(*key), :],
                gots[kind].at[n],
                red_ssem.at[kind],
                red_rsem.at[kind, n],
                groups[kind].device(*way[key]),
            )
            for n, key in enumerate(sorted(way))
        }

    reds = [red_copies(kind) for kind in (0, 1)]
    numbers = {key: n for n, key in enumerate(sorted(reds[0]))}

    def total_of(kind, slot, h, *keys):
        value = parts[kind][lines(slot, h), :]
        for key in keys:
            reds[kind][key].wait_recv()
            value = value + gots[kind][numbers[key]].astype(F32)
        return value

    def pass_on(kind, slot, h, *keys):
        sends[kind][lines(slot, h), :] = total_of(kind, slot, h, *keys).astype(BF16)
        reds[kind][slot, h].start()

    def image_pair(g):
        r = pl.ds(g * pair, pair)
        image_part[r, :] = add_up(
            jnp.dot(
                jnp.concatenate([w[b, r, :] for b in range(4)], 1),
                text_rows[c],
                preferred_element_type=F32,
            )
            for c, w in ((0, w_own), (1, w_other))
        )

    def text_pair(g):
        text_part[pl.ds(g * pair, pair), :] = add_up(
            lax.dot_general(
                w[g], image_rows[c], (((0,), (0,)), ((), ())), preferred_element_type=F32
            )
            for c, w in ((0, w_own), (1, w_got))
        )

    def products(g, *ready):
        weigh_pair(g)
        image_pair(g)
        for slot, h in ready:
            pass_on(0, slot, h)
        w_copies[g].wait_recv()
        text_pair(g)
        for slot, h in ready:
            pass_on(1, slot, h)

    def both(slot, h, *keys):
        for kind in (0, 1):
            pass_on(kind, slot, h, *keys)

    products(3, (7, 1), (7, 0), (6, 0), (6, 1))
    loss_step(0)
    products(1, (3, 0), (2, 0))
    loss_step(1)
    products(2, (5, 1), (4, 1))
    both(3, 1, (7, 1))
    both(5, 0, (7, 0))
    loss_step(2)
    products(0)
    loss_step(3)
    both(1, 0, (3, 0))
    both(1, 1, (5, 1))
    both(4, 0, (5, 0), (6, 0))
    both(2, 1, (6, 1), (3, 1))
    for n in (4, 5, 6, 7):
        loss = loss_step(n)
    loss = jnp.sum(jnp.sum(loss, 0, keepdims=True), 1, keepdims=True)
    total_rows = block * 2 * SLOTS * SLOTS
    loss_ref[...] = jnp.broadcast_to(loss / (2.0 * total_rows), loss_ref.shape)

    for h, keys in ((0, ((1, 0), (2, 0), (4, 0))), (1, ((4, 1), (1, 1), (2, 1)))):
        r = pl.ds(h * half, half)
        for kind, out, other in ((0, image_out, text_ref), (1, text_out, image_ref)):
            value = total_of(kind, 0, h, *keys)
            out[r, :] = (scale * 0.5) * (value - 2.0 * other[r, :].astype(F32))

    for kind in (0, 1):
        sent = rows[kind].at[0, pl.ds(0, 14 * half), :]
        remote(sent, sent, gather_send.at[kind], gather_recv.at[kind, 0], sibling).wait_send()
        sent = rows[kind].at[0]
        remote(sent, sent, fwd_send.at[kind], fwd_recv.at[kind, 0], sibling).wait_send()
        sent = sends[kind].at[pl.ds(0, 14 * half), :]
        remote(sent, sent, red_ssem.at[kind], red_rsem.at[kind, 0], sibling).wait_send()
    for c in w_copies + loss_copies + [row_out, col_out]:
        c.wait_send()


def on_device(image_embed, text_embed):
    block, width = image_embed.shape
    group = SLOTS * block
    dma = pltpu.SemaphoreType.DMA
    shape = jax.ShapeDtypeStruct
    vmem = pl.BlockSpec(memory_space=pltpu.VMEM)
    loss, image_grad, text_grad = pl.pallas_call(
        kernel,
        out_shape=(
            shape((8, 128), F32),
            shape((block, width), F32),
            shape((block, width), F32),
        ),
        in_specs=[vmem, vmem],
        out_specs=(vmem, vmem, vmem),
        scratch_shapes=[
            pltpu.VMEM((2, group, width), BF16),
            pltpu.VMEM((2, group, width), BF16),
            pltpu.VMEM((4, 4, 2 * block, 4 * block), F32),
            pltpu.VMEM((group, 128), F32),
            pltpu.VMEM((group, 128), F32),
            pltpu.VMEM((8, 2 * group), F32),
            pltpu.VMEM((8, 2 * group), F32),
            pltpu.VMEM((SLOTS, 2 * SLOTS, 128), F32),
            pltpu.VMEM((2 * SLOTS, 4 * SLOTS, 128), F32),
            pltpu.VMEM((SLOTS, 128), F32),
            pltpu.VMEM((2 * SLOTS, 128), F32),
            pltpu.VMEM((group, 128), F32),
            pltpu.VMEM((1, 2 * group), F32),
            pltpu.VMEM((4, group, 2 * block), BF16),
            pltpu.VMEM((4, group, 2 * block), BF16),
            pltpu.VMEM((4, group, 2 * block), BF16),
            pltpu.VMEM((group, width), F32),
            pltpu.VMEM((group, width), F32),
            pltpu.VMEM((group, width), BF16),
            pltpu.VMEM((group, width), BF16),
            pltpu.VMEM((14, block // 2, width), BF16),
            pltpu.VMEM((14, block // 2, width), BF16),
            pltpu.VMEM((7, 8, 128), F32),
            pltpu.VMEM((7, 8, 128), F32),
            dma((2,)),
            dma((2, 14)),
            dma((2,)),
            dma((2, SLOTS)),
            dma((1,)),
            dma((1,)),
            dma((1,)),
            dma((1,)),
            dma((7,)),
            dma((7,)),
            dma((4,)),
            dma((4,)),
            dma((2,)),
            dma((2, 14)),
        ],
        compiler_params=pltpu.CompilerParams(
            collective_id=0, has_side_effects=True, vmem_limit_bytes=56 * 2**20
        ),
    )(image_embed, text_embed)
    return loss[0, 0], image_grad, text_grad


def solution(mesh):
    return jax.shard_map(
        on_device,
        mesh=mesh,
        in_specs=(P(("inner", "outer"), None), P(("inner", "outer"), None)),
        out_specs=(P(), P(("inner", "outer"), None), P(("inner", "outer"), None)),
        check_vma=False,
    )
```

```python
import functools
import math

import jax
import jax.numpy as jnp
from jax import lax
from jax.experimental import pallas as pl
from jax.experimental.pallas import tpu as pltpu
from jax.sharding import PartitionSpec as P

F32, BF16 = jnp.float32, jnp.bfloat16
MESH = pl.DeviceIdType.MESH
OFFSETS = ((0, 0), (0, 1), (0, 3), (0, 2), (1, 0), (1, 1), (1, 3), (1, 2))
PLACE = (0, 2, 3, 4, 1, 5, 6, 7)
RING = 4
SLOTS = 8
LOG2E = math.log2(math.e)


def add_up(values):
    return functools.reduce(jnp.add, values)


class Group:
    def __init__(self, kind):
        inner, outer = lax.axis_index("inner"), lax.axis_index("outer")
        core, chip = lax.rem(outer, 2), outer // 2
        high, x = inner // RING, lax.rem(inner, RING)
        low, y = chip // RING, lax.rem(chip, RING)
        self.kind, self.y = kind, y
        self.place = y if kind else x
        self.cores, self.lows, self.highs = (core, 1 - core), (low, 1 - low), (high, 1 - high)
        self.places = [self.place] + [lax.rem(self.place + n, RING) for n in range(1, RING)]

    def index(self, plane_step, ring_step, core_step=0):
        if self.kind == 0:
            return self.highs[plane_step] * RING + self.places[ring_step]
        chip = self.lows[plane_step] * RING + self.places[ring_step]
        return chip * 2 + self.cores[core_step]

    def device(self, plane_step, ring_step, core_step=0):
        index = self.index(plane_step, ring_step, core_step)
        if self.kind:
            return {"outer": index}
        chip = self.lows[plane_step] * RING + self.y
        return {"inner": index, "outer": chip * 2 + self.cores[0]}

    def flips(self):
        near = self.place + 1 - 2 * lax.rem(self.place, 2)
        two = self.places[2]
        out = []
        for place in (near, two):
            if self.kind:
                out.append({"outer": (self.lows[0] * RING + place) * 2 + self.cores[0]})
            else:
                out.append({"inner": self.highs[0] * RING + place})
        return out


def kernel(
    image_ref,
    text_ref,
    loss_ref,
    image_out,
    text_out,
    image_rows,
    text_rows,
    scores,
    row_top,
    row_sum,
    col_top,
    col_sum,
    row_stats,
    col_stats,
    row_lse,
    col_lse,
    row_wide,
    col_wide,
    w_own,
    w_other,
    w_got,
    image_part,
    text_part,
    image_send,
    text_send,
    image_got,
    text_got,
    loss_out,
    loss_in,
    gather_send,
    gather_recv,
    fwd_send,
    fwd_recv,
    row_ssem,
    row_rsem,
    col_ssem,
    col_rsem,
    loss_ssem,
    loss_rsem,
    w_ssem,
    w_rsem,
    red_ssem,
    red_rsem,
):
    block, width = image_ref.shape
    half = block // 2
    pair = 2 * block
    scale = width ** (-0.5)
    inner, outer = lax.axis_index("inner"), lax.axis_index("outer")
    groups = (Group(0), Group(1))
    sibling = {"outer": groups[1].index(0, 0, 1)}
    own = (image_ref, text_ref)
    rows = (image_rows, text_rows)

    def remote(src, dst, ssem, rsem, device):
        return pltpu.make_async_remote_copy(
            src_ref=src,
            dst_ref=dst,
            send_sem=ssem,
            recv_sem=rsem,
            device_id=device,
            device_id_type=MESH,
        )

    RIGHT, LEFT, FAR, PARTNER = (0, 1), (0, 3), (0, 2), (1, 0)
    neighbours = [g.device(*o) for g in groups for o in (RIGHT, LEFT, PARTNER)] + [sibling]

    barrier = pltpu.get_barrier_semaphore()
    for device in neighbours:
        pl.semaphore_signal(barrier, inc=1, device_id=device, device_id_type=MESH)

    row_top[...] = jnp.full(row_top.shape, -1e30, F32)
    row_sum[...] = jnp.zeros(row_sum.shape, F32)
    col_top[...] = jnp.full(col_top.shape, -1e30, F32)
    col_sum[...] = jnp.zeros(col_sum.shape, F32)
    for kind in (0, 1):
        rows[kind][0, pl.ds(0, block), :] = own[kind][...]
    pl.semaphore_wait(barrier, len(neighbours))

    away = sorted(OFFSETS[1:], key=lambda o: -(o[0] + min(o[1], RING - o[1])))
    inner_peers = [groups[0].device(*o) for o in away]
    outer_peers = [groups[1].device(*o, c) for o in away for c in (1, 0)] + [sibling]

    def at(kind, core_step, slot, part=None):
        start, size = PLACE[slot] * block, block
        if part is not None:
            start, size = start + part * half, half
        return rows[kind].at[core_step, pl.ds(start, size), :]

    def copy(kind, src, slot, part, offset):
        n = 2 * (slot - 1) + part
        return remote(
            src,
            at(kind, 0, slot, part),
            gather_send.at[kind],
            gather_recv.at[kind, n],
            groups[kind].device(*offset),
        )

    def gather_copies(kind):
        out = {
            (3, 0): copy(kind, at(kind, 0, 2, 0), 3, 0, RIGHT),
            (3, 1): copy(kind, at(kind, 0, 1, 1), 3, 1, LEFT),
            (6, 0): copy(kind, at(kind, 0, 4, 0), 6, 0, RIGHT),
            (5, 0): copy(kind, at(kind, 0, 4, 0), 5, 0, LEFT),
            (7, 0): copy(kind, at(kind, 0, 6, 0), 7, 0, RIGHT),
            (5, 1): copy(kind, at(kind, 0, 1, 1), 5, 1, PARTNER),
            (6, 1): copy(kind, at(kind, 0, 2, 1), 6, 1, PARTNER),
            (7, 1): copy(kind, at(kind, 0, 3, 1), 7, 1, PARTNER),
        }
        for h in (0, 1):
            mine = own[kind].at[pl.ds(h * half, half), :]
            for slot, offset in ((2, RIGHT), (1, LEFT), (4, PARTNER)):
                out[slot, h] = copy(kind, mine, slot, h, offset)
        return out

    def fwd(kind, slot):
        return remote(
            own[kind] if slot == 0 else at(kind, 0, slot),
            at(kind, 1, slot),
            fwd_send.at[kind],
            fwd_recv.at[kind, slot],
            sibling,
        )

    copies = [gather_copies(kind) for kind in (0, 1)]
    fwds = [[fwd(kind, slot) for slot in range(SLOTS)] for kind in (0, 1)]

    def start(*keys):
        for key in keys:
            for kind in (0, 1):
                copies[kind][key].start()

    def arrived(*keys):
        for key in keys:
            for kind in (0, 1):
                copies[kind][key].wait_recv()

    def forward(*slots):
        for slot in slots:
            for kind in (0, 1):
                fwds[kind][slot].start()

    start((4, 0), (2, 1), (1, 1), (4, 1), (2, 0), (1, 0))
    forward(0)

    product = image_ref[...].astype(F32) * text_ref[...].astype(F32)
    positive = scale * jnp.sum(product, 0, keepdims=True)
    positive = add_up(positive[:, i : i + 128] for i in range(0, width, 128))

    def multiply(a, b):
        image = image_rows[0, pl.ds(a * pair, pair), :]
        for c in (0, 1):
            text = text_rows[c, pl.ds(b * pair, pair), :]
            scores[a, b, :, pl.ds(c * pair, pair)] = (scale * LOG2E) * lax.dot_general(
                image, text, (((1,), (1,)), ((), ())), preferred_element_type=F32
            )

    def count(a, b):
        step = 32
        k = pl.ds(b * 2 * pair, 2 * pair)
        old = col_top[:, k]
        top = old
        for r in range(0, pair, step):
            value = scores[a, b, pl.ds(r, step), :].reshape(step // 8, 8, 2 * pair)
            top = jnp.maximum(top, jnp.max(value, 0))
        total = col_sum[:, k] * jnp.exp2(old - top)
        for r in range(0, pair, step):
            value = scores[a, b, pl.ds(r, step), :]
            here = pl.ds(a * pair + r, step)
            lanes = [value[:, i : i + 128] for i in range(0, 2 * pair, 128)]
            before = row_top[here, :]
            row = functools.reduce(jnp.maximum, lanes, before)
            row_sum[here, :] = row_sum[here, :] * jnp.exp2(before - row) + add_up(
                jnp.exp2(lane - row) for lane in lanes
            )
            row_top[here, :] = row
            value = value.reshape(step // 8, 8, 2 * pair)
            total = total + jnp.sum(jnp.exp2(value - top[None]), 0)
        col_top[:, k] = top
        col_sum[:, k] = total

    waiting = []

    def shell(n):
        for a, b in [(n, j) for j in range(n + 1)] + [(j, n) for j in range(n)]:
            multiply(a, b)
            if waiting:
                count(*waiting.pop())
            waiting.append((a, b))

    def sib_arrived(*slots):
        for slot in slots:
            for kind in (0, 1):
                fwds[kind][slot].wait_recv()

    arrived((1, 1))
    start((3, 1), (5, 1))
    arrived((4, 0))
    start((6, 0), (5, 0))
    arrived((2, 1))
    start((6, 1))
    arrived((2, 0))
    start((3, 0))
    arrived((1, 0))
    arrived((4, 1))
    forward(4, 1, 2)
    sib_arrived(0, 4)
    shell(0)
    arrived((3, 1))
    start((7, 1))
    arrived((6, 0))
    start((7, 0))
    sib_arrived(1, 2)
    shell(1)
    arrived((3, 0))
    forward(3)
    arrived((5, 0), (5, 1))
    forward(5)
    arrived((6, 1))
    forward(6)
    sib_arrived(3, 5)
    shell(2)
    arrived((7, 0), (7, 1))
    forward(7)
    sib_arrived(6, 7)
    shell(3)
    count(*waiting.pop())

    for slot, offset in enumerate(OFFSETS):
        i = groups[0].index(*offset)
        place = PLACE[slot]
        r = pl.ds(place * block, block)
        lanes = jnp.transpose(row_top[r, :])
        top = jnp.max(lanes, 0, keepdims=True)
        total = jnp.sum(jnp.transpose(row_sum[r, :]) * jnp.exp2(lanes - top), 0, keepdims=True)
        row_stats[inner, pl.ds(i, 1), :] = top
        row_stats[inner, pl.ds(i + SLOTS, 1), :] = total
        for c in (0, 1):
            o = groups[1].index(*offset, c)
            k = pl.ds((place // 2) * 2 * pair + c * pair + (place % 2) * block, block)
            lanes = col_top[:, k]
            top = jnp.max(lanes, 0, keepdims=True)
            total = jnp.sum(col_sum[:, k] * jnp.exp2(lanes - top), 0, keepdims=True)
            col_stats[outer, pl.ds(o, 1), :] = top
            col_stats[outer, pl.ds(o + 2 * SLOTS, 1), :] = total

    row_stats[inner, pl.ds(2 * SLOTS, 8), :] = jnp.concatenate(
        [positive, jnp.zeros((7, 128), F32)], 0
    )

    def spread(ref, me, ssem, rsem, peers):
        for device in peers:
            remote(ref.at[me], ref.at[me], ssem, rsem, device).start()
        every = ref.at[pl.ds(0, len(peers))]
        return remote(every, every, ssem, rsem, sibling)

    col_out = spread(col_stats, outer, col_ssem.at[0], col_rsem.at[0], outer_peers)
    row_out = spread(row_stats, inner, row_ssem.at[0], row_rsem.at[0], inner_peers)
    row_out.wait_recv()
    col_out.wait_recv()

    def combine(ref, count):
        tops = [ref[n, 0:count, :] for n in range(count)]
        top = functools.reduce(jnp.maximum, tops)
        total = add_up(
            ref[n, count : 2 * count, :] * jnp.exp2(tops[n] - top) for n in range(count)
        )
        return top + LOG2E * jnp.log(total)

    row_value = combine(row_stats, SLOTS)
    col_value = combine(col_stats, 2 * SLOTS)
    row_lse[...] = row_value
    col_lse[...] = col_value
    for slot, offset in enumerate(OFFSETS):
        i = groups[0].index(*offset)
        line = row_lse[pl.ds(i, 1), :]
        place = PLACE[slot]
        row_wide[pl.ds(place * block, block), :] = jnp.transpose(
            jnp.broadcast_to(line, (block, block))
        )
        for c in (0, 1):
            o = groups[1].index(*offset, c)
            k = pl.ds((place // 2) * 2 * pair + c * pair + (place % 2) * block, block)
            col_wide[:, k] = col_lse[pl.ds(o, 1), :]

    def weigh(a, b):
        step = 32
        for r in range(0, pair, step):
            here = pl.ds(a * pair + r, step)
            line = jnp.concatenate([row_wide[here, :]] * 2, 1)
            for c, out in ((0, w_own), (1, w_other)):
                value = scores[a, b, pl.ds(r, step), pl.ds(c * pair, pair)]
                there = pl.ds((2 * b + c) * pair, pair)
                weight = jnp.exp2(value - line) + jnp.exp2(value - col_wide[:, there])
                out[b, here, :] = weight.astype(BF16)

    w_copies = [
        remote(w_other.at[b], w_got.at[b], w_ssem.at[b], w_rsem.at[b], sibling) for b in range(4)
    ]
    weighed = set()

    def weigh_pair(g):
        for a, b in [(a, g) for a in range(4)] + [(g, b) for b in range(4)]:
            if (a, b) not in weighed:
                weighed.add((a, b))
                weigh(a, b)
            if len([1 for w in weighed if w[1] == g]) == 4 and (g, "sent") not in weighed:
                weighed.add((g, "sent"))
                w_copies[g].start()

    paired = add_up([row_stats[n, pl.ds(2 * SLOTS, 8), :] for n in range(SLOTS)])
    shares = (
        row_value * (1.0 / LOG2E) - 2.0 * paired,
        (col_value[0:8] + col_value[8:16]) * (1.0 / LOG2E),
    )
    others = (
        [sibling, groups[1].device(*PARTNER)] + groups[1].flips(),
        [groups[0].device(*PARTNER)] + groups[0].flips(),
    )
    loss_copies = [
        [
            remote(
                loss_out.at[kind, n],
                loss_in.at[kind, n],
                loss_ssem.at[kind, n],
                loss_rsem.at[kind, n],
                device,
            )
            for n, device in enumerate(others[kind])
        ]
        for kind in (0, 1)
    ]

    def loss_step(kind, n):
        if n == 0:
            value = shares[kind]
        else:
            loss_copies[kind][n - 1].wait_recv()
            value = loss_out[kind, n - 1] + loss_in[kind, n - 1]
        if n < len(others[kind]):
            loss_out[kind, n] = value
            loss_copies[kind][n].start()
        return value

    loss_step(0, 0)
    loss_step(1, 0)

    parts = (image_part, text_part)
    sends = (image_send, text_send)
    gots = (image_got, text_got)

    def lines(slot, h):
        return pl.ds(PLACE[slot] * block + h * half, half)

    def red_copies(kind):
        way = {(7, 0): RIGHT, (5, 0): RIGHT, (6, 0): LEFT, (3, 0): RIGHT, (3, 1): LEFT}
        way.update({(1, h): RIGHT for h in (0, 1)})
        way.update({(2, h): LEFT for h in (0, 1)})
        way.update({(slot, 1): PARTNER for slot in (4, 5, 6, 7)})
        way[4, 0] = PARTNER
        return {
            key: remote(
                sends[kind].at[lines(*key), :],
                gots[kind].at[n],
                red_ssem.at[kind],
                red_rsem.at[kind, n],
                groups[kind].device(*way[key]),
            )
            for n, key in enumerate(sorted(way))
        }

    reds = [red_copies(kind) for kind in (0, 1)]
    numbers = {key: n for n, key in enumerate(sorted(reds[0]))}

    def total_of(kind, slot, h, *keys):
        value = parts[kind][lines(slot, h), :]
        for key in keys:
            reds[kind][key].wait_recv()
            value = value + gots[kind][numbers[key]].astype(F32)
        return value

    def pass_on(kind, slot, h, *keys):
        sends[kind][lines(slot, h), :] = total_of(kind, slot, h, *keys).astype(BF16)
        reds[kind][slot, h].start()

    def image_pair(g):
        r = pl.ds(g * pair, pair)
        image_part[r, :] = add_up(
            jnp.dot(
                jnp.concatenate([w[b, r, :] for b in range(4)], 1),
                text_rows[c],
                preferred_element_type=F32,
            )
            for c, w in ((0, w_own), (1, w_other))
        )

    def text_pair(g):
        text_part[pl.ds(g * pair, pair), :] = add_up(
            lax.dot_general(
                w[g], image_rows[c], (((0,), (0,)), ((), ())), preferred_element_type=F32
            )
            for c, w in ((0, w_own), (1, w_got))
        )

    def products(g, following, *ready):
        image_pair(g)
        for slot, h in ready:
            pass_on(0, slot, h)
        if following is not None:
            weigh_pair(following)
        w_copies[g].wait_recv()
        text_pair(g)
        for slot, h in ready:
            pass_on(1, slot, h)

    def both(slot, h, *keys):
        for kind in (0, 1):
            pass_on(kind, slot, h, *keys)

    weigh_pair(3)
    products(3, 2, (7, 1), (7, 0), (6, 0), (6, 1))
    loss_step(0, 1)
    loss_step(1, 1)
    products(2, 1, (3, 0), (5, 1))
    loss_step(0, 2)
    loss_step(1, 2)
    both(3, 1, (7, 1))
    both(5, 0, (7, 0))
    products(1, 0, (2, 0))
    loss_step(0, 3)
    products(0, None, (4, 1))
    both(1, 0, (3, 0))
    both(4, 0, (5, 0), (6, 0))
    both(1, 1, (5, 1))
    both(2, 1, (6, 1), (3, 1))
    loss = loss_step(0, 4) + loss_step(1, 3)
    loss = jnp.sum(jnp.sum(loss, 0, keepdims=True), 1, keepdims=True)
    total_rows = block * 2 * SLOTS * SLOTS
    loss_ref[...] = jnp.broadcast_to(loss / (2.0 * total_rows), loss_ref.shape)

    for h, keys in ((0, ((1, 0), (2, 0), (4, 0))), (1, ((4, 1), (1, 1), (2, 1)))):
        r = pl.ds(h * half, half)
        for kind, out in ((0, image_out), (1, text_out)):
            out[r, :] = total_of(kind, 0, h, *keys)

    for kind in (0, 1):
        sent = rows[kind].at[0, pl.ds(0, 14 * half), :]
        remote(sent, sent, gather_send.at[kind], gather_recv.at[kind, 0], sibling).wait_send()
        sent = rows[kind].at[0]
        remote(sent, sent, fwd_send.at[kind], fwd_recv.at[kind, 0], sibling).wait_send()
        sent = sends[kind].at[pl.ds(0, 14 * half), :]
        remote(sent, sent, red_ssem.at[kind], red_rsem.at[kind, 0], sibling).wait_send()
    for c in w_copies + loss_copies[0] + loss_copies[1] + [row_out, col_out]:
        c.wait_send()


def finish(image_ref, text_ref, loss_ref, image_sum, text_sum, loss_out, image_out, text_out):
    half_scale = 0.5 * image_ref.shape[1] ** (-0.5)
    image_out[...] = half_scale * (image_sum[...] - 2.0 * text_ref[...].astype(F32))
    text_out[...] = half_scale * (text_sum[...] - 2.0 * image_ref[...].astype(F32))
    loss_out[0, 0] = loss_ref[0, 0]


def on_device(image_embed, text_embed):
    block, width = image_embed.shape
    group = SLOTS * block
    dma = pltpu.SemaphoreType.DMA
    shape = jax.ShapeDtypeStruct
    vmem = pl.BlockSpec(memory_space=pltpu.VMEM)
    loss, image_sum, text_sum = pl.pallas_call(
        kernel,
        out_shape=(
            shape((8, 128), F32),
            shape((block, width), F32),
            shape((block, width), F32),
        ),
        in_specs=[vmem, vmem],
        out_specs=(vmem, vmem, vmem),
        scratch_shapes=[
            pltpu.VMEM((2, group, width), BF16),
            pltpu.VMEM((2, group, width), BF16),
            pltpu.VMEM((4, 4, 2 * block, 4 * block), F32),
            pltpu.VMEM((group, 128), F32),
            pltpu.VMEM((group, 128), F32),
            pltpu.VMEM((8, 2 * group), F32),
            pltpu.VMEM((8, 2 * group), F32),
            pltpu.VMEM((SLOTS, 3 * SLOTS, 128), F32),
            pltpu.VMEM((2 * SLOTS, 4 * SLOTS, 128), F32),
            pltpu.VMEM((SLOTS, 128), F32),
            pltpu.VMEM((2 * SLOTS, 128), F32),
            pltpu.VMEM((group, 128), F32),
            pltpu.VMEM((1, 2 * group), F32),
            pltpu.VMEM((4, group, 2 * block), BF16),
            pltpu.VMEM((4, group, 2 * block), BF16),
            pltpu.VMEM((4, group, 2 * block), BF16),
            pltpu.VMEM((group, width), F32),
            pltpu.VMEM((group, width), F32),
            pltpu.VMEM((group, width), BF16),
            pltpu.VMEM((group, width), BF16),
            pltpu.VMEM((14, block // 2, width), BF16),
            pltpu.VMEM((14, block // 2, width), BF16),
            pltpu.VMEM((2, 4, 8, 128), F32),
            pltpu.VMEM((2, 4, 8, 128), F32),
            dma((2,)),
            dma((2, 14)),
            dma((2,)),
            dma((2, SLOTS)),
            dma((1,)),
            dma((1,)),
            dma((1,)),
            dma((1,)),
            dma((2, 4)),
            dma((2, 4)),
            dma((4,)),
            dma((4,)),
            dma((2,)),
            dma((2, 14)),
        ],
        compiler_params=pltpu.CompilerParams(
            collective_id=0, has_side_effects=True, vmem_limit_bytes=44 * 2**20
        ),
    )(image_embed, text_embed)
    loss, image_grad, text_grad = pl.pallas_call(
        finish,
        out_shape=(
            shape((1, 1), F32),
            shape((block, width), F32),
            shape((block, width), F32),
        ),
        in_specs=[vmem] * 5,
        out_specs=(pl.BlockSpec(memory_space=pltpu.SMEM), vmem, vmem),
    )(image_embed, text_embed, loss, image_sum, text_sum)
    return loss.reshape(()), image_grad, text_grad


def solution(mesh):
    return jax.shard_map(
        on_device,
        mesh=mesh,
        in_specs=(P(("inner", "outer"), None), P(("inner", "outer"), None)),
        out_specs=(P(), P(("inner", "outer"), None), P(("inner", "outer"), None)),
        check_vma=False,
    )
```

```python
import functools
import math

import jax
import jax.numpy as jnp
from jax import lax
from jax.experimental import pallas as pl
from jax.experimental.pallas import tpu as pltpu
from jax.sharding import PartitionSpec as P

F32, BF16 = jnp.float32, jnp.bfloat16
MESH = pl.DeviceIdType.MESH
OFFSETS = ((0, 0), (0, 1), (0, 3), (0, 2), (1, 0), (1, 1), (1, 3), (1, 2))
PLACE = (0, 2, 3, 4, 1, 5, 6, 7)
RING = 4
SLOTS = 8
LOG2E = math.log2(math.e)


def add_up(values):
    return functools.reduce(jnp.add, values)


class Group:
    def __init__(self, kind):
        inner, outer = lax.axis_index("inner"), lax.axis_index("outer")
        core, chip = lax.rem(outer, 2), outer // 2
        high, x = inner // RING, lax.rem(inner, RING)
        low, y = chip // RING, lax.rem(chip, RING)
        self.kind, self.y = kind, y
        self.place = y if kind else x
        self.cores, self.lows, self.highs = (core, 1 - core), (low, 1 - low), (high, 1 - high)
        self.places = [self.place] + [lax.rem(self.place + n, RING) for n in range(1, RING)]

    def index(self, plane_step, ring_step, core_step=0):
        if self.kind == 0:
            return self.highs[plane_step] * RING + self.places[ring_step]
        chip = self.lows[plane_step] * RING + self.places[ring_step]
        return chip * 2 + self.cores[core_step]

    def device(self, plane_step, ring_step, core_step=0):
        index = self.index(plane_step, ring_step, core_step)
        if self.kind:
            return {"outer": index}
        chip = self.lows[plane_step] * RING + self.y
        return {"inner": index, "outer": chip * 2 + self.cores[0]}

    def flips(self):
        near = self.place + 1 - 2 * lax.rem(self.place, 2)
        two = self.places[2]
        out = []
        for place in (near, two):
            if self.kind:
                out.append({"outer": (self.lows[0] * RING + place) * 2 + self.cores[0]})
            else:
                out.append({"inner": self.highs[0] * RING + place})
        return out


def kernel(
    image_ref,
    text_ref,
    loss_ref,
    image_out,
    text_out,
    image_rows,
    text_rows,
    scores,
    row_top,
    row_sum,
    col_top,
    col_sum,
    row_stats,
    col_stats,
    row_lse,
    col_lse,
    row_wide,
    col_wide,
    w_own,
    w_other,
    w_got,
    image_part,
    text_part,
    image_send,
    text_send,
    image_got,
    text_got,
    loss_out,
    loss_in,
    gather_send,
    gather_recv,
    fwd_send,
    fwd_recv,
    row_ssem,
    row_rsem,
    col_ssem,
    col_rsem,
    loss_ssem,
    loss_rsem,
    w_ssem,
    w_rsem,
    red_ssem,
    red_rsem,
    load_sem,
):
    block, width = image_ref.shape
    half = block // 2
    pair = 2 * block
    scale = width ** (-0.5)
    inner, outer = lax.axis_index("inner"), lax.axis_index("outer")
    groups = (Group(0), Group(1))
    sibling = {"outer": groups[1].index(0, 0, 1)}
    rows = (image_rows, text_rows)

    def remote(src, dst, ssem, rsem, device):
        return pltpu.make_async_remote_copy(
            src_ref=src,
            dst_ref=dst,
            send_sem=ssem,
            recv_sem=rsem,
            device_id=device,
            device_id_type=MESH,
        )

    RIGHT, LEFT, FAR, PARTNER = (0, 1), (0, 3), (0, 2), (1, 0)
    neighbours = [g.device(*o) for g in groups for o in (RIGHT, LEFT, PARTNER)] + [sibling]

    loads = [
        pltpu.make_async_copy(ref, rows[kind].at[0, pl.ds(0, block), :], load_sem.at[kind])
        for kind, ref in ((0, image_ref), (1, text_ref))
    ]
    for c in loads:
        c.start()
    barrier = pltpu.get_barrier_semaphore()
    for device in neighbours:
        pl.semaphore_signal(barrier, inc=1, device_id=device, device_id_type=MESH)

    row_top[...] = jnp.full(row_top.shape, -1e30, F32)
    row_sum[...] = jnp.zeros(row_sum.shape, F32)
    col_top[...] = jnp.full(col_top.shape, -1e30, F32)
    col_sum[...] = jnp.zeros(col_sum.shape, F32)
    for c in loads:
        c.wait()
    pl.semaphore_wait(barrier, len(neighbours))

    away = sorted(OFFSETS[1:], key=lambda o: -(o[0] + min(o[1], RING - o[1])))
    inner_peers = [groups[0].device(*o) for o in away]
    outer_peers = [groups[1].device(*o, c) for o in away for c in (1, 0)] + [sibling]

    def at(kind, core_step, slot, part=None):
        start, size = PLACE[slot] * block, block
        if part is not None:
            start, size = start + part * half, half
        return rows[kind].at[core_step, pl.ds(start, size), :]

    def copy(kind, src, slot, part, offset):
        n = 2 * (slot - 1) + part
        return remote(
            src,
            at(kind, 0, slot, part),
            gather_send.at[kind],
            gather_recv.at[kind, n],
            groups[kind].device(*offset),
        )

    def gather_copies(kind):
        out = {
            (3, 0): copy(kind, at(kind, 0, 2, 0), 3, 0, RIGHT),
            (3, 1): copy(kind, at(kind, 0, 1, 1), 3, 1, LEFT),
            (6, 0): copy(kind, at(kind, 0, 4, 0), 6, 0, RIGHT),
            (5, 0): copy(kind, at(kind, 0, 4, 0), 5, 0, LEFT),
            (7, 0): copy(kind, at(kind, 0, 6, 0), 7, 0, RIGHT),
            (5, 1): copy(kind, at(kind, 0, 1, 1), 5, 1, PARTNER),
            (6, 1): copy(kind, at(kind, 0, 2, 1), 6, 1, PARTNER),
            (7, 1): copy(kind, at(kind, 0, 3, 1), 7, 1, PARTNER),
        }
        for h in (0, 1):
            mine = at(kind, 0, 0, h)
            for slot, offset in ((2, RIGHT), (1, LEFT), (4, PARTNER)):
                out[slot, h] = copy(kind, mine, slot, h, offset)
        return out

    def fwd(kind, slot):
        return remote(
            at(kind, 0, slot),
            at(kind, 1, slot),
            fwd_send.at[kind],
            fwd_recv.at[kind, slot],
            sibling,
        )

    copies = [gather_copies(kind) for kind in (0, 1)]
    fwds = [[fwd(kind, slot) for slot in range(SLOTS)] for kind in (0, 1)]

    def start(*keys):
        for key in keys:
            for kind in (0, 1):
                copies[kind][key].start()

    def arrived(*keys):
        for key in keys:
            for kind in (0, 1):
                copies[kind][key].wait_recv()

    def forward(*slots):
        for slot in slots:
            for kind in (0, 1):
                fwds[kind][slot].start()

    start((4, 0), (2, 1), (1, 1), (4, 1), (2, 0), (1, 0))
    forward(0)

    mine = pl.ds(0, block)
    product = image_rows[0, mine, :].astype(F32) * text_rows[0, mine, :].astype(F32)
    positive = scale * jnp.sum(product, 0, keepdims=True)
    positive = add_up(positive[:, i : i + 128] for i in range(0, width, 128))

    def multiply(a, b):
        image = image_rows[0, pl.ds(a * pair, pair), :]
        for c in (0, 1):
            text = text_rows[c, pl.ds(b * pair, pair), :]
            scores[a, b, :, pl.ds(c * pair, pair)] = (scale * LOG2E) * lax.dot_general(
                image, text, (((1,), (1,)), ((), ())), preferred_element_type=F32
            )

    def count(a, b):
        step = 32
        k = pl.ds(b * 2 * pair, 2 * pair)
        old = col_top[:, k]
        top = old
        for r in range(0, pair, step):
            value = scores[a, b, pl.ds(r, step), :].reshape(step // 8, 8, 2 * pair)
            top = jnp.maximum(top, jnp.max(value, 0))
        total = col_sum[:, k] * jnp.exp2(old - top)
        for r in range(0, pair, step):
            value = scores[a, b, pl.ds(r, step), :]
            here = pl.ds(a * pair + r, step)
            lanes = [value[:, i : i + 128] for i in range(0, 2 * pair, 128)]
            before = row_top[here, :]
            row = functools.reduce(jnp.maximum, lanes, before)
            row_sum[here, :] = row_sum[here, :] * jnp.exp2(before - row) + add_up(
                jnp.exp2(lane - row) for lane in lanes
            )
            row_top[here, :] = row
            value = value.reshape(step // 8, 8, 2 * pair)
            total = total + jnp.sum(jnp.exp2(value - top[None]), 0)
        col_top[:, k] = top
        col_sum[:, k] = total

    waiting = []

    def tiles(todo):
        for a, b in todo:
            multiply(a, b)
            if waiting:
                count(*waiting.pop())
            waiting.append((a, b))

    def shell(n, *slots):
        tiles([(n, b) for b in range(n)])
        sib_arrived(*slots)
        tiles([(a, n) for a in range(n + 1)])

    def sib_arrived(*slots):
        for slot in slots:
            for kind in (0, 1):
                fwds[kind][slot].wait_recv()

    arrived((1, 1))
    start((3, 1), (5, 1))
    arrived((4, 0))
    start((6, 0), (5, 0))
    arrived((2, 1))
    start((6, 1))
    arrived((2, 0))
    start((3, 0))
    arrived((1, 0))
    arrived((4, 1))
    forward(4, 1, 2)
    shell(0, 0, 4)
    arrived((3, 1))
    start((7, 1))
    arrived((6, 0))
    start((7, 0))
    shell(1, 1, 2)
    arrived((3, 0))
    forward(3)
    arrived((5, 0), (5, 1))
    forward(5)
    arrived((6, 1))
    forward(6)
    shell(2, 3, 5)
    arrived((7, 0), (7, 1))
    forward(7)
    shell(3, 6, 7)
    count(*waiting.pop())

    def lse(top, total):
        most = jnp.max(top, 0, keepdims=True)
        total = jnp.sum(total * jnp.exp2(top - most), 0, keepdims=True)
        return most + LOG2E * jnp.log(total)

    for slot, offset in enumerate(OFFSETS):
        place = PLACE[slot]
        for c in (0, 1):
            o = groups[1].index(*offset, c)
            k = pl.ds((place // 2) * 2 * pair + c * pair + (place % 2) * block, block)
            col_stats[outer, pl.ds(o, 1), :] = lse(col_top[:, k], col_sum[:, k])
    for slot, offset in enumerate(OFFSETS):
        i = groups[0].index(*offset)
        r = pl.ds(PLACE[slot] * block, block)
        row_stats[inner, pl.ds(i, 1), :] = lse(
            jnp.transpose(row_top[r, :]), jnp.transpose(row_sum[r, :])
        )
    row_stats[inner, pl.ds(SLOTS, 8), :] = jnp.concatenate(
        [positive, jnp.zeros((7, 128), F32)], 0
    )

    def spread(ref, me, ssem, rsem, peers):
        for device in peers:
            remote(ref.at[me], ref.at[me], ssem, rsem, device).start()
        every = ref.at[pl.ds(0, len(peers))]
        return remote(every, every, ssem, rsem, sibling)

    col_out = spread(col_stats, outer, col_ssem.at[0], col_rsem.at[0], outer_peers)
    row_out = spread(row_stats, inner, row_ssem.at[0], row_rsem.at[0], inner_peers)
    row_out.wait_recv()
    col_out.wait_recv()

    def combine(ref, count):
        values = [ref[n, 0:count, :] for n in range(count)]
        top = functools.reduce(jnp.maximum, values)
        return top + LOG2E * jnp.log(add_up([jnp.exp2(value - top) for value in values]))

    row_value = combine(row_stats, SLOTS)
    col_value = combine(col_stats, 2 * SLOTS)
    row_lse[...] = row_value
    col_lse[...] = col_value
    for slot, offset in enumerate(OFFSETS):
        i = groups[0].index(*offset)
        line = row_lse[pl.ds(i, 1), :]
        place = PLACE[slot]
        row_wide[pl.ds(place * block, block), :] = jnp.transpose(
            jnp.broadcast_to(line, (block, block))
        )
        for c in (0, 1):
            o = groups[1].index(*offset, c)
            k = pl.ds((place // 2) * 2 * pair + c * pair + (place % 2) * block, block)
            col_wide[:, k] = col_lse[pl.ds(o, 1), :]

    def weigh(a, b):
        step = 32
        for r in range(0, pair, step):
            here = pl.ds(a * pair + r, step)
            line = jnp.concatenate([row_wide[here, :]] * 2, 1)
            for c, out in ((0, w_own), (1, w_other)):
                value = scores[a, b, pl.ds(r, step), pl.ds(c * pair, pair)]
                there = pl.ds((2 * b + c) * pair, pair)
                weight = jnp.exp2(value - line) + jnp.exp2(value - col_wide[:, there])
                out[b, here, :] = weight.astype(BF16)

    w_copies = [
        remote(w_other.at[b], w_got.at[b], w_ssem.at[b], w_rsem.at[b], sibling) for b in range(4)
    ]
    weighed = set()

    def weigh_pair(g):
        for a, b in [(a, g) for a in range(4)] + [(g, b) for b in range(4)]:
            if (a, b) not in weighed:
                weighed.add((a, b))
                weigh(a, b)
            if len([1 for w in weighed if w[1] == g]) == 4 and (g, "sent") not in weighed:
                weighed.add((g, "sent"))
                w_copies[g].start()

    paired = add_up([row_stats[n, pl.ds(SLOTS, 8), :] for n in range(SLOTS)])
    shares = (
        row_value * (1.0 / LOG2E) - 2.0 * paired,
        (col_value[0:8] + col_value[8:16]) * (1.0 / LOG2E),
    )
    others = (
        [sibling, groups[1].device(*PARTNER)] + groups[1].flips(),
        [groups[0].device(*PARTNER)] + groups[0].flips(),
    )
    loss_copies = [
        [
            remote(
                loss_out.at[kind, n],
                loss_in.at[kind, n],
                loss_ssem.at[kind, n],
                loss_rsem.at[kind, n],
                device,
            )
            for n, device in enumerate(others[kind])
        ]
        for kind in (0, 1)
    ]

    def loss_step(kind, n):
        if n == 0:
            value = shares[kind]
        else:
            loss_copies[kind][n - 1].wait_recv()
            value = loss_out[kind, n - 1] + loss_in[kind, n - 1]
        if n < len(others[kind]):
            loss_out[kind, n] = value
            loss_copies[kind][n].start()
        return value

    loss_step(0, 0)
    loss_step(1, 0)

    parts = (image_part, text_part)
    sends = (image_send, text_send)
    gots = (image_got, text_got)

    def lines(slot, h):
        return pl.ds(PLACE[slot] * block + h * half, half)

    def red_copies(kind):
        way = {(7, 0): RIGHT, (5, 0): RIGHT, (6, 0): LEFT, (3, 0): RIGHT, (3, 1): LEFT}
        way.update({(1, h): RIGHT for h in (0, 1)})
        way.update({(2, h): LEFT for h in (0, 1)})
        way.update({(slot, 1): PARTNER for slot in (4, 5, 6, 7)})
        way[4, 0] = PARTNER
        return {
            key: remote(
                sends[kind].at[lines(*key), :],
                gots[kind].at[n],
                red_ssem.at[kind],
                red_rsem.at[kind, n],
                groups[kind].device(*way[key]),
            )
            for n, key in enumerate(sorted(way))
        }

    reds = [red_copies(kind) for kind in (0, 1)]
    numbers = {key: n for n, key in enumerate(sorted(reds[0]))}

    def total_of(kind, slot, h, *keys):
        value = parts[kind][lines(slot, h), :]
        for key in keys:
            reds[kind][key].wait_recv()
            value = value + gots[kind][numbers[key]].astype(F32)
        return value

    def pass_on(kind, slot, h, *keys):
        sends[kind][lines(slot, h), :] = total_of(kind, slot, h, *keys).astype(BF16)
        reds[kind][slot, h].start()

    def image_pair(g):
        r = pl.ds(g * pair, pair)
        image_part[r, :] = add_up(
            jnp.dot(
                jnp.concatenate([w[b, r, :] for b in range(4)], 1),
                text_rows[c],
                preferred_element_type=F32,
            )
            for c, w in ((0, w_own), (1, w_other))
        )

    def text_pair(g):
        text_part[pl.ds(g * pair, pair), :] = add_up(
            lax.dot_general(
                w[g], image_rows[c], (((0,), (0,)), ((), ())), preferred_element_type=F32
            )
            for c, w in ((0, w_own), (1, w_got))
        )

    def products(g, following, *ready):
        image_pair(g)
        for slot, h in ready:
            pass_on(0, slot, h)
        if following is not None:
            weigh_pair(following)
        w_copies[g].wait_recv()
        text_pair(g)
        for slot, h in ready:
            pass_on(1, slot, h)

    def both(slot, h, *keys):
        for kind in (0, 1):
            pass_on(kind, slot, h, *keys)

    weigh_pair(3)
    products(3, 2, (7, 1), (7, 0), (6, 0), (6, 1))
    loss_step(0, 1)
    loss_step(1, 1)
    products(2, 1, (3, 0), (5, 1))
    loss_step(0, 2)
    loss_step(1, 2)
    both(3, 1, (7, 1))
    both(5, 0, (7, 0))
    products(1, 0, (2, 0))
    loss_step(0, 3)
    products(0, None, (4, 1))
    both(1, 0, (3, 0))
    both(4, 0, (5, 0), (6, 0))
    both(1, 1, (5, 1))
    both(2, 1, (6, 1), (3, 1))
    loss = loss_step(0, 4) + loss_step(1, 3)
    loss = jnp.sum(jnp.sum(loss, 0, keepdims=True), 1, keepdims=True)
    total_rows = block * 2 * SLOTS * SLOTS
    loss_ref[...] = jnp.broadcast_to(loss / (2.0 * total_rows), loss_ref.shape)

    for h, keys in ((0, ((1, 0), (2, 0), (4, 0))), (1, ((4, 1), (1, 1), (2, 1)))):
        r = pl.ds(h * half, half)
        for kind, out in ((0, image_out), (1, text_out)):
            out[r, :] = total_of(kind, 0, h, *keys)

    for kind in (0, 1):
        sent = rows[kind].at[0, pl.ds(0, 14 * half), :]
        remote(sent, sent, gather_send.at[kind], gather_recv.at[kind, 0], sibling).wait_send()
        sent = rows[kind].at[0]
        remote(sent, sent, fwd_send.at[kind], fwd_recv.at[kind, 0], sibling).wait_send()
        sent = sends[kind].at[pl.ds(0, 14 * half), :]
        remote(sent, sent, red_ssem.at[kind], red_rsem.at[kind, 0], sibling).wait_send()
    for c in w_copies + loss_copies[0] + loss_copies[1] + [row_out, col_out]:
        c.wait_send()


def finish(image_ref, text_ref, loss_ref, image_sum, text_sum, loss_out, image_out, text_out):
    half_scale = 0.5 * image_ref.shape[1] ** (-0.5)
    image_out[...] = half_scale * (image_sum[...] - 2.0 * text_ref[...].astype(F32))
    text_out[...] = half_scale * (text_sum[...] - 2.0 * image_ref[...].astype(F32))
    loss_out[0, 0] = loss_ref[0, 0]


def on_device(image_embed, text_embed):
    block, width = image_embed.shape
    group = SLOTS * block
    dma = pltpu.SemaphoreType.DMA
    shape = jax.ShapeDtypeStruct
    vmem = pl.BlockSpec(memory_space=pltpu.VMEM)
    loss, image_sum, text_sum = pl.pallas_call(
        kernel,
        out_shape=(
            shape((8, 128), F32),
            shape((block, width), F32),
            shape((block, width), F32),
        ),
        in_specs=[pl.BlockSpec(memory_space=pltpu.HBM)] * 2,
        out_specs=(vmem, vmem, vmem),
        scratch_shapes=[
            pltpu.VMEM((2, group, width), BF16),
            pltpu.VMEM((2, group, width), BF16),
            pltpu.VMEM((4, 4, 2 * block, 4 * block), F32),
            pltpu.VMEM((group, 128), F32),
            pltpu.VMEM((group, 128), F32),
            pltpu.VMEM((8, 2 * group), F32),
            pltpu.VMEM((8, 2 * group), F32),
            pltpu.VMEM((SLOTS, 2 * SLOTS, 128), F32),
            pltpu.VMEM((2 * SLOTS, 2 * SLOTS, 128), F32),
            pltpu.VMEM((SLOTS, 128), F32),
            pltpu.VMEM((2 * SLOTS, 128), F32),
            pltpu.VMEM((group, 128), F32),
            pltpu.VMEM((1, 2 * group), F32),
            pltpu.VMEM((4, group, 2 * block), BF16),
            pltpu.VMEM((4, group, 2 * block), BF16),
            pltpu.VMEM((4, group, 2 * block), BF16),
            pltpu.VMEM((group, width), F32),
            pltpu.VMEM((group, width), F32),
            pltpu.VMEM((group, width), BF16),
            pltpu.VMEM((group, width), BF16),
            pltpu.VMEM((14, block // 2, width), BF16),
            pltpu.VMEM((14, block // 2, width), BF16),
            pltpu.VMEM((2, 4, 8, 128), F32),
            pltpu.VMEM((2, 4, 8, 128), F32),
            dma((2,)),
            dma((2, 14)),
            dma((2,)),
            dma((2, SLOTS)),
            dma((1,)),
            dma((1,)),
            dma((1,)),
            dma((1,)),
            dma((2, 4)),
            dma((2, 4)),
            dma((4,)),
            dma((4,)),
            dma((2,)),
            dma((2, 14)),
            dma((2,)),
        ],
        compiler_params=pltpu.CompilerParams(
            collective_id=0, has_side_effects=True, vmem_limit_bytes=56 * 2**20
        ),
    )(image_embed, text_embed)
    loss, image_grad, text_grad = pl.pallas_call(
        finish,
        out_shape=(
            shape((1, 1), F32),
            shape((block, width), F32),
            shape((block, width), F32),
        ),
        in_specs=[vmem] * 5,
        out_specs=(pl.BlockSpec(memory_space=pltpu.SMEM), vmem, vmem),
    )(image_embed, text_embed, loss, image_sum, text_sum)
    return loss.reshape(()), image_grad, text_grad


def solution(mesh):
    return jax.shard_map(
        on_device,
        mesh=mesh,
        in_specs=(P(("inner", "outer"), None), P(("inner", "outer"), None)),
        out_specs=(P(), P(("inner", "outer"), None), P(("inner", "outer"), None)),
        check_vma=False,
    )
```

```python
import functools
import math

import jax
import jax.numpy as jnp
from jax import lax
from jax.experimental import pallas as pl
from jax.experimental.pallas import tpu as pltpu
from jax.sharding import PartitionSpec as P

F32, BF16 = jnp.float32, jnp.bfloat16
MESH = pl.DeviceIdType.MESH
OFFSETS = ((0, 0), (0, 1), (0, 3), (0, 2), (1, 0), (1, 1), (1, 3), (1, 2))
PLACE = (0, 2, 3, 4, 1, 5, 6, 7)
RING = 4
SLOTS = 8
LOG2E = math.log2(math.e)


def add_up(values):
    return functools.reduce(jnp.add, values)


class Group:
    def __init__(self, kind):
        inner, outer = lax.axis_index("inner"), lax.axis_index("outer")
        core, chip = lax.rem(outer, 2), outer // 2
        high, x = inner // RING, lax.rem(inner, RING)
        low, y = chip // RING, lax.rem(chip, RING)
        self.kind, self.y = kind, y
        self.place = y if kind else x
        self.cores, self.lows, self.highs = (core, 1 - core), (low, 1 - low), (high, 1 - high)
        self.places = [self.place] + [lax.rem(self.place + n, RING) for n in range(1, RING)]

    def index(self, plane_step, ring_step, core_step=0):
        if self.kind == 0:
            return self.highs[plane_step] * RING + self.places[ring_step]
        chip = self.lows[plane_step] * RING + self.places[ring_step]
        return chip * 2 + self.cores[core_step]

    def device(self, plane_step, ring_step, core_step=0):
        index = self.index(plane_step, ring_step, core_step)
        if self.kind:
            return {"outer": index}
        chip = self.lows[plane_step] * RING + self.y
        return {"inner": index, "outer": chip * 2 + self.cores[0]}


def kernel(
    image_ref,
    text_ref,
    loss_ref,
    image_out,
    text_out,
    image_rows,
    text_rows,
    scores,
    row_top,
    row_sum,
    col_top,
    col_sum,
    row_stats,
    col_stats,
    row_lse,
    col_lse,
    row_wide,
    col_wide,
    w_own,
    w_other,
    w_got,
    image_part,
    text_part,
    image_send,
    text_send,
    image_got,
    text_got,
    image_loss,
    image_loss_ring,
    text_loss,
    text_loss_ring,
    gather_send,
    gather_recv,
    fwd_send,
    fwd_recv,
    row_ssem,
    row_rsem,
    col_ssem,
    col_rsem,
    loss_ssem,
    loss_rsem,
    w_ssem,
    w_rsem,
    red_ssem,
    red_rsem,
    load_sem,
):
    block, width = image_ref.shape
    half = block // 2
    pair = 2 * block
    scale = width ** (-0.5)
    inner, outer = lax.axis_index("inner"), lax.axis_index("outer")
    groups = (Group(0), Group(1))
    sibling = {"outer": groups[1].index(0, 0, 1)}
    rows = (image_rows, text_rows)

    def remote(src, dst, ssem, rsem, device):
        return pltpu.make_async_remote_copy(
            src_ref=src,
            dst_ref=dst,
            send_sem=ssem,
            recv_sem=rsem,
            device_id=device,
            device_id_type=MESH,
        )

    RIGHT, LEFT, FAR, PARTNER = (0, 1), (0, 3), (0, 2), (1, 0)
    neighbours = [g.device(*o) for g in groups for o in (RIGHT, LEFT, PARTNER)] + [sibling]

    loads = [
        pltpu.make_async_copy(ref, rows[kind].at[0, pl.ds(0, block), :], load_sem.at[kind])
        for kind, ref in ((0, image_ref), (1, text_ref))
    ]
    for c in loads:
        c.start()
    barrier = pltpu.get_barrier_semaphore()
    for device in neighbours:
        pl.semaphore_signal(barrier, inc=1, device_id=device, device_id_type=MESH)

    row_top[...] = jnp.full(row_top.shape, -1e30, F32)
    row_sum[...] = jnp.zeros(row_sum.shape, F32)
    col_top[...] = jnp.full(col_top.shape, -1e30, F32)
    col_sum[...] = jnp.zeros(col_sum.shape, F32)
    for c in loads:
        c.wait()
    pl.semaphore_wait(barrier, len(neighbours))

    away = sorted(OFFSETS[1:], key=lambda o: -(o[0] + min(o[1], RING - o[1])))
    inner_peers = [groups[0].device(*o) for o in away]
    outer_peers = [groups[1].device(*o, c) for o in away for c in (1, 0)] + [sibling]

    def at(kind, core_step, slot, part=None):
        start, size = PLACE[slot] * block, block
        if part is not None:
            start, size = start + part * half, half
        return rows[kind].at[core_step, pl.ds(start, size), :]

    def copy(kind, src, slot, part, offset):
        n = 2 * (slot - 1) + part
        return remote(
            src,
            at(kind, 0, slot, part),
            gather_send.at[kind],
            gather_recv.at[kind, n],
            groups[kind].device(*offset),
        )

    def gather_copies(kind):
        out = {
            (3, 0): copy(kind, at(kind, 0, 2, 0), 3, 0, RIGHT),
            (3, 1): copy(kind, at(kind, 0, 1, 1), 3, 1, LEFT),
            (6, 0): copy(kind, at(kind, 0, 4, 0), 6, 0, RIGHT),
            (5, 0): copy(kind, at(kind, 0, 4, 0), 5, 0, LEFT),
            (7, 0): copy(kind, at(kind, 0, 6, 0), 7, 0, RIGHT),
            (5, 1): copy(kind, at(kind, 0, 1, 1), 5, 1, PARTNER),
            (6, 1): copy(kind, at(kind, 0, 2, 1), 6, 1, PARTNER),
            (7, 1): copy(kind, at(kind, 0, 3, 1), 7, 1, PARTNER),
        }
        for h in (0, 1):
            mine = at(kind, 0, 0, h)
            for slot, offset in ((2, RIGHT), (1, LEFT), (4, PARTNER)):
                out[slot, h] = copy(kind, mine, slot, h, offset)
        return out

    PARCELS = ((0, 2), (2, 2), (4, 2), (6, 1), (7, 1))

    def fwd(kind, n):
        first, count = PARCELS[n]
        here = pl.ds(first * block, count * block)
        return remote(
            rows[kind].at[0, here, :],
            rows[kind].at[1, here, :],
            fwd_send.at[kind],
            fwd_recv.at[kind, n],
            sibling,
        )

    copies = [gather_copies(kind) for kind in (0, 1)]
    fwds = [[fwd(kind, n) for n in range(len(PARCELS))] for kind in (0, 1)]

    def start(*keys):
        for key in keys:
            for kind in (0, 1):
                copies[kind][key].start()

    def arrived(*keys):
        for key in keys:
            for kind in (0, 1):
                copies[kind][key].wait_recv()

    def forward(*parcels):
        for n in parcels:
            for kind in (0, 1):
                fwds[kind][n].start()

    start((4, 0), (2, 1), (1, 1), (4, 1), (2, 0), (1, 0))

    mine = pl.ds(0, block)
    product = image_rows[0, mine, :].astype(F32) * text_rows[0, mine, :].astype(F32)
    positive = scale * jnp.sum(product, 0, keepdims=True)
    positive = add_up(positive[:, i : i + 128] for i in range(0, width, 128))

    def multiply(a, b):
        image = image_rows[0, pl.ds(a * pair, pair), :]
        for c in (0, 1):
            text = text_rows[c, pl.ds(b * pair, pair), :]
            scores[a, b, :, pl.ds(c * pair, pair)] = (scale * LOG2E) * lax.dot_general(
                image, text, (((1,), (1,)), ((), ())), preferred_element_type=F32
            )

    def count(a, b):
        step = 32
        k = pl.ds(b * 2 * pair, 2 * pair)
        old = col_top[:, k]
        top = old
        for r in range(0, pair, step):
            value = scores[a, b, pl.ds(r, step), :].reshape(step // 8, 8, 2 * pair)
            top = jnp.maximum(top, jnp.max(value, 0))
        total = col_sum[:, k] * jnp.exp2(old - top)
        for r in range(0, pair, step):
            value = scores[a, b, pl.ds(r, step), :]
            here = pl.ds(a * pair + r, step)
            lanes = [value[:, i : i + 128] for i in range(0, 2 * pair, 128)]
            before = row_top[here, :]
            row = functools.reduce(jnp.maximum, lanes, before)
            row_sum[here, :] = row_sum[here, :] * jnp.exp2(before - row) + add_up(
                jnp.exp2(lane - row) for lane in lanes
            )
            row_top[here, :] = row
            value = value.reshape(step // 8, 8, 2 * pair)
            total = total + jnp.sum(jnp.exp2(value - top[None]), 0)
        col_top[:, k] = top
        col_sum[:, k] = total

    waiting = []

    def tiles(todo):
        for a, b in todo:
            multiply(a, b)
            if waiting:
                count(*waiting.pop())
            waiting.append((a, b))

    def shell(n, *parcels):
        tiles([(n, b) for b in range(n)])
        sib_arrived(*parcels)
        tiles([(a, n) for a in range(n + 1)])

    def sib_arrived(*parcels):
        for n in parcels:
            for kind in (0, 1):
                fwds[kind][n].wait_recv()

    arrived((1, 1))
    start((3, 1), (5, 1))
    arrived((4, 0))
    start((6, 0), (5, 0))
    arrived((2, 1))
    start((6, 1))
    arrived((2, 0))
    start((3, 0))
    arrived((1, 0))
    arrived((4, 1))
    forward(0, 1)
    arrived((3, 1))
    start((7, 1))
    arrived((6, 0))
    start((7, 0))
    shell(0, 0)
    shell(1, 1)
    arrived((3, 0), (5, 0), (5, 1))
    forward(2)
    arrived((6, 1))
    forward(3)
    shell(2, 2)
    arrived((7, 0), (7, 1))
    forward(4)
    shell(3, 3, 4)
    count(*waiting.pop())

    def lse(top, total):
        most = jnp.max(top, 0, keepdims=True)
        total = jnp.sum(total * jnp.exp2(top - most), 0, keepdims=True)
        return most + LOG2E * jnp.log(total)

    for slot, offset in enumerate(OFFSETS):
        place = PLACE[slot]
        for c in (0, 1):
            o = groups[1].index(*offset, c)
            k = pl.ds((place // 2) * 2 * pair + c * pair + (place % 2) * block, block)
            col_stats[outer, pl.ds(o, 1), :] = lse(col_top[:, k], col_sum[:, k])
    for slot, offset in enumerate(OFFSETS):
        i = groups[0].index(*offset)
        r = pl.ds(PLACE[slot] * block, block)
        row_stats[inner, pl.ds(i, 1), :] = lse(
            jnp.transpose(row_top[r, :]), jnp.transpose(row_sum[r, :])
        )
    row_stats[inner, pl.ds(SLOTS, 8), :] = jnp.concatenate(
        [positive, jnp.zeros((7, 128), F32)], 0
    )

    def spread(ref, me, ssem, rsem, peers):
        for device in peers:
            remote(ref.at[me], ref.at[me], ssem, rsem, device).start()
        every = ref.at[pl.ds(0, len(peers))]
        return remote(every, every, ssem, rsem, sibling)

    col_out = spread(col_stats, outer, col_ssem.at[0], col_rsem.at[0], outer_peers)
    row_out = spread(row_stats, inner, row_ssem.at[0], row_rsem.at[0], inner_peers)
    row_out.wait_recv()
    col_out.wait_recv()

    def combine(ref, count):
        values = [ref[n, 0:count, :] for n in range(count)]
        top = functools.reduce(jnp.maximum, values)
        return top + LOG2E * jnp.log(add_up([jnp.exp2(value - top) for value in values]))

    row_value = combine(row_stats, SLOTS)
    col_value = combine(col_stats, 2 * SLOTS)
    row_lse[...] = row_value
    col_lse[...] = col_value
    for slot, offset in enumerate(OFFSETS):
        i = groups[0].index(*offset)
        line = row_lse[pl.ds(i, 1), :]
        place = PLACE[slot]
        row_wide[pl.ds(place * block, block), :] = jnp.transpose(
            jnp.broadcast_to(line, (block, block))
        )
        for c in (0, 1):
            o = groups[1].index(*offset, c)
            k = pl.ds((place // 2) * 2 * pair + c * pair + (place % 2) * block, block)
            col_wide[:, k] = col_lse[pl.ds(o, 1), :]

    def weigh(a, b):
        step = 32
        for r in range(0, pair, step):
            here = pl.ds(a * pair + r, step)
            line = jnp.concatenate([row_wide[here, :]] * 2, 1)
            for c, out in ((0, w_own), (1, w_other)):
                value = scores[a, b, pl.ds(r, step), pl.ds(c * pair, pair)]
                there = pl.ds((2 * b + c) * pair, pair)
                weight = jnp.exp2(value - line) + jnp.exp2(value - col_wide[:, there])
                out[b, here, :] = weight.astype(BF16)

    w_copies = [
        remote(w_other.at[b], w_got.at[b], w_ssem.at[b], w_rsem.at[b], sibling) for b in range(4)
    ]
    weighed = set()

    def weigh_jobs(g):
        todo = [t for t in [(a, g) for a in range(4)] + [(g, b) for b in range(4)] if t not in weighed]
        todo = sorted(set(todo), key=todo.index)
        weighed.update(todo)
        return [functools.partial(weigh, *t) for t in todo]

    paired = add_up([row_stats[n, pl.ds(SLOTS, 8), :] for n in range(SLOTS)])
    shares = (
        row_value * (1.0 / LOG2E) - 2.0 * paired,
        (col_value[0:8] + col_value[8:16]) * (1.0 / LOG2E),
    )
    high, low, core = groups[0].highs[0], groups[0].lows[0], groups[0].cores[0]
    who = (2 * lax.rem(high + low, 2) + core, high)
    others = (
        [groups[1].device(1, 0, 1), groups[1].device(*PARTNER), sibling],
        [groups[0].device(*PARTNER)],
    )
    losses = ((image_loss, image_loss_ring), (text_loss, text_loss_ring))

    def loss_near(kind):
        losses[kind][0][who[kind]] = shares[kind]
        return spread(
            losses[kind][0], who[kind], loss_ssem.at[kind, 0], loss_rsem.at[kind, 0], others[kind]
        )

    def loss_ring(kind, near):
        group = groups[1 - kind]
        near.wait_recv()
        ref = losses[kind][0]
        losses[kind][1][group.place] = add_up([ref[n] for n in range(ref.shape[0])])
        return spread(
            losses[kind][1],
            group.place,
            loss_ssem.at[kind, 1],
            loss_rsem.at[kind, 1],
            [group.device(0, n) for n in (2, 1, 3)],
        )

    def loss_sum(kind, ring):
        ring.wait_recv()
        return add_up([losses[kind][1][n] for n in range(RING)])

    parts = (image_part, text_part)
    sends = (image_send, text_send)
    gots = (image_got, text_got)

    def lines(slot, h):
        return pl.ds(PLACE[slot] * block + h * half, half)

    def red_copies(kind):
        way = {(7, 0): RIGHT, (5, 0): RIGHT, (6, 0): LEFT, (3, 0): RIGHT, (3, 1): LEFT}
        way.update({(1, h): RIGHT for h in (0, 1)})
        way.update({(2, h): LEFT for h in (0, 1)})
        way.update({(slot, 1): PARTNER for slot in (4, 5, 6, 7)})
        way[4, 0] = PARTNER
        return {
            key: remote(
                sends[kind].at[lines(*key), :],
                gots[kind].at[n],
                red_ssem.at[kind],
                red_rsem.at[kind, n],
                groups[kind].device(*way[key]),
            )
            for n, key in enumerate(sorted(way))
        }

    reds = [red_copies(kind) for kind in (0, 1)]
    numbers = {key: n for n, key in enumerate(sorted(reds[0]))}

    def total_of(kind, slot, h, *keys):
        value = parts[kind][lines(slot, h), :]
        for key in keys:
            reds[kind][key].wait_recv()
            value = value + gots[kind][numbers[key]].astype(F32)
        return value

    READY = {(7, 0), (7, 1), (6, 0), (6, 1), (3, 0), (5, 1), (2, 0), (4, 1)}

    def pass_on(kind, slot, h, *keys):
        if (slot, h) not in READY:
            sends[kind][lines(slot, h), :] = total_of(kind, slot, h, *keys).astype(BF16)
        reds[kind][slot, h].start()

    def product(kind, g, jobs=()):
        chunks = width // pair
        for n in range(chunks):
            k = pl.ds(n * pair, pair)
            if kind == 0:
                value = add_up(
                    [
                        jnp.dot(
                            jnp.concatenate([w[b, pl.ds(g * pair, pair), :] for b in range(4)], 1),
                            text_rows[c, :, k],
                            preferred_element_type=F32,
                        )
                        for c, w in ((0, w_own), (1, w_other))
                    ]
                )
            else:
                value = add_up(
                    [
                        lax.dot_general(
                            w[g],
                            image_rows[c, :, k],
                            (((0,), (0,)), ((), ())),
                            preferred_element_type=F32,
                        )
                        for c, w in ((0, w_own), (1, w_got))
                    ]
                )
            for job in jobs[n::chunks]:
                job()
            for i in range(4):
                slot, h = PLACE.index(2 * g + i // 2), i % 2
                piece = value[i * half : (i + 1) * half]
                if (slot, h) in READY:
                    sends[kind][lines(slot, h), k] = piece.astype(BF16)
                else:
                    parts[kind][lines(slot, h), k] = piece

    def products(g, following, beside, *ready):
        product(0, g, weigh_jobs(following) if following is not None else ())
        for slot, h in ready:
            pass_on(0, slot, h)
        if following is not None:
            w_copies[following].start()
        w_copies[g].wait_recv()
        product(1, g, weigh_jobs(beside) if beside is not None else ())
        for slot, h in ready:
            pass_on(1, slot, h)
        if beside is not None:
            w_copies[beside].start()

    def both(slot, h, *keys):
        for kind in (0, 1):
            pass_on(kind, slot, h, *keys)

    for n, job in enumerate(weigh_jobs(3)):
        job()
        if n == 3:
            w_copies[3].start()
    near_copies = [loss_near(kind) for kind in (0, 1)]
    products(3, 2, 1, (7, 1), (7, 0), (6, 0), (6, 1))
    ring_copies = [loss_ring(kind, near_copies[kind]) for kind in (0, 1)]
    products(2, 0, None, (3, 0), (5, 1))
    both(3, 1, (7, 1))
    both(5, 0, (7, 0))
    products(1, None, None, (2, 0))
    products(0, None, None, (4, 1))
    both(1, 0, (3, 0))
    both(2, 1, (6, 1), (3, 1))
    both(4, 0, (5, 0), (6, 0))
    both(1, 1, (5, 1))
    loss = loss_sum(0, ring_copies[0]) + loss_sum(1, ring_copies[1])
    loss = jnp.sum(jnp.sum(loss, 0, keepdims=True), 1, keepdims=True)
    total_rows = block * 2 * SLOTS * SLOTS
    loss_ref[...] = jnp.broadcast_to(loss / (2.0 * total_rows), loss_ref.shape)

    for h, keys in ((0, ((1, 0), (2, 0), (4, 0))), (1, ((4, 1), (1, 1), (2, 1)))):
        r = pl.ds(h * half, half)
        for kind, out in ((0, image_out), (1, text_out)):
            out[r, :] = total_of(kind, 0, h, *keys)

    for kind in (0, 1):
        sent = rows[kind].at[0, pl.ds(0, 14 * half), :]
        remote(sent, sent, gather_send.at[kind], gather_recv.at[kind, 0], sibling).wait_send()
        sent = rows[kind].at[0]
        remote(sent, sent, fwd_send.at[kind], fwd_recv.at[kind, 0], sibling).wait_send()
        sent = sends[kind].at[pl.ds(0, 14 * half), :]
        remote(sent, sent, red_ssem.at[kind], red_rsem.at[kind, 0], sibling).wait_send()
    for c in w_copies + near_copies + ring_copies + [row_out, col_out]:
        c.wait_send()


def finish(image_ref, text_ref, loss_ref, image_sum, text_sum, loss_out, image_out, text_out):
    half_scale = 0.5 * image_ref.shape[1] ** (-0.5)
    image_out[...] = half_scale * (image_sum[...] - 2.0 * text_ref[...].astype(F32))
    text_out[...] = half_scale * (text_sum[...] - 2.0 * image_ref[...].astype(F32))
    loss_out[0, 0] = loss_ref[0, 0]


def on_device(image_embed, text_embed):
    block, width = image_embed.shape
    group = SLOTS * block
    dma = pltpu.SemaphoreType.DMA
    shape = jax.ShapeDtypeStruct
    vmem = pl.BlockSpec(memory_space=pltpu.VMEM)
    loss, image_sum, text_sum = pl.pallas_call(
        kernel,
        out_shape=(
            shape((8, 128), F32),
            shape((block, width), F32),
            shape((block, width), F32),
        ),
        in_specs=[pl.BlockSpec(memory_space=pltpu.HBM)] * 2,
        out_specs=(vmem, vmem, vmem),
        scratch_shapes=[
            pltpu.VMEM((2, group, width), BF16),
            pltpu.VMEM((2, group, width), BF16),
            pltpu.VMEM((4, 4, 2 * block, 4 * block), F32),
            pltpu.VMEM((group, 128), F32),
            pltpu.VMEM((group, 128), F32),
            pltpu.VMEM((8, 2 * group), F32),
            pltpu.VMEM((8, 2 * group), F32),
            pltpu.VMEM((SLOTS, 2 * SLOTS, 128), F32),
            pltpu.VMEM((2 * SLOTS, 2 * SLOTS, 128), F32),
            pltpu.VMEM((SLOTS, 128), F32),
            pltpu.VMEM((2 * SLOTS, 128), F32),
            pltpu.VMEM((group, 128), F32),
            pltpu.VMEM((1, 2 * group), F32),
            pltpu.VMEM((4, group, 2 * block), BF16),
            pltpu.VMEM((4, group, 2 * block), BF16),
            pltpu.VMEM((4, group, 2 * block), BF16),
            pltpu.VMEM((group, width), F32),
            pltpu.VMEM((group, width), F32),
            pltpu.VMEM((group, width), BF16),
            pltpu.VMEM((group, width), BF16),
            pltpu.VMEM((14, block // 2, width), BF16),
            pltpu.VMEM((14, block // 2, width), BF16),
            pltpu.VMEM((4, 8, 128), F32),
            pltpu.VMEM((RING, 8, 128), F32),
            pltpu.VMEM((2, 8, 128), F32),
            pltpu.VMEM((RING, 8, 128), F32),
            dma((2,)),
            dma((2, 14)),
            dma((2,)),
            dma((2, 5)),
            dma((1,)),
            dma((1,)),
            dma((1,)),
            dma((1,)),
            dma((2, 2)),
            dma((2, 2)),
            dma((4,)),
            dma((4,)),
            dma((2,)),
            dma((2, 14)),
            dma((2,)),
        ],
        compiler_params=pltpu.CompilerParams(
            collective_id=0, has_side_effects=True, vmem_limit_bytes=56 * 2**20
        ),
    )(image_embed, text_embed)
    loss, image_grad, text_grad = pl.pallas_call(
        finish,
        out_shape=(
            shape((1, 1), F32),
            shape((block, width), F32),
            shape((block, width), F32),
        ),
        in_specs=[vmem] * 5,
        out_specs=(pl.BlockSpec(memory_space=pltpu.SMEM), vmem, vmem),
    )(image_embed, text_embed, loss, image_sum, text_sum)
    return loss.reshape(()), image_grad, text_grad


def solution(mesh):
    return jax.shard_map(
        on_device,
        mesh=mesh,
        in_specs=(P(("inner", "outer"), None), P(("inner", "outer"), None)),
        out_specs=(P(), P(("inner", "outer"), None), P(("inner", "outer"), None)),
        check_vma=False,
    )
```

```python
import functools
import math

import jax
import jax.numpy as jnp
from jax import lax
from jax.experimental import pallas as pl
from jax.experimental.pallas import tpu as pltpu
from jax.sharding import PartitionSpec as P

F32, BF16 = jnp.float32, jnp.bfloat16
MESH = pl.DeviceIdType.MESH
OFFSETS = ((0, 0), (0, 1), (0, 3), (0, 2), (1, 0), (1, 1), (1, 3), (1, 2))
PLACE = (0, 2, 3, 4, 1, 5, 6, 7)
RING = 4
SLOTS = 8
LOG2E = math.log2(math.e)


def add_up(values):
    return functools.reduce(jnp.add, values)


class Group:
    def __init__(self, kind):
        inner, outer = lax.axis_index("inner"), lax.axis_index("outer")
        core, chip = lax.rem(outer, 2), outer // 2
        high, x = inner // RING, lax.rem(inner, RING)
        low, y = chip // RING, lax.rem(chip, RING)
        self.kind, self.y = kind, y
        self.place = y if kind else x
        self.cores, self.lows, self.highs = (core, 1 - core), (low, 1 - low), (high, 1 - high)
        self.places = [self.place] + [lax.rem(self.place + n, RING) for n in range(1, RING)]

    def index(self, plane_step, ring_step, core_step=0):
        if self.kind == 0:
            return self.highs[plane_step] * RING + self.places[ring_step]
        chip = self.lows[plane_step] * RING + self.places[ring_step]
        return chip * 2 + self.cores[core_step]

    def device(self, plane_step, ring_step, core_step=0):
        index = self.index(plane_step, ring_step, core_step)
        if self.kind:
            return {"outer": index}
        chip = self.lows[plane_step] * RING + self.y
        return {"inner": index, "outer": chip * 2 + self.cores[0]}


def kernel(
    image_ref,
    text_ref,
    loss_ref,
    image_out,
    text_out,
    image_rows,
    text_rows,
    scores,
    row_top,
    row_sum,
    col_top,
    col_sum,
    row_stats,
    col_stats,
    row_lse,
    col_lse,
    row_wide,
    col_wide,
    w_own,
    w_other,
    w_got,
    image_part,
    text_part,
    image_send,
    text_send,
    image_got,
    text_got,
    image_loss,
    image_loss_ring,
    text_loss,
    text_loss_ring,
    gather_send,
    gather_recv,
    fwd_send,
    fwd_recv,
    row_ssem,
    row_rsem,
    col_ssem,
    col_rsem,
    loss_ssem,
    loss_rsem,
    w_ssem,
    w_rsem,
    red_ssem,
    red_rsem,
    load_sem,
):
    block, width = image_ref.shape
    half = block // 2
    pair = 2 * block
    scale = width ** (-0.5)
    inner, outer = lax.axis_index("inner"), lax.axis_index("outer")
    groups = (Group(0), Group(1))
    sibling = {"outer": groups[1].index(0, 0, 1)}
    rows = (image_rows, text_rows)

    def remote(src, dst, ssem, rsem, device):
        return pltpu.make_async_remote_copy(
            src_ref=src,
            dst_ref=dst,
            send_sem=ssem,
            recv_sem=rsem,
            device_id=device,
            device_id_type=MESH,
        )

    RIGHT, LEFT, FAR, PARTNER = (0, 1), (0, 3), (0, 2), (1, 0)
    neighbours = [g.device(*o) for g in groups for o in (RIGHT, LEFT, PARTNER)] + [sibling]

    loads = [
        pltpu.make_async_copy(ref, rows[kind].at[0, pl.ds(0, block), :], load_sem.at[kind])
        for kind, ref in ((0, image_ref), (1, text_ref))
    ]
    for c in loads:
        c.start()
    barrier = pltpu.get_barrier_semaphore()
    for device in neighbours:
        pl.semaphore_signal(barrier, inc=1, device_id=device, device_id_type=MESH)

    row_top[...] = jnp.full(row_top.shape, -1e30, F32)
    row_sum[...] = jnp.zeros(row_sum.shape, F32)
    col_top[...] = jnp.full(col_top.shape, -1e30, F32)
    col_sum[...] = jnp.zeros(col_sum.shape, F32)
    for c in loads:
        c.wait()
    pl.semaphore_wait(barrier, len(neighbours))

    away = sorted(OFFSETS[1:], key=lambda o: -(o[0] + min(o[1], RING - o[1])))
    inner_peers = [groups[0].device(*o) for o in away]
    outer_peers = [groups[1].device(*o, c) for o in away for c in (1, 0)] + [sibling]

    def at(kind, core_step, slot, part=None):
        start, size = PLACE[slot] * block, block
        if part is not None:
            start, size = start + part * half, half
        return rows[kind].at[core_step, pl.ds(start, size), :]

    def copy(kind, src, slot, part, offset):
        n = 2 * (slot - 1) + part
        return remote(
            src,
            at(kind, 0, slot, part),
            gather_send.at[kind],
            gather_recv.at[kind, n],
            groups[kind].device(*offset),
        )

    def gather_copies(kind):
        out = {
            (3, 0): copy(kind, at(kind, 0, 2, 0), 3, 0, RIGHT),
            (3, 1): copy(kind, at(kind, 0, 1, 1), 3, 1, LEFT),
            (6, 0): copy(kind, at(kind, 0, 4, 0), 6, 0, RIGHT),
            (5, 0): copy(kind, at(kind, 0, 4, 0), 5, 0, LEFT),
            (7, 0): copy(kind, at(kind, 0, 6, 0), 7, 0, RIGHT),
            (5, 1): copy(kind, at(kind, 0, 1, 1), 5, 1, PARTNER),
            (6, 1): copy(kind, at(kind, 0, 2, 1), 6, 1, PARTNER),
            (7, 1): copy(kind, at(kind, 0, 3, 1), 7, 1, PARTNER),
        }
        for h in (0, 1):
            mine = at(kind, 0, 0, h)
            for slot, offset in ((2, RIGHT), (1, LEFT), (4, PARTNER)):
                out[slot, h] = copy(kind, mine, slot, h, offset)
        return out

    PARCELS = ((0, 2), (2, 2), (4, 2), (6, 1), (7, 1))

    def fwd(kind, n):
        first, count = PARCELS[n]
        here = pl.ds(first * block, count * block)
        return remote(
            rows[kind].at[0, here, :],
            rows[kind].at[1, here, :],
            fwd_send.at[kind],
            fwd_recv.at[kind, n],
            sibling,
        )

    copies = [gather_copies(kind) for kind in (0, 1)]
    fwds = [[fwd(kind, n) for n in range(len(PARCELS))] for kind in (0, 1)]

    def start(*keys):
        for key in keys:
            for kind in (0, 1):
                copies[kind][key].start()

    def arrived(*keys):
        for key in keys:
            for kind in (0, 1):
                copies[kind][key].wait_recv()

    def forward(*parcels):
        for n in parcels:
            for kind in (0, 1):
                fwds[kind][n].start()

    start((4, 0), (2, 1), (1, 1), (4, 1), (2, 0), (1, 0))

    mine = pl.ds(0, block)
    product = image_rows[0, mine, :].astype(F32) * text_rows[0, mine, :].astype(F32)
    positive = scale * jnp.sum(product, 0, keepdims=True)
    positive = add_up(positive[:, i : i + 128] for i in range(0, width, 128))

    def multiply(a, b, c):
        image = image_rows[0, pl.ds(a * pair, pair), :]
        text = text_rows[c, pl.ds(b * pair, pair), :]
        scores[a, b, :, pl.ds(c * pair, pair)] = (scale * LOG2E) * lax.dot_general(
            image, text, (((1,), (1,)), ((), ())), preferred_element_type=F32
        )

    def count(a, b, c):
        step = 32
        k = pl.ds((2 * b + c) * pair, pair)
        old = col_top[:, k]
        top = old
        for r in range(0, pair, step):
            value = scores[a, b, pl.ds(r, step), pl.ds(c * pair, pair)]
            top = jnp.maximum(top, jnp.max(value.reshape(step // 8, 8, pair), 0))
        total = col_sum[:, k] * jnp.exp2(old - top)
        for r in range(0, pair, step):
            value = scores[a, b, pl.ds(r, step), pl.ds(c * pair, pair)]
            here = pl.ds(a * pair + r, step)
            lanes = [value[:, i : i + 128] for i in range(0, pair, 128)]
            before = row_top[here, :]
            row = functools.reduce(jnp.maximum, lanes, before)
            row_sum[here, :] = row_sum[here, :] * jnp.exp2(before - row) + add_up(
                [jnp.exp2(lane - row) for lane in lanes]
            )
            row_top[here, :] = row
            value = value.reshape(step // 8, 8, pair)
            total = total + jnp.sum(jnp.exp2(value - top[None]), 0)
        col_top[:, k] = top
        col_sum[:, k] = total

    waiting = []

    def tiles(todo):
        for tile in todo:
            multiply(*tile)
            if waiting:
                count(*waiting.pop())
            waiting.append(tile)

    def shell(n, *parcels):
        tiles([(n, b, c) for b in range(n) for c in (0, 1)])
        tiles([(a, n, 0) for a in range(n + 1)])
        sib_arrived(*parcels)
        tiles([(a, n, 1) for a in range(n + 1)])

    def sib_arrived(*parcels):
        for n in parcels:
            for kind in (0, 1):
                fwds[kind][n].wait_recv()

    arrived((1, 1))
    start((3, 1), (5, 1))
    arrived((4, 0))
    start((6, 0), (5, 0))
    arrived((2, 1))
    start((6, 1))
    arrived((2, 0))
    start((3, 0))
    arrived((1, 0))
    arrived((4, 1))
    forward(0, 1)
    arrived((3, 1))
    start((7, 1))
    arrived((6, 0))
    start((7, 0))
    shell(0, 0)
    shell(1, 1)
    arrived((3, 0), (5, 0), (5, 1))
    forward(2)
    arrived((6, 1))
    forward(3)
    shell(2, 2)
    arrived((7, 0), (7, 1))
    forward(4)
    shell(3, 3, 4)
    count(*waiting.pop())

    def lse(top, total):
        most = jnp.max(top, 0, keepdims=True)
        total = jnp.sum(total * jnp.exp2(top - most), 0, keepdims=True)
        return most + LOG2E * jnp.log(total)

    for slot, offset in enumerate(OFFSETS):
        place = PLACE[slot]
        for c in (0, 1):
            o = groups[1].index(*offset, c)
            k = pl.ds((place // 2) * 2 * pair + c * pair + (place % 2) * block, block)
            col_stats[outer, pl.ds(o, 1), :] = lse(col_top[:, k], col_sum[:, k])
    for slot, offset in enumerate(OFFSETS):
        i = groups[0].index(*offset)
        r = pl.ds(PLACE[slot] * block, block)
        row_stats[inner, pl.ds(i, 1), :] = lse(
            jnp.transpose(row_top[r, :]), jnp.transpose(row_sum[r, :])
        )
    row_stats[inner, pl.ds(SLOTS, 8), :] = jnp.concatenate(
        [positive, jnp.zeros((7, 128), F32)], 0
    )

    def spread(ref, me, ssem, rsem, peers):
        for device in peers:
            remote(ref.at[me], ref.at[me], ssem, rsem, device).start()
        every = ref.at[pl.ds(0, len(peers))]
        return remote(every, every, ssem, rsem, sibling)

    col_out = spread(col_stats, outer, col_ssem.at[0], col_rsem.at[0], outer_peers)
    row_out = spread(row_stats, inner, row_ssem.at[0], row_rsem.at[0], inner_peers)
    row_out.wait_recv()
    col_out.wait_recv()

    def combine(ref, count):
        values = [ref[n, 0:count, :] for n in range(count)]
        top = functools.reduce(jnp.maximum, values)
        return top + LOG2E * jnp.log(add_up([jnp.exp2(value - top) for value in values]))

    row_value = combine(row_stats, SLOTS)
    col_value = combine(col_stats, 2 * SLOTS)
    row_lse[...] = row_value
    col_lse[...] = col_value
    for slot, offset in enumerate(OFFSETS):
        i = groups[0].index(*offset)
        line = row_lse[pl.ds(i, 1), :]
        place = PLACE[slot]
        row_wide[pl.ds(place * block, block), :] = jnp.transpose(
            jnp.broadcast_to(line, (block, block))
        )
        for c in (0, 1):
            o = groups[1].index(*offset, c)
            k = pl.ds((place // 2) * 2 * pair + c * pair + (place % 2) * block, block)
            col_wide[:, k] = col_lse[pl.ds(o, 1), :]

    def weigh(a, b):
        step = 32
        for r in range(0, pair, step):
            here = pl.ds(a * pair + r, step)
            line = jnp.concatenate([row_wide[here, :]] * 2, 1)
            for c, out in ((0, w_own), (1, w_other)):
                value = scores[a, b, pl.ds(r, step), pl.ds(c * pair, pair)]
                there = pl.ds((2 * b + c) * pair, pair)
                weight = jnp.exp2(value - line) + jnp.exp2(value - col_wide[:, there])
                out[b, here, :] = weight.astype(BF16)

    def w_copy(n, b, r):
        return remote(w_other.at[b, r, :], w_got.at[b, r, :], w_ssem.at[n], w_rsem.at[n], sibling)

    w_copies = [[w_copy(b, b, pl.ds(0, 4 * pair))] for b in range(3)]
    w_copies.append([w_copy(3 + a, 3, pl.ds(a * pair, pair)) for a in range(4)])

    weighed = set()

    def weigh_jobs(g):
        todo = [t for t in [(a, g) for a in range(4)] + [(g, b) for b in range(4)] if t not in weighed]
        todo = sorted(set(todo), key=todo.index)
        weighed.update(todo)
        return [functools.partial(weigh, *t) for t in todo]

    paired = add_up([row_stats[n, pl.ds(SLOTS, 8), :] for n in range(SLOTS)])
    shares = (
        row_value * (1.0 / LOG2E) - 2.0 * paired,
        (col_value[0:8] + col_value[8:16]) * (1.0 / LOG2E),
    )
    high, low, core = groups[0].highs[0], groups[0].lows[0], groups[0].cores[0]
    who = (2 * lax.rem(high + low, 2) + core, high)
    others = (
        [groups[1].device(1, 0, 1), groups[1].device(*PARTNER), sibling],
        [groups[0].device(*PARTNER)],
    )
    losses = ((image_loss, image_loss_ring), (text_loss, text_loss_ring))

    def loss_near(kind):
        losses[kind][0][who[kind]] = shares[kind]
        return spread(
            losses[kind][0], who[kind], loss_ssem.at[kind, 0], loss_rsem.at[kind, 0], others[kind]
        )

    def loss_ring(kind, near):
        group = groups[1 - kind]
        near.wait_recv()
        ref = losses[kind][0]
        losses[kind][1][group.place] = add_up([ref[n] for n in range(ref.shape[0])])
        return spread(
            losses[kind][1],
            group.place,
            loss_ssem.at[kind, 1],
            loss_rsem.at[kind, 1],
            [group.device(0, n) for n in (2, 1, 3)],
        )

    def loss_sum(kind, ring):
        ring.wait_recv()
        return add_up([losses[kind][1][n] for n in range(RING)])

    parts = (image_part, text_part)
    sends = (image_send, text_send)
    gots = (image_got, text_got)

    def lines(slot, h):
        return pl.ds(PLACE[slot] * block + h * half, half)

    def red_copies(kind):
        way = {(7, 0): RIGHT, (5, 0): RIGHT, (6, 0): LEFT, (3, 0): RIGHT, (3, 1): LEFT}
        way.update({(1, h): RIGHT for h in (0, 1)})
        way.update({(2, h): LEFT for h in (0, 1)})
        way.update({(slot, 1): PARTNER for slot in (4, 5, 6, 7)})
        way[4, 0] = PARTNER
        return {
            key: remote(
                sends[kind].at[lines(*key), :],
                gots[kind].at[n],
                red_ssem.at[kind],
                red_rsem.at[kind, n],
                groups[kind].device(*way[key]),
            )
            for n, key in enumerate(sorted(way))
        }

    reds = [red_copies(kind) for kind in (0, 1)]
    numbers = {key: n for n, key in enumerate(sorted(reds[0]))}

    def total_of(kind, slot, h, *keys):
        value = parts[kind][lines(slot, h), :]
        for key in keys:
            reds[kind][key].wait_recv()
            value = value + gots[kind][numbers[key]].astype(F32)
        return value

    READY = {(7, 0), (7, 1), (6, 0), (6, 1), (3, 0), (5, 1), (2, 0), (4, 1)}

    def pass_on(kind, slot, h, *keys):
        if (slot, h) not in READY:
            sends[kind][lines(slot, h), :] = total_of(kind, slot, h, *keys).astype(BF16)
        reds[kind][slot, h].start()

    def product(kind, g, jobs=()):
        chunks = width // pair
        for n in range(chunks):
            k = pl.ds(n * pair, pair)
            if kind == 0:
                value = add_up(
                    [
                        jnp.dot(
                            jnp.concatenate([w[b, pl.ds(g * pair, pair), :] for b in range(4)], 1),
                            text_rows[c, :, k],
                            preferred_element_type=F32,
                        )
                        for c, w in ((0, w_own), (1, w_other))
                    ]
                )
            else:
                value = add_up(
                    [
                        lax.dot_general(
                            w[g],
                            image_rows[c, :, k],
                            (((0,), (0,)), ((), ())),
                            preferred_element_type=F32,
                        )
                        for c, w in ((0, w_own), (1, w_got))
                    ]
                )
            for job in jobs[n::chunks]:
                job()
            for i in range(4):
                slot, h = PLACE.index(2 * g + i // 2), i % 2
                piece = value[i * half : (i + 1) * half]
                if (slot, h) in READY:
                    sends[kind][lines(slot, h), k] = piece.astype(BF16)
                else:
                    parts[kind][lines(slot, h), k] = piece

    def image(g, beside=None):
        product(0, g, weigh_jobs(beside) if beside is not None else ())
        if beside is not None:
            for c in w_copies[beside]:
                c.start()

    def text(g, beside=None):
        for c in w_copies[g]:
            c.wait_recv()
        product(1, g, weigh_jobs(beside) if beside is not None else ())
        if beside is not None:
            for c in w_copies[beside]:
                c.start()

    for n, job in enumerate(weigh_jobs(3)):
        job()
        if n < 4:
            w_copies[3][n].start()
    product(0, 3, weigh_jobs(2))
    pass_on(0, 7, 1)
    pass_on(0, 7, 0)
    w_copies[2][0].start()
    near_copies = [loss_near(kind) for kind in (0, 1)]
    pass_on(0, 6, 1)
    text(3, 1)
    pass_on(1, 7, 1)
    pass_on(1, 7, 0)
    pass_on(0, 6, 0)
    image(2, 0)
    pass_on(1, 6, 1)
    pass_on(0, 3, 0)
    ring_copies = [loss_ring(0, near_copies[0])]
    text(2)
    pass_on(1, 3, 0)
    pass_on(1, 5, 1)
    pass_on(1, 6, 0)
    pass_on(0, 5, 1)
    ring_copies.append(loss_ring(1, near_copies[1]))
    image(1)
    pass_on(0, 3, 1, (7, 1))
    pass_on(0, 5, 0, (7, 0))
    text(1)
    pass_on(1, 5, 0, (7, 0))
    pass_on(1, 3, 1, (7, 1))
    image(0)
    pass_on(0, 4, 1)
    pass_on(0, 2, 0)
    pass_on(0, 1, 0, (3, 0))
    text(0)
    pass_on(1, 4, 1)
    pass_on(1, 2, 0)
    pass_on(1, 1, 0, (3, 0))
    pass_on(0, 2, 1, (6, 1), (3, 1))
    pass_on(1, 1, 1, (5, 1))
    pass_on(0, 4, 0, (5, 0), (6, 0))
    pass_on(0, 1, 1, (5, 1))
    pass_on(1, 4, 0, (5, 0), (6, 0))
    pass_on(1, 2, 1, (6, 1), (3, 1))
    loss = loss_sum(0, ring_copies[0]) + loss_sum(1, ring_copies[1])
    loss = jnp.sum(jnp.sum(loss, 0, keepdims=True), 1, keepdims=True)
    total_rows = block * 2 * SLOTS * SLOTS
    loss_ref[...] = jnp.broadcast_to(loss / (2.0 * total_rows), loss_ref.shape)

    for h, keys in ((0, ((1, 0), (2, 0), (4, 0))), (1, ((4, 1), (1, 1), (2, 1)))):
        r = pl.ds(h * half, half)
        for kind, out in ((0, image_out), (1, text_out)):
            out[r, :] = total_of(kind, 0, h, *keys)

    for kind in (0, 1):
        sent = rows[kind].at[0, pl.ds(0, 14 * half), :]
        remote(sent, sent, gather_send.at[kind], gather_recv.at[kind, 0], sibling).wait_send()
        sent = rows[kind].at[0]
        remote(sent, sent, fwd_send.at[kind], fwd_recv.at[kind, 0], sibling).wait_send()
        sent = sends[kind].at[pl.ds(0, 14 * half), :]
        remote(sent, sent, red_ssem.at[kind], red_rsem.at[kind, 0], sibling).wait_send()
    for c in sum(w_copies, []) + near_copies + ring_copies + [row_out, col_out]:
        c.wait_send()


def finish(image_ref, text_ref, loss_ref, image_sum, text_sum, loss_out, image_out, text_out):
    half_scale = 0.5 * image_ref.shape[1] ** (-0.5)
    image_out[...] = half_scale * (image_sum[...] - 2.0 * text_ref[...].astype(F32))
    text_out[...] = half_scale * (text_sum[...] - 2.0 * image_ref[...].astype(F32))
    loss_out[0, 0] = loss_ref[0, 0]


def on_device(image_embed, text_embed):
    block, width = image_embed.shape
    group = SLOTS * block
    dma = pltpu.SemaphoreType.DMA
    shape = jax.ShapeDtypeStruct
    vmem = pl.BlockSpec(memory_space=pltpu.VMEM)
    loss, image_sum, text_sum = pl.pallas_call(
        kernel,
        out_shape=(
            shape((8, 128), F32),
            shape((block, width), F32),
            shape((block, width), F32),
        ),
        in_specs=[pl.BlockSpec(memory_space=pltpu.HBM)] * 2,
        out_specs=(vmem, vmem, vmem),
        scratch_shapes=[
            pltpu.VMEM((2, group, width), BF16),
            pltpu.VMEM((2, group, width), BF16),
            pltpu.VMEM((4, 4, 2 * block, 4 * block), F32),
            pltpu.VMEM((group, 128), F32),
            pltpu.VMEM((group, 128), F32),
            pltpu.VMEM((8, 2 * group), F32),
            pltpu.VMEM((8, 2 * group), F32),
            pltpu.VMEM((SLOTS, 2 * SLOTS, 128), F32),
            pltpu.VMEM((2 * SLOTS, 2 * SLOTS, 128), F32),
            pltpu.VMEM((SLOTS, 128), F32),
            pltpu.VMEM((2 * SLOTS, 128), F32),
            pltpu.VMEM((group, 128), F32),
            pltpu.VMEM((1, 2 * group), F32),
            pltpu.VMEM((4, group, 2 * block), BF16),
            pltpu.VMEM((4, group, 2 * block), BF16),
            pltpu.VMEM((4, group, 2 * block), BF16),
            pltpu.VMEM((group, width), F32),
            pltpu.VMEM((group, width), F32),
            pltpu.VMEM((group, width), BF16),
            pltpu.VMEM((group, width), BF16),
            pltpu.VMEM((14, block // 2, width), BF16),
            pltpu.VMEM((14, block // 2, width), BF16),
            pltpu.VMEM((4, 8, 128), F32),
            pltpu.VMEM((RING, 8, 128), F32),
            pltpu.VMEM((2, 8, 128), F32),
            pltpu.VMEM((RING, 8, 128), F32),
            dma((2,)),
            dma((2, 14)),
            dma((2,)),
            dma((2, 5)),
            dma((1,)),
            dma((1,)),
            dma((1,)),
            dma((1,)),
            dma((2, 2)),
            dma((2, 2)),
            dma((7,)),
            dma((7,)),
            dma((2,)),
            dma((2, 14)),
            dma((2,)),
        ],
        compiler_params=pltpu.CompilerParams(
            collective_id=0, has_side_effects=True, vmem_limit_bytes=56 * 2**20
        ),
    )(image_embed, text_embed)
    loss, image_grad, text_grad = pl.pallas_call(
        finish,
        out_shape=(
            shape((1, 1), F32),
            shape((block, width), F32),
            shape((block, width), F32),
        ),
        in_specs=[vmem] * 5,
        out_specs=(pl.BlockSpec(memory_space=pltpu.SMEM), vmem, vmem),
    )(image_embed, text_embed, loss, image_sum, text_sum)
    return loss.reshape(()), image_grad, text_grad


def solution(mesh):
    return jax.shard_map(
        on_device,
        mesh=mesh,
        in_specs=(P(("inner", "outer"), None), P(("inner", "outer"), None)),
        out_specs=(P(), P(("inner", "outer"), None), P(("inner", "outer"), None)),
        check_vma=False,
    )
```

```python
import functools
import math

import jax
import jax.numpy as jnp
from jax import lax
from jax.experimental import pallas as pl
from jax.experimental.pallas import tpu as pltpu
from jax.sharding import PartitionSpec as P

F32, BF16 = jnp.float32, jnp.bfloat16
MESH = pl.DeviceIdType.MESH
OFFSETS = ((0, 0), (0, 1), (0, 3), (0, 2), (1, 0), (1, 1), (1, 3), (1, 2))
PLACE = (0, 2, 3, 4, 1, 5, 6, 7)
RING = 4
SLOTS = 8
LOG2E = math.log2(math.e)


def add_up(values):
    return functools.reduce(jnp.add, values)


class Group:
    def __init__(self, kind):
        inner, outer = lax.axis_index("inner"), lax.axis_index("outer")
        core, chip = lax.rem(outer, 2), outer // 2
        high, x = inner // RING, lax.rem(inner, RING)
        low, y = chip // RING, lax.rem(chip, RING)
        self.kind, self.y = kind, y
        self.place = y if kind else x
        self.cores, self.lows, self.highs = (core, 1 - core), (low, 1 - low), (high, 1 - high)
        self.places = [self.place] + [lax.rem(self.place + n, RING) for n in range(1, RING)]

    def index(self, plane_step, ring_step, core_step=0):
        if self.kind == 0:
            return self.highs[plane_step] * RING + self.places[ring_step]
        chip = self.lows[plane_step] * RING + self.places[ring_step]
        return chip * 2 + self.cores[core_step]

    def device(self, plane_step, ring_step, core_step=0):
        index = self.index(plane_step, ring_step, core_step)
        if self.kind:
            return {"outer": index}
        chip = self.lows[plane_step] * RING + self.y
        return {"inner": index, "outer": chip * 2 + self.cores[0]}


def kernel(
    image_ref,
    text_ref,
    loss_ref,
    image_out,
    text_out,
    image_rows,
    text_rows,
    scores,
    row_top,
    row_sum,
    col_top,
    col_sum,
    row_stats,
    col_stats,
    row_lse,
    col_lse,
    row_wide,
    col_wide,
    w_own,
    w_other,
    w_got,
    image_part,
    text_part,
    image_send,
    text_send,
    image_got,
    text_got,
    image_loss,
    image_loss_ring,
    text_loss,
    text_loss_ring,
    gather_send,
    gather_recv,
    fwd_send,
    fwd_recv,
    row_ssem,
    row_rsem,
    col_ssem,
    col_rsem,
    loss_ssem,
    loss_rsem,
    w_ssem,
    w_rsem,
    red_ssem,
    red_rsem,
    load_sem,
):
    block, width = image_ref.shape
    half = block // 2
    pair = 2 * block
    scale = width ** (-0.5)
    inner, outer = lax.axis_index("inner"), lax.axis_index("outer")
    groups = (Group(0), Group(1))
    sibling = {"outer": groups[1].index(0, 0, 1)}
    rows = (image_rows, text_rows)

    def remote(src, dst, ssem, rsem, device):
        return pltpu.make_async_remote_copy(
            src_ref=src,
            dst_ref=dst,
            send_sem=ssem,
            recv_sem=rsem,
            device_id=device,
            device_id_type=MESH,
        )

    RIGHT, LEFT, FAR, PARTNER = (0, 1), (0, 3), (0, 2), (1, 0)
    neighbours = [g.device(*o) for g in groups for o in (RIGHT, LEFT, PARTNER)] + [sibling]

    loads = [
        pltpu.make_async_copy(ref, rows[kind].at[0, pl.ds(0, block), :], load_sem.at[kind])
        for kind, ref in ((0, image_ref), (1, text_ref))
    ]
    for c in loads:
        c.start()
    barrier = pltpu.get_barrier_semaphore()
    for device in neighbours:
        pl.semaphore_signal(barrier, inc=1, device_id=device, device_id_type=MESH)

    row_top[...] = jnp.full(row_top.shape, -1e30, F32)
    row_sum[...] = jnp.zeros(row_sum.shape, F32)
    col_top[...] = jnp.full(col_top.shape, -1e30, F32)
    col_sum[...] = jnp.zeros(col_sum.shape, F32)
    for c in loads:
        c.wait()
    pl.semaphore_wait(barrier, len(neighbours))

    def hops(offset):
        return offset[0] + min(offset[1], RING - offset[1])

    away = sorted(OFFSETS[1:], key=hops, reverse=True)

    def at(kind, slot, part, piece):
        start, size = PLACE[slot] * block + part * half, half
        if piece is not None:
            start, size = start + piece * (half // 2), half // 2
        return rows[kind].at[0, pl.ds(start, size), :]

    def gather_copies(kind):
        way = {
            (3, 0): (2, RIGHT),
            (5, 0): (4, LEFT),
            (5, 1): (1, PARTNER),
            (6, 1): (2, PARTNER),
        }
        for h in (0, 1):
            way.update({(2, h): (0, RIGHT), (1, h): (0, LEFT), (4, h): (0, PARTNER)})
            way.update(
                {
                    (3, 1, h): (1, LEFT),
                    (6, 0, h): (4, RIGHT),
                    (7, 0, h): (6, RIGHT),
                    (7, 1, h): (3, PARTNER),
                }
            )
        out = {}
        for n, (key, (source, offset)) in enumerate(sorted(way.items())):
            slot, part, piece = key if len(key) == 3 else key + (None,)
            out[key] = remote(
                at(kind, source, part, piece),
                at(kind, slot, part, piece),
                gather_send.at[kind],
                gather_recv.at[kind, n],
                groups[kind].device(*offset),
            )
        return out

    PARCELS = ((0, 2), (2, 2), (4, 2), (6, 1), (7, 1))

    def fwd(kind, n):
        first, count = PARCELS[n]
        here = pl.ds(first * block, count * block)
        return remote(
            rows[kind].at[0, here, :],
            rows[kind].at[1, here, :],
            fwd_send.at[kind],
            fwd_recv.at[kind, n],
            sibling,
        )

    copies = [gather_copies(kind) for kind in (0, 1)]
    fwds = [[fwd(kind, n) for n in range(len(PARCELS))] for kind in (0, 1)]

    def start(*keys):
        for key in keys:
            for kind in (0, 1):
                copies[kind][key].start()

    def arrived(*keys):
        for key in keys:
            for kind in (0, 1):
                copies[kind][key].wait_recv()

    def forward(*parcels):
        for n in parcels:
            for kind in (1, 0):
                fwds[kind][n].start()

    start((1, 1), (4, 0), (2, 1), (4, 1), (2, 0), (1, 0))

    mine = pl.ds(0, block)
    product = image_rows[0, mine, :].astype(F32) * text_rows[0, mine, :].astype(F32)
    positive = scale * jnp.sum(product, 0, keepdims=True)
    positive = add_up(positive[:, i : i + 128] for i in range(0, width, 128))

    def multiply(a, b, c):
        image = image_rows[0, pl.ds(a * pair, pair), :]
        text = text_rows[c, pl.ds(b * pair, pair), :]
        scores[a, b, :, pl.ds(c * pair, pair)] = (scale * LOG2E) * lax.dot_general(
            image, text, (((1,), (1,)), ((), ())), preferred_element_type=F32
        )

    def count(a, b, c):
        step = 32
        k = pl.ds((2 * b + c) * pair, pair)
        old = col_top[:, k]
        top = old
        for r in range(0, pair, step):
            value = scores[a, b, pl.ds(r, step), pl.ds(c * pair, pair)]
            top = jnp.maximum(top, jnp.max(value.reshape(step // 8, 8, pair), 0))
        total = col_sum[:, k] * jnp.exp2(old - top)
        for r in range(0, pair, step):
            value = scores[a, b, pl.ds(r, step), pl.ds(c * pair, pair)]
            here = pl.ds(a * pair + r, step)
            lanes = [value[:, i : i + 128] for i in range(0, pair, 128)]
            before = row_top[here, :]
            row = functools.reduce(jnp.maximum, lanes, before)
            row_sum[here, :] = row_sum[here, :] * jnp.exp2(before - row) + add_up(
                [jnp.exp2(lane - row) for lane in lanes]
            )
            row_top[here, :] = row
            value = value.reshape(step // 8, 8, pair)
            total = total + jnp.sum(jnp.exp2(value - top[None]), 0)
        col_top[:, k] = top
        col_sum[:, k] = total

    waiting = []

    def tiles(todo):
        for tile in todo:
            multiply(*tile)
            if waiting:
                count(*waiting.pop())
            waiting.append(tile)

    def shell(n, *parcels):
        tiles([(n, b, c) for b in range(n) for c in (0, 1)])
        tiles([(a, n, 0) for a in range(n + 1)])
        sib_arrived(*parcels)
        tiles([(a, n, 1) for a in range(n + 1)])

    def sib_arrived(*parcels):
        for n in parcels:
            fwds[1][n].wait_recv()

    arrived((1, 1))
    start((3, 1, 0), (3, 1, 1), (5, 1))
    arrived((4, 0))
    start((6, 0, 0), (6, 0, 1), (5, 0))
    arrived((2, 1))
    start((6, 1))
    arrived((2, 0))
    start((3, 0))
    arrived((1, 0), (4, 1))
    forward(0, 1)
    for n in (0, 1):
        arrived((3, 1, n))
        start((7, 1, n))
        arrived((6, 0, n))
        start((7, 0, n))
    shell(0, 0)
    shell(1, 1)
    arrived((3, 0), (5, 0), (5, 1))
    forward(2)
    arrived((6, 1))
    forward(3)
    shell(2, 2)
    for kind in (1, 0):
        for key in ((7, 1, 0), (7, 0, 0), (7, 1, 1), (7, 0, 1)):
            copies[kind][key].wait_recv()
        fwds[kind][4].start()
    shell(3, 3, 4)
    count(*waiting.pop())

    def lse(top, total):
        most = jnp.max(top, 0, keepdims=True)
        total = jnp.sum(total * jnp.exp2(top - most), 0, keepdims=True)
        return most + LOG2E * jnp.log(total)

    for slot, offset in enumerate(OFFSETS):
        place = PLACE[slot]
        for c in (0, 1):
            o = groups[1].index(*offset, c)
            k = pl.ds((place // 2) * 2 * pair + c * pair + (place % 2) * block, block)
            col_stats[outer, pl.ds(o, 1), :] = lse(col_top[:, k], col_sum[:, k])
    for slot, offset in enumerate(OFFSETS):
        i = groups[0].index(*offset)
        r = pl.ds(PLACE[slot] * block, block)
        row_stats[inner, pl.ds(i, 1), :] = lse(
            jnp.transpose(row_top[r, :]), jnp.transpose(row_sum[r, :])
        )
    row_stats[inner, pl.ds(SLOTS, 8), :] = jnp.concatenate(
        [positive, jnp.zeros((7, 128), F32)], 0
    )

    def spread(ref, me, ssem, rsem, peers):
        for device in peers:
            remote(ref.at[me], ref.at[me], ssem, rsem, device).start()
        return every(ref, ssem, rsem, len(peers))

    def every(ref, ssem, rsem, count):
        some = ref.at[pl.ds(0, count)]
        return remote(some, some, ssem, rsem, sibling)

    rows_in = (row_stats.at[inner], row_ssem.at[0], row_rsem.at[0])
    cols_in = (col_stats.at[outer], col_ssem.at[0], col_rsem.at[0])
    for offset in away:
        for (ref, ssem, rsem), device in (
            (rows_in, groups[0].device(*offset)),
            (cols_in, groups[1].device(*offset, 1)),
            (cols_in, groups[1].device(*offset, 0)),
        ):
            remote(ref, ref, ssem, rsem, device).start()
    remote(cols_in[0], cols_in[0], cols_in[1], cols_in[2], sibling).start()
    row_out = every(row_stats, row_ssem.at[0], row_rsem.at[0], SLOTS - 1)
    col_out = every(col_stats, col_ssem.at[0], col_rsem.at[0], 2 * SLOTS - 1)
    row_out.wait_recv()
    col_out.wait_recv()

    def combine(ref, count):
        values = [ref[n, 0:count, :] for n in range(count)]
        top = functools.reduce(jnp.maximum, values)
        return top + LOG2E * jnp.log(add_up([jnp.exp2(value - top) for value in values]))

    row_value = combine(row_stats, SLOTS)
    col_value = combine(col_stats, 2 * SLOTS)
    row_lse[...] = row_value
    col_lse[...] = col_value
    for slot, offset in enumerate(OFFSETS):
        i = groups[0].index(*offset)
        line = row_lse[pl.ds(i, 1), :]
        place = PLACE[slot]
        row_wide[pl.ds(place * block, block), :] = jnp.transpose(
            jnp.broadcast_to(line, (block, block))
        )
        for c in (0, 1):
            o = groups[1].index(*offset, c)
            k = pl.ds((place // 2) * 2 * pair + c * pair + (place % 2) * block, block)
            col_wide[:, k] = col_lse[pl.ds(o, 1), :]

    def weigh(a, b):
        step = 32
        for r in range(0, pair, step):
            here = pl.ds(a * pair + r, step)
            line = jnp.concatenate([row_wide[here, :]] * 2, 1)
            for c, out in ((0, w_own), (1, w_other)):
                value = scores[a, b, pl.ds(r, step), pl.ds(c * pair, pair)]
                there = pl.ds((2 * b + c) * pair, pair)
                weight = jnp.exp2(value - line) + jnp.exp2(value - col_wide[:, there])
                out[b, here, :] = weight.astype(BF16)

    def w_copy(n, b, r):
        return remote(w_other.at[b, r, :], w_got.at[b, r, :], w_ssem.at[n], w_rsem.at[n], sibling)

    w_copies = [[w_copy(b, b, pl.ds(0, 4 * pair))] for b in range(3)]
    w_copies.append([w_copy(3 + a, 3, pl.ds(a * pair, pair)) for a in range(4)])

    weighed = set()

    def weigh_jobs(g):
        todo = [t for t in [(a, g) for a in range(4)] + [(g, b) for b in range(4)] if t not in weighed]
        todo = sorted(set(todo), key=todo.index)
        weighed.update(todo)
        return [functools.partial(weigh, *t) for t in todo]

    paired = add_up([row_stats[n, pl.ds(SLOTS, 8), :] for n in range(SLOTS)])
    shares = (
        row_value * (1.0 / LOG2E) - 2.0 * paired,
        (col_value[0:8] + col_value[8:16]) * (1.0 / LOG2E),
    )
    high, low, core = groups[0].highs[0], groups[0].lows[0], groups[0].cores[0]
    who = (2 * lax.rem(high + low, 2) + core, high)
    others = (
        [groups[1].device(1, 0, 1), groups[1].device(*PARTNER), sibling],
        [groups[0].device(*PARTNER)],
    )
    losses = ((image_loss, image_loss_ring), (text_loss, text_loss_ring))

    def loss_near(kind):
        losses[kind][0][who[kind]] = shares[kind]
        return spread(
            losses[kind][0], who[kind], loss_ssem.at[kind, 0], loss_rsem.at[kind, 0], others[kind]
        )

    def loss_ring(kind, near):
        group = groups[1 - kind]
        near.wait_recv()
        ref = losses[kind][0]
        losses[kind][1][group.place] = add_up([ref[n] for n in range(ref.shape[0])])
        return spread(
            losses[kind][1],
            group.place,
            loss_ssem.at[kind, 1],
            loss_rsem.at[kind, 1],
            [group.device(0, n) for n in (2, 1, 3)],
        )

    def loss_sum(kind, ring):
        ring.wait_recv()
        return add_up([losses[kind][1][n] for n in range(RING)])

    parts = (image_part, text_part)
    sends = (image_send, text_send)
    gots = (image_got, text_got)

    def lines(slot, h):
        return pl.ds(PLACE[slot] * block + h * half, half)

    def red_copies(kind):
        way = {(7, 0): RIGHT, (5, 0): RIGHT, (6, 0): LEFT, (3, 0): RIGHT, (3, 1): LEFT}
        way.update({(1, h): RIGHT for h in (0, 1)})
        way.update({(2, h): LEFT for h in (0, 1)})
        way.update({(slot, 1): PARTNER for slot in (4, 5, 6, 7)})
        way[4, 0] = PARTNER
        return {
            key: remote(
                sends[kind].at[lines(*key), :],
                gots[kind].at[n],
                red_ssem.at[kind],
                red_rsem.at[kind, n],
                groups[kind].device(*way[key]),
            )
            for n, key in enumerate(sorted(way))
        }

    reds = [red_copies(kind) for kind in (0, 1)]
    numbers = {key: n for n, key in enumerate(sorted(reds[0]))}

    def total_of(kind, slot, h, *keys):
        value = parts[kind][lines(slot, h), :]
        for key in keys:
            reds[kind][key].wait_recv()
            value = value + gots[kind][numbers[key]].astype(F32)
        return value

    READY = {(7, 0), (7, 1), (6, 0), (6, 1), (3, 0), (5, 1), (2, 0), (4, 1)}

    def pass_on(kind, slot, h, *keys):
        if (slot, h) not in READY:
            sends[kind][lines(slot, h), :] = total_of(kind, slot, h, *keys).astype(BF16)
        reds[kind][slot, h].start()

    def product(kind, g, jobs=()):
        chunks = width // pair
        for n in range(chunks):
            k = pl.ds(n * pair, pair)
            if kind == 0:
                value = add_up(
                    [
                        jnp.dot(
                            jnp.concatenate([w[b, pl.ds(g * pair, pair), :] for b in range(4)], 1),
                            text_rows[c, :, k],
                            preferred_element_type=F32,
                        )
                        for c, w in ((0, w_own), (1, w_other))
                    ]
                )
            else:
                value = add_up(
                    [
                        lax.dot_general(
                            w[g],
                            image_rows[c, :, k],
                            (((0,), (0,)), ((), ())),
                            preferred_element_type=F32,
                        )
                        for c, w in ((0, w_own), (1, w_got))
                    ]
                )
            for job in jobs[n::chunks]:
                job()
            for i in range(4):
                slot, h = PLACE.index(2 * g + i // 2), i % 2
                piece = value[i * half : (i + 1) * half]
                if (slot, h) in READY:
                    sends[kind][lines(slot, h), k] = piece.astype(BF16)
                else:
                    parts[kind][lines(slot, h), k] = piece

    def image(g, beside=None):
        product(0, g, weigh_jobs(beside) if beside is not None else ())
        if beside is not None:
            for c in w_copies[beside]:
                c.start()

    def text(g, beside=None):
        for c in w_copies[g]:
            c.wait_recv()
        product(1, g, weigh_jobs(beside) if beside is not None else ())
        if beside is not None:
            for c in w_copies[beside]:
                c.start()

    for n, job in enumerate(weigh_jobs(3)):
        job()
        if n < 4:
            w_copies[3][n].start()
    product(0, 3, weigh_jobs(2))
    pass_on(0, 7, 1)
    pass_on(0, 7, 0)
    w_copies[2][0].start()
    near_copies = [loss_near(kind) for kind in (0, 1)]
    pass_on(0, 6, 1)
    for c in fwds[0]:
        c.wait_recv()
    text(3, 1)
    pass_on(1, 7, 1)
    pass_on(1, 7, 0)
    pass_on(0, 6, 0)
    image(2, 0)
    pass_on(1, 6, 1)
    pass_on(0, 3, 0)
    ring_copies = [loss_ring(0, near_copies[0])]
    text(2)
    pass_on(1, 3, 0)
    pass_on(1, 5, 1)
    pass_on(1, 6, 0)
    pass_on(0, 5, 1)
    ring_copies.append(loss_ring(1, near_copies[1]))
    image(1)
    pass_on(0, 3, 1, (7, 1))
    pass_on(0, 5, 0, (7, 0))
    text(1)
    pass_on(1, 5, 0, (7, 0))
    pass_on(1, 3, 1, (7, 1))
    image(0)
    pass_on(0, 4, 1)
    pass_on(0, 2, 0)
    pass_on(0, 1, 0, (3, 0))
    text(0)
    pass_on(1, 4, 1)
    pass_on(1, 2, 0)
    pass_on(1, 1, 0, (3, 0))
    pass_on(0, 2, 1, (6, 1), (3, 1))
    pass_on(1, 1, 1, (5, 1))
    pass_on(0, 4, 0, (5, 0), (6, 0))
    pass_on(0, 1, 1, (5, 1))
    pass_on(1, 4, 0, (5, 0), (6, 0))
    pass_on(1, 2, 1, (6, 1), (3, 1))
    loss = loss_sum(0, ring_copies[0]) + loss_sum(1, ring_copies[1])
    loss = jnp.sum(jnp.sum(loss, 0, keepdims=True), 1, keepdims=True)
    total_rows = block * 2 * SLOTS * SLOTS
    loss_ref[...] = jnp.broadcast_to(loss / (2.0 * total_rows), loss_ref.shape)

    for h, keys in ((0, ((1, 0), (2, 0), (4, 0))), (1, ((4, 1), (1, 1), (2, 1)))):
        r = pl.ds(h * half, half)
        for kind, out in ((0, image_out), (1, text_out)):
            out[r, :] = total_of(kind, 0, h, *keys)

    for kind in (0, 1):
        sent = rows[kind].at[0, pl.ds(0, 14 * half), :]
        remote(sent, sent, gather_send.at[kind], gather_recv.at[kind, 0], sibling).wait_send()
        sent = rows[kind].at[0]
        remote(sent, sent, fwd_send.at[kind], fwd_recv.at[kind, 0], sibling).wait_send()
        sent = sends[kind].at[pl.ds(0, 14 * half), :]
        remote(sent, sent, red_ssem.at[kind], red_rsem.at[kind, 0], sibling).wait_send()
    for c in sum(w_copies, []) + near_copies + ring_copies + [row_out, col_out]:
        c.wait_send()


def finish(image_ref, text_ref, loss_ref, image_sum, text_sum, loss_out, image_out, text_out):
    half_scale = 0.5 * image_ref.shape[1] ** (-0.5)
    image_out[...] = half_scale * (image_sum[...] - 2.0 * text_ref[...].astype(F32))
    text_out[...] = half_scale * (text_sum[...] - 2.0 * image_ref[...].astype(F32))
    loss_out[0, 0] = loss_ref[0, 0]


def on_device(image_embed, text_embed):
    block, width = image_embed.shape
    group = SLOTS * block
    dma = pltpu.SemaphoreType.DMA
    shape = jax.ShapeDtypeStruct
    vmem = pl.BlockSpec(memory_space=pltpu.VMEM)
    loss, image_sum, text_sum = pl.pallas_call(
        kernel,
        out_shape=(
            shape((8, 128), F32),
            shape((block, width), F32),
            shape((block, width), F32),
        ),
        in_specs=[pl.BlockSpec(memory_space=pltpu.HBM)] * 2,
        out_specs=(vmem, vmem, vmem),
        scratch_shapes=[
            pltpu.VMEM((2, group, width), BF16),
            pltpu.VMEM((2, group, width), BF16),
            pltpu.VMEM((4, 4, 2 * block, 4 * block), F32),
            pltpu.VMEM((group, 128), F32),
            pltpu.VMEM((group, 128), F32),
            pltpu.VMEM((8, 2 * group), F32),
            pltpu.VMEM((8, 2 * group), F32),
            pltpu.VMEM((SLOTS, 2 * SLOTS, 128), F32),
            pltpu.VMEM((2 * SLOTS, 2 * SLOTS, 128), F32),
            pltpu.VMEM((SLOTS, 128), F32),
            pltpu.VMEM((2 * SLOTS, 128), F32),
            pltpu.VMEM((group, 128), F32),
            pltpu.VMEM((1, 2 * group), F32),
            pltpu.VMEM((4, group, 2 * block), BF16),
            pltpu.VMEM((4, group, 2 * block), BF16),
            pltpu.VMEM((4, group, 2 * block), BF16),
            pltpu.VMEM((group, width), F32),
            pltpu.VMEM((group, width), F32),
            pltpu.VMEM((group, width), BF16),
            pltpu.VMEM((group, width), BF16),
            pltpu.VMEM((14, block // 2, width), BF16),
            pltpu.VMEM((14, block // 2, width), BF16),
            pltpu.VMEM((4, 8, 128), F32),
            pltpu.VMEM((RING, 8, 128), F32),
            pltpu.VMEM((2, 8, 128), F32),
            pltpu.VMEM((RING, 8, 128), F32),
            dma((2,)),
            dma((2, 18)),
            dma((2,)),
            dma((2, 5)),
            dma((1,)),
            dma((1,)),
            dma((1,)),
            dma((1,)),
            dma((2, 2)),
            dma((2, 2)),
            dma((7,)),
            dma((7,)),
            dma((2,)),
            dma((2, 14)),
            dma((2,)),
        ],
        compiler_params=pltpu.CompilerParams(
            collective_id=0, has_side_effects=True, vmem_limit_bytes=56 * 2**20
        ),
    )(image_embed, text_embed)
    loss, image_grad, text_grad = pl.pallas_call(
        finish,
        out_shape=(
            shape((1, 1), F32),
            shape((block, width), F32),
            shape((block, width), F32),
        ),
        in_specs=[vmem] * 5,
        out_specs=(pl.BlockSpec(memory_space=pltpu.SMEM), vmem, vmem),
    )(image_embed, text_embed, loss, image_sum, text_sum)
    return loss.reshape(()), image_grad, text_grad


def solution(mesh):
    return jax.shard_map(
        on_device,
        mesh=mesh,
        in_specs=(P(("inner", "outer"), None), P(("inner", "outer"), None)),
        out_specs=(P(), P(("inner", "outer"), None), P(("inner", "outer"), None)),
        check_vma=False,
    )
```

```python
import functools
import math

import jax
import jax.numpy as jnp
from jax import lax
from jax.experimental import pallas as pl
from jax.experimental.pallas import tpu as pltpu
from jax.sharding import PartitionSpec as P

F32, BF16 = jnp.float32, jnp.bfloat16
MESH = pl.DeviceIdType.MESH
OFFSETS = ((0, 0), (0, 1), (0, 3), (0, 2), (1, 0), (1, 1), (1, 3), (1, 2))
PLACE = (0, 2, 3, 4, 1, 5, 6, 7)
RING = 4
SLOTS = 8
LOG2E = math.log2(math.e)


def add_up(values):
    return functools.reduce(jnp.add, values)


class Group:
    def __init__(self, kind):
        inner, outer = lax.axis_index("inner"), lax.axis_index("outer")
        core, chip = lax.rem(outer, 2), outer // 2
        high, x = inner // RING, lax.rem(inner, RING)
        low, y = chip // RING, lax.rem(chip, RING)
        self.kind, self.y = kind, y
        self.place = y if kind else x
        self.cores, self.lows, self.highs = (core, 1 - core), (low, 1 - low), (high, 1 - high)
        self.places = [self.place] + [lax.rem(self.place + n, RING) for n in range(1, RING)]

    def index(self, plane_step, ring_step, core_step=0):
        if self.kind == 0:
            return self.highs[plane_step] * RING + self.places[ring_step]
        chip = self.lows[plane_step] * RING + self.places[ring_step]
        return chip * 2 + self.cores[core_step]

    def device(self, plane_step, ring_step, core_step=0):
        index = self.index(plane_step, ring_step, core_step)
        if self.kind:
            return {"outer": index}
        chip = self.lows[plane_step] * RING + self.y
        return {"inner": index, "outer": chip * 2 + self.cores[0]}


def kernel(
    image_ref,
    text_ref,
    loss_ref,
    image_out,
    text_out,
    image_rows,
    text_rows,
    scores,
    row_top,
    row_sum,
    col_top,
    col_sum,
    row_stats,
    col_stats,
    row_lse,
    col_lse,
    row_wide,
    col_wide,
    w_own,
    w_other,
    w_got,
    image_part,
    text_part,
    image_send,
    text_send,
    image_got,
    text_got,
    image_loss,
    image_loss_ring,
    text_loss,
    text_loss_ring,
    gather_send,
    gather_recv,
    fwd_send,
    fwd_recv,
    row_ssem,
    row_rsem,
    col_ssem,
    col_rsem,
    loss_ssem,
    loss_rsem,
    w_ssem,
    w_rsem,
    red_ssem,
    red_rsem,
    load_sem,
):
    block, width = image_ref.shape
    half = block // 2
    pair = 2 * block
    scale = width ** (-0.5)
    inner, outer = lax.axis_index("inner"), lax.axis_index("outer")
    groups = (Group(0), Group(1))
    sibling = {"outer": groups[1].index(0, 0, 1)}
    rows = (image_rows, text_rows)

    def remote(src, dst, ssem, rsem, device):
        return pltpu.make_async_remote_copy(
            src_ref=src,
            dst_ref=dst,
            send_sem=ssem,
            recv_sem=rsem,
            device_id=device,
            device_id_type=MESH,
        )

    RIGHT, LEFT, FAR, PARTNER = (0, 1), (0, 3), (0, 2), (1, 0)
    neighbours = [g.device(*o) for g in groups for o in (RIGHT, LEFT, PARTNER)] + [sibling]

    loads = [
        pltpu.make_async_copy(ref, rows[kind].at[0, pl.ds(0, block), :], load_sem.at[kind])
        for kind, ref in ((0, image_ref), (1, text_ref))
    ]
    for c in loads:
        c.start()
    barrier = pltpu.get_barrier_semaphore()
    for device in neighbours:
        pl.semaphore_signal(barrier, inc=1, device_id=device, device_id_type=MESH)

    row_top[...] = jnp.full(row_top.shape, -1e30, F32)
    row_sum[...] = jnp.zeros(row_sum.shape, F32)
    col_top[...] = jnp.full(col_top.shape, -1e30, F32)
    col_sum[...] = jnp.zeros(col_sum.shape, F32)
    for c in loads:
        c.wait()
    pl.semaphore_wait(barrier, len(neighbours))

    away = sorted(OFFSETS[1:], key=lambda o: -(o[0] + min(o[1], RING - o[1])))
    inner_peers = [groups[0].device(*o) for o in away]
    outer_peers = [groups[1].device(*o, c) for o in away for c in (1, 0)] + [sibling]

    def at(kind, core_step, slot, part=None):
        start, size = PLACE[slot] * block, block
        if part is not None:
            start, size = start + part * half, half
        return rows[kind].at[core_step, pl.ds(start, size), :]

    def copy(kind, src, slot, part, offset):
        n = 2 * (slot - 1) + part
        return remote(
            src,
            at(kind, 0, slot, part),
            gather_send.at[kind],
            gather_recv.at[kind, n],
            groups[kind].device(*offset),
        )

    def gather_copies(kind):
        out = {
            (3, 0): copy(kind, at(kind, 0, 2, 0), 3, 0, RIGHT),
            (3, 1): copy(kind, at(kind, 0, 1, 1), 3, 1, LEFT),
            (6, 0): copy(kind, at(kind, 0, 4, 0), 6, 0, RIGHT),
            (5, 0): copy(kind, at(kind, 0, 4, 0), 5, 0, LEFT),
            (7, 0): copy(kind, at(kind, 0, 6, 0), 7, 0, RIGHT),
            (5, 1): copy(kind, at(kind, 0, 1, 1), 5, 1, PARTNER),
            (6, 1): copy(kind, at(kind, 0, 2, 1), 6, 1, PARTNER),
            (7, 1): copy(kind, at(kind, 0, 3, 1), 7, 1, PARTNER),
        }
        for h in (0, 1):
            mine = at(kind, 0, 0, h)
            for slot, offset in ((2, RIGHT), (1, LEFT), (4, PARTNER)):
                out[slot, h] = copy(kind, mine, slot, h, offset)
        return out

    PARCELS = ((0, 2), (2, 2), (4, 2), (6, 1), (7, 1))

    def fwd(kind, n):
        first, count = PARCELS[n]
        here = pl.ds(first * block, count * block)
        return remote(
            rows[kind].at[0, here, :],
            rows[kind].at[1, here, :],
            fwd_send.at[kind],
            fwd_recv.at[kind, n],
            sibling,
        )

    copies = [gather_copies(kind) for kind in (0, 1)]
    fwds = [[fwd(kind, n) for n in range(len(PARCELS))] for kind in (0, 1)]

    def start(*keys):
        for key in keys:
            for kind in (0, 1):
                copies[kind][key].start()

    def arrived(*keys):
        for key in keys:
            for kind in (0, 1):
                copies[kind][key].wait_recv()

    def forward(*parcels):
        for n in parcels:
            for kind in (1, 0):
                fwds[kind][n].start()

    start((4, 0), (2, 1), (1, 1), (4, 1), (2, 0), (1, 0))

    mine = pl.ds(0, block)
    product = image_rows[0, mine, :].astype(F32) * text_rows[0, mine, :].astype(F32)
    positive = scale * jnp.sum(product, 0, keepdims=True)
    positive = add_up(positive[:, i : i + 128] for i in range(0, width, 128))

    def multiply(a, b, c):
        image = image_rows[0, pl.ds(a * pair, pair), :]
        text = text_rows[c, pl.ds(b * pair, pair), :]
        scores[a, b, :, pl.ds(c * pair, pair)] = (scale * LOG2E) * lax.dot_general(
            image, text, (((1,), (1,)), ((), ())), preferred_element_type=F32
        )

    def count(a, b, c):
        step = 32
        k = pl.ds((2 * b + c) * pair, pair)
        old = col_top[:, k]
        top = old
        for r in range(0, pair, step):
            value = scores[a, b, pl.ds(r, step), pl.ds(c * pair, pair)]
            top = jnp.maximum(top, jnp.max(value.reshape(step // 8, 8, pair), 0))
        total = col_sum[:, k] * jnp.exp2(old - top)
        for r in range(0, pair, step):
            value = scores[a, b, pl.ds(r, step), pl.ds(c * pair, pair)]
            here = pl.ds(a * pair + r, step)
            lanes = [value[:, i : i + 128] for i in range(0, pair, 128)]
            before = row_top[here, :]
            row = functools.reduce(jnp.maximum, lanes, before)
            row_sum[here, :] = row_sum[here, :] * jnp.exp2(before - row) + add_up(
                [jnp.exp2(lane - row) for lane in lanes]
            )
            row_top[here, :] = row
            value = value.reshape(step // 8, 8, pair)
            total = total + jnp.sum(jnp.exp2(value - top[None]), 0)
        col_top[:, k] = top
        col_sum[:, k] = total

    waiting = []

    def tiles(todo):
        for tile in todo:
            multiply(*tile)
            if waiting:
                count(*waiting.pop())
            waiting.append(tile)

    def shell(n, *parcels):
        tiles([(n, b, c) for b in range(n) for c in (0, 1)])
        tiles([(a, n, 0) for a in range(n + 1)])
        sib_arrived(*parcels)
        tiles([(a, n, 1) for a in range(n + 1)])

    def sib_arrived(*parcels):
        for n in parcels:
            fwds[1][n].wait_recv()

    arrived((1, 1))
    start((3, 1), (5, 1))
    arrived((4, 0))
    start((6, 0), (5, 0))
    arrived((2, 1))
    start((6, 1))
    arrived((2, 0))
    start((3, 0))
    arrived((1, 0))
    arrived((4, 1))
    forward(0, 1)
    arrived((3, 1))
    start((7, 1))
    arrived((6, 0))
    start((7, 0))
    shell(0, 0)
    shell(1, 1)
    arrived((3, 0), (5, 0), (5, 1))
    forward(2)
    arrived((6, 1))
    forward(3)
    shell(2, 2)
    for kind in (1, 0):
        for h in (1, 0):
            copies[kind][7, h].wait_recv()
        fwds[kind][4].start()
    shell(3, 3, 4)
    count(*waiting.pop())

    def lse(top, total):
        most = jnp.max(top, 0, keepdims=True)
        total = jnp.sum(total * jnp.exp2(top - most), 0, keepdims=True)
        return most + LOG2E * jnp.log(total)

    for slot, offset in enumerate(OFFSETS):
        place = PLACE[slot]
        for c in (0, 1):
            o = groups[1].index(*offset, c)
            k = pl.ds((place // 2) * 2 * pair + c * pair + (place % 2) * block, block)
            col_stats[outer, pl.ds(o, 1), :] = lse(col_top[:, k], col_sum[:, k])
    for slot, offset in enumerate(OFFSETS):
        i = groups[0].index(*offset)
        r = pl.ds(PLACE[slot] * block, block)
        row_stats[inner, pl.ds(i, 1), :] = lse(
            jnp.transpose(row_top[r, :]), jnp.transpose(row_sum[r, :])
        )
    row_stats[inner, pl.ds(SLOTS, 8), :] = jnp.concatenate(
        [positive, jnp.zeros((7, 128), F32)], 0
    )

    def spread(ref, me, ssem, rsem, peers):
        for device in peers:
            remote(ref.at[me], ref.at[me], ssem, rsem, device).start()
        every = ref.at[pl.ds(0, len(peers))]
        return remote(every, every, ssem, rsem, sibling)

    col_out = spread(col_stats, outer, col_ssem.at[0], col_rsem.at[0], outer_peers)
    row_out = spread(row_stats, inner, row_ssem.at[0], row_rsem.at[0], inner_peers)
    row_out.wait_recv()
    col_out.wait_recv()

    def combine(ref, count):
        values = [ref[n, 0:count, :] for n in range(count)]
        top = functools.reduce(jnp.maximum, values)
        return top + LOG2E * jnp.log(add_up([jnp.exp2(value - top) for value in values]))

    row_value = combine(row_stats, SLOTS)
    col_value = combine(col_stats, 2 * SLOTS)
    row_lse[...] = row_value
    col_lse[...] = col_value
    for slot, offset in enumerate(OFFSETS):
        i = groups[0].index(*offset)
        line = row_lse[pl.ds(i, 1), :]
        place = PLACE[slot]
        row_wide[pl.ds(place * block, block), :] = jnp.transpose(
            jnp.broadcast_to(line, (block, block))
        )
        for c in (0, 1):
            o = groups[1].index(*offset, c)
            k = pl.ds((place // 2) * 2 * pair + c * pair + (place % 2) * block, block)
            col_wide[:, k] = col_lse[pl.ds(o, 1), :]

    def weigh(a, b):
        step = 32
        for r in range(0, pair, step):
            here = pl.ds(a * pair + r, step)
            line = jnp.concatenate([row_wide[here, :]] * 2, 1)
            for c, out in ((0, w_own), (1, w_other)):
                value = scores[a, b, pl.ds(r, step), pl.ds(c * pair, pair)]
                there = pl.ds((2 * b + c) * pair, pair)
                weight = jnp.exp2(value - line) + jnp.exp2(value - col_wide[:, there])
                out[b, here, :] = weight.astype(BF16)

    def w_copy(n, b, r):
        return remote(w_other.at[b, r, :], w_got.at[b, r, :], w_ssem.at[n], w_rsem.at[n], sibling)

    w_copies = [[w_copy(b, b, pl.ds(0, 4 * pair))] for b in range(3)]
    w_copies.append([w_copy(3 + a, 3, pl.ds(a * pair, pair)) for a in range(4)])

    weighed = set()

    def weigh_jobs(g):
        todo = [t for t in [(a, g) for a in range(4)] + [(g, b) for b in range(4)] if t not in weighed]
        todo = sorted(set(todo), key=todo.index)
        weighed.update(todo)
        return [functools.partial(weigh, *t) for t in todo]

    paired = add_up([row_stats[n, pl.ds(SLOTS, 8), :] for n in range(SLOTS)])
    shares = (
        row_value * (1.0 / LOG2E) - 2.0 * paired,
        (col_value[0:8] + col_value[8:16]) * (1.0 / LOG2E),
    )
    high, low, core = groups[0].highs[0], groups[0].lows[0], groups[0].cores[0]
    who = (2 * lax.rem(high + low, 2) + core, high)
    others = (
        [groups[1].device(1, 0, 1), groups[1].device(*PARTNER), sibling],
        [groups[0].device(*PARTNER)],
    )
    losses = ((image_loss, image_loss_ring), (text_loss, text_loss_ring))

    def loss_near(kind):
        losses[kind][0][who[kind]] = shares[kind]
        return spread(
            losses[kind][0], who[kind], loss_ssem.at[kind, 0], loss_rsem.at[kind, 0], others[kind]
        )

    def loss_ring(kind, near):
        group = groups[1 - kind]
        near.wait_recv()
        ref = losses[kind][0]
        losses[kind][1][group.place] = add_up([ref[n] for n in range(ref.shape[0])])
        return spread(
            losses[kind][1],
            group.place,
            loss_ssem.at[kind, 1],
            loss_rsem.at[kind, 1],
            [group.device(0, n) for n in (2, 1, 3)],
        )

    def loss_sum(kind, ring):
        ring.wait_recv()
        return add_up([losses[kind][1][n] for n in range(RING)])

    parts = (image_part, text_part)
    sends = (image_send, text_send)
    gots = (image_got, text_got)

    def lines(slot, h):
        return pl.ds(PLACE[slot] * block + h * half, half)

    def red_copies(kind):
        way = {(7, 0): RIGHT, (5, 0): RIGHT, (6, 0): LEFT, (3, 0): RIGHT, (3, 1): LEFT}
        way.update({(1, h): RIGHT for h in (0, 1)})
        way.update({(2, h): LEFT for h in (0, 1)})
        way.update({(slot, 1): PARTNER for slot in (4, 5, 6, 7)})
        way[4, 0] = PARTNER
        return {
            key: remote(
                sends[kind].at[lines(*key), :],
                gots[kind].at[n],
                red_ssem.at[kind],
                red_rsem.at[kind, n],
                groups[kind].device(*way[key]),
            )
            for n, key in enumerate(sorted(way))
        }

    reds = [red_copies(kind) for kind in (0, 1)]
    numbers = {key: n for n, key in enumerate(sorted(reds[0]))}

    def total_of(kind, slot, h, *keys):
        value = parts[kind][lines(slot, h), :]
        for key in keys:
            reds[kind][key].wait_recv()
            value = value + gots[kind][numbers[key]].astype(F32)
        return value

    READY = {(7, 0), (7, 1), (6, 0), (6, 1), (3, 0), (5, 1), (2, 0), (4, 1)}

    def pass_on(kind, slot, h, *keys):
        if (slot, h) not in READY:
            sends[kind][lines(slot, h), :] = total_of(kind, slot, h, *keys).astype(BF16)
        reds[kind][slot, h].start()

    def product(kind, g, jobs=()):
        chunks = width // pair
        for n in range(chunks):
            k = pl.ds(n * pair, pair)
            if kind == 0:
                value = add_up(
                    [
                        jnp.dot(
                            jnp.concatenate([w[b, pl.ds(g * pair, pair), :] for b in range(4)], 1),
                            text_rows[c, :, k],
                            preferred_element_type=F32,
                        )
                        for c, w in ((0, w_own), (1, w_other))
                    ]
                )
            else:
                value = add_up(
                    [
                        lax.dot_general(
                            w[g],
                            image_rows[c, :, k],
                            (((0,), (0,)), ((), ())),
                            preferred_element_type=F32,
                        )
                        for c, w in ((0, w_own), (1, w_got))
                    ]
                )
            for job in jobs[n::chunks]:
                job()
            for i in range(4):
                slot, h = PLACE.index(2 * g + i // 2), i % 2
                piece = value[i * half : (i + 1) * half]
                if (slot, h) in READY:
                    sends[kind][lines(slot, h), k] = piece.astype(BF16)
                else:
                    parts[kind][lines(slot, h), k] = piece

    def image(g, beside=None):
        product(0, g, weigh_jobs(beside) if beside is not None else ())
        if beside is not None:
            for c in w_copies[beside]:
                c.start()

    def text(g, beside=None):
        for c in w_copies[g]:
            c.wait_recv()
        product(1, g, weigh_jobs(beside) if beside is not None else ())
        if beside is not None:
            for c in w_copies[beside]:
                c.start()

    for n, job in enumerate(weigh_jobs(3)):
        job()
        if n < 4:
            w_copies[3][n].start()
    product(0, 3, weigh_jobs(2))
    pass_on(0, 7, 1)
    pass_on(0, 7, 0)
    w_copies[2][0].start()
    near_copies = [loss_near(kind) for kind in (0, 1)]
    pass_on(0, 6, 1)
    for c in fwds[0]:
        c.wait_recv()
    text(3, 1)
    pass_on(1, 7, 1)
    pass_on(1, 7, 0)
    pass_on(0, 6, 0)
    image(2, 0)
    pass_on(1, 6, 1)
    pass_on(0, 3, 0)
    ring_copies = [loss_ring(0, near_copies[0])]
    text(2)
    pass_on(1, 3, 0)
    pass_on(1, 5, 1)
    pass_on(1, 6, 0)
    pass_on(0, 5, 1)
    ring_copies.append(loss_ring(1, near_copies[1]))
    image(1)
    pass_on(0, 3, 1, (7, 1))
    pass_on(0, 5, 0, (7, 0))
    text(1)
    pass_on(1, 5, 0, (7, 0))
    pass_on(1, 3, 1, (7, 1))
    image(0)
    pass_on(0, 4, 1)
    pass_on(0, 2, 0)
    pass_on(0, 1, 0, (3, 0))
    text(0)
    pass_on(1, 4, 1)
    pass_on(1, 2, 0)
    pass_on(1, 1, 0, (3, 0))
    pass_on(0, 2, 1, (6, 1), (3, 1))
    pass_on(1, 1, 1, (5, 1))
    pass_on(0, 4, 0, (5, 0), (6, 0))
    pass_on(0, 1, 1, (5, 1))
    pass_on(1, 4, 0, (5, 0), (6, 0))
    pass_on(1, 2, 1, (6, 1), (3, 1))
    loss = loss_sum(0, ring_copies[0]) + loss_sum(1, ring_copies[1])
    loss = jnp.sum(jnp.sum(loss, 0, keepdims=True), 1, keepdims=True)
    total_rows = block * 2 * SLOTS * SLOTS
    loss_ref[...] = jnp.broadcast_to(loss / (2.0 * total_rows), loss_ref.shape)

    for h, keys in ((0, ((1, 0), (2, 0), (4, 0))), (1, ((4, 1), (1, 1), (2, 1)))):
        r = pl.ds(h * half, half)
        for kind, out in ((0, image_out), (1, text_out)):
            out[r, :] = total_of(kind, 0, h, *keys)

    for kind in (0, 1):
        sent = rows[kind].at[0, pl.ds(0, 14 * half), :]
        remote(sent, sent, gather_send.at[kind], gather_recv.at[kind, 0], sibling).wait_send()
        sent = rows[kind].at[0]
        remote(sent, sent, fwd_send.at[kind], fwd_recv.at[kind, 0], sibling).wait_send()
        sent = sends[kind].at[pl.ds(0, 14 * half), :]
        remote(sent, sent, red_ssem.at[kind], red_rsem.at[kind, 0], sibling).wait_send()
    for c in sum(w_copies, []) + near_copies + ring_copies + [row_out, col_out]:
        c.wait_send()


def finish(image_ref, text_ref, loss_ref, image_sum, text_sum, loss_out, image_out, text_out):
    half_scale = 0.5 * image_ref.shape[1] ** (-0.5)
    image_out[...] = half_scale * (image_sum[...] - 2.0 * text_ref[...].astype(F32))
    text_out[...] = half_scale * (text_sum[...] - 2.0 * image_ref[...].astype(F32))
    loss_out[0, 0] = loss_ref[0, 0]


def on_device(image_embed, text_embed):
    block, width = image_embed.shape
    group = SLOTS * block
    dma = pltpu.SemaphoreType.DMA
    shape = jax.ShapeDtypeStruct
    vmem = pl.BlockSpec(memory_space=pltpu.VMEM)
    loss, image_sum, text_sum = pl.pallas_call(
        kernel,
        out_shape=(
            shape((8, 128), F32),
            shape((block, width), F32),
            shape((block, width), F32),
        ),
        in_specs=[pl.BlockSpec(memory_space=pltpu.HBM)] * 2,
        out_specs=(vmem, vmem, vmem),
        scratch_shapes=[
            pltpu.VMEM((2, group, width), BF16),
            pltpu.VMEM((2, group, width), BF16),
            pltpu.VMEM((4, 4, 2 * block, 4 * block), F32),
            pltpu.VMEM((group, 128), F32),
            pltpu.VMEM((group, 128), F32),
            pltpu.VMEM((8, 2 * group), F32),
            pltpu.VMEM((8, 2 * group), F32),
            pltpu.VMEM((SLOTS, 2 * SLOTS, 128), F32),
            pltpu.VMEM((2 * SLOTS, 2 * SLOTS, 128), F32),
            pltpu.VMEM((SLOTS, 128), F32),
            pltpu.VMEM((2 * SLOTS, 128), F32),
            pltpu.VMEM((group, 128), F32),
            pltpu.VMEM((1, 2 * group), F32),
            pltpu.VMEM((4, group, 2 * block), BF16),
            pltpu.VMEM((4, group, 2 * block), BF16),
            pltpu.VMEM((4, group, 2 * block), BF16),
            pltpu.VMEM((group, width), F32),
            pltpu.VMEM((group, width), F32),
            pltpu.VMEM((group, width), BF16),
            pltpu.VMEM((group, width), BF16),
            pltpu.VMEM((14, block // 2, width), BF16),
            pltpu.VMEM((14, block // 2, width), BF16),
            pltpu.VMEM((4, 8, 128), F32),
            pltpu.VMEM((RING, 8, 128), F32),
            pltpu.VMEM((2, 8, 128), F32),
            pltpu.VMEM((RING, 8, 128), F32),
            dma((2,)),
            dma((2, 14)),
            dma((2,)),
            dma((2, 5)),
            dma((1,)),
            dma((1,)),
            dma((1,)),
            dma((1,)),
            dma((2, 2)),
            dma((2, 2)),
            dma((7,)),
            dma((7,)),
            dma((2,)),
            dma((2, 14)),
            dma((2,)),
        ],
        compiler_params=pltpu.CompilerParams(
            collective_id=0, has_side_effects=True, vmem_limit_bytes=56 * 2**20
        ),
    )(image_embed, text_embed)
    loss, image_grad, text_grad = pl.pallas_call(
        finish,
        out_shape=(
            shape((1, 1), F32),
            shape((block, width), F32),
            shape((block, width), F32),
        ),
        in_specs=[vmem] * 5,
        out_specs=(pl.BlockSpec(memory_space=pltpu.SMEM), vmem, vmem),
    )(image_embed, text_embed, loss, image_sum, text_sum)
    return loss.reshape(()), image_grad, text_grad


def solution(mesh):
    return jax.shard_map(
        on_device,
        mesh=mesh,
        in_specs=(P(("inner", "outer"), None), P(("inner", "outer"), None)),
        out_specs=(P(), P(("inner", "outer"), None), P(("inner", "outer"), None)),
        check_vma=False,
    )
```

```python
import functools
import math

import jax
import jax.numpy as jnp
from jax import lax
from jax.experimental import pallas as pl
from jax.experimental.pallas import tpu as pltpu
from jax.sharding import PartitionSpec as P

F32, BF16 = jnp.float32, jnp.bfloat16
MESH = pl.DeviceIdType.MESH
OFFSETS = ((0, 0), (0, 1), (0, 3), (0, 2), (1, 0), (1, 1), (1, 3), (1, 2))
PLACE = (0, 2, 3, 4, 1, 5, 6, 7)
RING = 4
SLOTS = 8
LOG2E = math.log2(math.e)


def add_up(values):
    return functools.reduce(jnp.add, values)


class Group:
    def __init__(self, kind):
        inner, outer = lax.axis_index("inner"), lax.axis_index("outer")
        core, chip = lax.rem(outer, 2), outer // 2
        high, x = inner // RING, lax.rem(inner, RING)
        low, y = chip // RING, lax.rem(chip, RING)
        self.kind, self.y = kind, y
        self.place = y if kind else x
        self.cores, self.lows, self.highs = (core, 1 - core), (low, 1 - low), (high, 1 - high)
        self.places = [self.place] + [lax.rem(self.place + n, RING) for n in range(1, RING)]

    def index(self, plane_step, ring_step, core_step=0):
        if self.kind == 0:
            return self.highs[plane_step] * RING + self.places[ring_step]
        chip = self.lows[plane_step] * RING + self.places[ring_step]
        return chip * 2 + self.cores[core_step]

    def device(self, plane_step, ring_step, core_step=0):
        index = self.index(plane_step, ring_step, core_step)
        if self.kind:
            return {"outer": index}
        chip = self.lows[plane_step] * RING + self.y
        return {"inner": index, "outer": chip * 2 + self.cores[0]}


def kernel(
    image_ref,
    text_ref,
    loss_ref,
    image_out,
    text_out,
    image_rows,
    text_rows,
    scores,
    row_top,
    row_sum,
    col_top,
    col_sum,
    row_stats,
    col_stats,
    row_lse,
    col_lse,
    row_wide,
    col_wide,
    w_own,
    w_other,
    w_got,
    image_part,
    text_part,
    image_send,
    text_send,
    image_got,
    text_got,
    image_loss,
    image_loss_ring,
    text_loss,
    text_loss_ring,
    gather_send,
    gather_recv,
    fwd_send,
    fwd_recv,
    row_ssem,
    row_rsem,
    col_ssem,
    col_rsem,
    loss_ssem,
    loss_rsem,
    w_ssem,
    w_rsem,
    red_ssem,
    red_rsem,
    load_sem,
):
    block, width = image_ref.shape
    half = block // 2
    pair = 2 * block
    scale = width ** (-0.5)
    inner, outer = lax.axis_index("inner"), lax.axis_index("outer")
    groups = (Group(0), Group(1))
    sibling = {"outer": groups[1].index(0, 0, 1)}
    rows = (image_rows, text_rows)

    def remote(src, dst, ssem, rsem, device):
        return pltpu.make_async_remote_copy(
            src_ref=src,
            dst_ref=dst,
            send_sem=ssem,
            recv_sem=rsem,
            device_id=device,
            device_id_type=MESH,
        )

    RIGHT, LEFT, FAR, PARTNER = (0, 1), (0, 3), (0, 2), (1, 0)
    neighbours = [g.device(*o) for g in groups for o in (RIGHT, LEFT, PARTNER)] + [sibling]

    loads = [
        pltpu.make_async_copy(ref, rows[kind].at[0, pl.ds(0, block), :], load_sem.at[kind])
        for kind, ref in ((0, image_ref), (1, text_ref))
    ]
    for c in loads:
        c.start()
    barrier = pltpu.get_barrier_semaphore()
    for device in neighbours:
        pl.semaphore_signal(barrier, inc=1, device_id=device, device_id_type=MESH)

    row_top[...] = jnp.full(row_top.shape, -1e30, F32)
    row_sum[...] = jnp.zeros(row_sum.shape, F32)
    col_top[...] = jnp.full(col_top.shape, -1e30, F32)
    col_sum[...] = jnp.zeros(col_sum.shape, F32)
    for c in loads:
        c.wait()
    pl.semaphore_wait(barrier, len(neighbours))

    away = sorted(OFFSETS[1:], key=lambda o: -(o[0] + min(o[1], RING - o[1])))
    inner_peers = [groups[0].device(*o) for o in away]
    outer_peers = [groups[1].device(*o, c) for o in away for c in (1, 0)] + [sibling]

    def at(kind, core_step, slot, part=None):
        start, size = PLACE[slot] * block, block
        if part is not None:
            start, size = start + part * half, half
        return rows[kind].at[core_step, pl.ds(start, size), :]

    def copy(kind, src, slot, part, offset):
        n = 2 * (slot - 1) + part
        return remote(
            src,
            at(kind, 0, slot, part),
            gather_send.at[kind],
            gather_recv.at[kind, n],
            groups[kind].device(*offset),
        )

    def gather_copies(kind):
        out = {
            (3, 0): copy(kind, at(kind, 0, 2, 0), 3, 0, RIGHT),
            (3, 1): copy(kind, at(kind, 0, 1, 1), 3, 1, LEFT),
            (6, 0): copy(kind, at(kind, 0, 4, 0), 6, 0, RIGHT),
            (5, 0): copy(kind, at(kind, 0, 4, 0), 5, 0, LEFT),
            (7, 0): copy(kind, at(kind, 0, 6, 0), 7, 0, RIGHT),
            (5, 1): copy(kind, at(kind, 0, 1, 1), 5, 1, PARTNER),
            (6, 1): copy(kind, at(kind, 0, 2, 1), 6, 1, PARTNER),
            (7, 1): copy(kind, at(kind, 0, 3, 1), 7, 1, PARTNER),
        }
        for h in (0, 1):
            mine = at(kind, 0, 0, h)
            for slot, offset in ((2, RIGHT), (1, LEFT), (4, PARTNER)):
                out[slot, h] = copy(kind, mine, slot, h, offset)
        return out

    PARCELS = ((0, 2), (2, 2), (4, 2), (6, 1), (7, 1))

    def fwd(kind, n):
        first, count = PARCELS[n]
        here = pl.ds(first * block, count * block)
        return remote(
            rows[kind].at[0, here, :],
            rows[kind].at[1, here, :],
            fwd_send.at[kind],
            fwd_recv.at[kind, n],
            sibling,
        )

    copies = [gather_copies(kind) for kind in (0, 1)]
    fwds = [[fwd(kind, n) for n in range(len(PARCELS))] for kind in (0, 1)]

    def start(*keys):
        for key in keys:
            for kind in (0, 1):
                copies[kind][key].start()

    def arrived(*keys):
        for key in keys:
            for kind in (0, 1):
                copies[kind][key].wait_recv()

    def forward(*parcels):
        for n in parcels:
            for kind in (1, 0):
                fwds[kind][n].start()

    start((4, 0), (2, 1), (1, 1), (4, 1), (2, 0), (1, 0))

    mine = pl.ds(0, block)
    product = image_rows[0, mine, :].astype(F32) * text_rows[0, mine, :].astype(F32)
    positive = scale * jnp.sum(product, 0, keepdims=True)
    positive = add_up(positive[:, i : i + 128] for i in range(0, width, 128))

    def multiply(a, b, c):
        image = image_rows[0, pl.ds(a * pair, pair), :]
        text = text_rows[c, pl.ds(b * pair, pair), :]
        scores[a, b, :, pl.ds(c * pair, pair)] = (scale * LOG2E) * lax.dot_general(
            image, text, (((1,), (1,)), ((), ())), preferred_element_type=F32
        )

    def count(a, b, c):
        step = 32
        k = pl.ds((2 * b + c) * pair, pair)
        old = col_top[:, k]
        top = old
        for r in range(0, pair, step):
            value = scores[a, b, pl.ds(r, step), pl.ds(c * pair, pair)]
            top = jnp.maximum(top, jnp.max(value.reshape(step // 8, 8, pair), 0))
        total = col_sum[:, k] * jnp.exp2(old - top)
        for r in range(0, pair, step):
            value = scores[a, b, pl.ds(r, step), pl.ds(c * pair, pair)]
            here = pl.ds(a * pair + r, step)
            lanes = [value[:, i : i + 128] for i in range(0, pair, 128)]
            before = row_top[here, :]
            row = functools.reduce(jnp.maximum, lanes, before)
            row_sum[here, :] = row_sum[here, :] * jnp.exp2(before - row) + add_up(
                [jnp.exp2(lane - row) for lane in lanes]
            )
            row_top[here, :] = row
            value = value.reshape(step // 8, 8, pair)
            total = total + jnp.sum(jnp.exp2(value - top[None]), 0)
        col_top[:, k] = top
        col_sum[:, k] = total

    waiting = []

    def tiles(todo):
        for tile in todo:
            multiply(*tile)
            if waiting:
                count(*waiting.pop())
            waiting.append(tile)

    def shell(n, *parcels):
        tiles([(n, b, c) for b in range(n) for c in (0, 1)])
        tiles([(a, n, 0) for a in range(n + 1)])
        sib_arrived(*parcels)
        tiles([(a, n, 1) for a in range(n + 1)])

    def sib_arrived(*parcels):
        for n in parcels:
            fwds[1][n].wait_recv()

    arrived((1, 1))
    start((3, 1), (5, 1))
    arrived((4, 0))
    start((6, 0), (5, 0))
    arrived((2, 1))
    start((6, 1))
    arrived((2, 0))
    start((3, 0))
    arrived((1, 0))
    arrived((4, 1))
    forward(0, 1)
    arrived((3, 1))
    start((7, 1))
    arrived((6, 0))
    start((7, 0))
    shell(0, 0)
    shell(1, 1)
    arrived((3, 0), (5, 0), (5, 1))
    forward(2)
    arrived((6, 1))
    forward(3)
    shell(2, 2)
    for kind in (1, 0):
        for h in (1, 0):
            copies[kind][7, h].wait_recv()
        fwds[kind][4].start()
    shell(3, 3, 4)
    count(*waiting.pop())

    def lse(top, total):
        most = jnp.max(top, 0, keepdims=True)
        total = jnp.sum(total * jnp.exp2(top - most), 0, keepdims=True)
        return most + LOG2E * jnp.log(total)

    for slot, offset in enumerate(OFFSETS):
        place = PLACE[slot]
        for c in (0, 1):
            o = groups[1].index(*offset, c)
            k = pl.ds((place // 2) * 2 * pair + c * pair + (place % 2) * block, block)
            col_stats[outer, pl.ds(o, 1), :] = lse(col_top[:, k], col_sum[:, k])
    for slot, offset in enumerate(OFFSETS):
        i = groups[0].index(*offset)
        r = pl.ds(PLACE[slot] * block, block)
        row_stats[inner, pl.ds(i, 1), :] = lse(
            jnp.transpose(row_top[r, :]), jnp.transpose(row_sum[r, :])
        )
    row_stats[inner, pl.ds(SLOTS, 8), :] = jnp.concatenate(
        [positive, jnp.zeros((7, 128), F32)], 0
    )

    def spread(ref, me, ssem, rsem, peers):
        for device in peers:
            remote(ref.at[me], ref.at[me], ssem, rsem, device).start()
        every = ref.at[pl.ds(0, len(peers))]
        return remote(every, every, ssem, rsem, sibling)

    col_out = spread(col_stats, outer, col_ssem.at[0], col_rsem.at[0], outer_peers)
    row_out = spread(row_stats, inner, row_ssem.at[0], row_rsem.at[0], inner_peers)
    row_out.wait_recv()
    col_out.wait_recv()

    def combine(ref, count):
        values = [ref[n, 0:count, :] for n in range(count)]
        top = functools.reduce(jnp.maximum, values)
        return top + LOG2E * jnp.log(add_up([jnp.exp2(value - top) for value in values]))

    row_value = combine(row_stats, SLOTS)
    col_value = combine(col_stats, 2 * SLOTS)
    row_lse[...] = row_value
    col_lse[...] = col_value
    for slot, offset in enumerate(OFFSETS):
        i = groups[0].index(*offset)
        line = row_lse[pl.ds(i, 1), :]
        place = PLACE[slot]
        row_wide[pl.ds(place * block, block), :] = jnp.transpose(
            jnp.broadcast_to(line, (block, block))
        )
        for c in (0, 1):
            o = groups[1].index(*offset, c)
            k = pl.ds((place // 2) * 2 * pair + c * pair + (place % 2) * block, block)
            col_wide[:, k] = col_lse[pl.ds(o, 1), :]

    def weigh(a, b):
        step = 32
        for r in range(0, pair, step):
            here = pl.ds(a * pair + r, step)
            line = jnp.concatenate([row_wide[here, :]] * 2, 1)
            for c, out in ((0, w_own), (1, w_other)):
                value = scores[a, b, pl.ds(r, step), pl.ds(c * pair, pair)]
                there = pl.ds((2 * b + c) * pair, pair)
                weight = jnp.exp2(value - line) + jnp.exp2(value - col_wide[:, there])
                out[b, here, :] = weight.astype(BF16)

    def w_copy(n, b, r):
        return remote(w_other.at[b, r, :], w_got.at[b, r, :], w_ssem.at[n], w_rsem.at[n], sibling)

    w_copies = [[w_copy(b, b, pl.ds(0, 4 * pair))] for b in range(3)]
    w_copies.append([w_copy(3 + a, 3, pl.ds(a * pair, pair)) for a in range(4)])

    weighed = set()

    def weigh_jobs(g):
        todo = [t for t in [(a, g) for a in range(4)] + [(g, b) for b in range(4)] if t not in weighed]
        todo = sorted(set(todo), key=todo.index)
        weighed.update(todo)
        return [functools.partial(weigh, *t) for t in todo]

    paired = add_up([row_stats[n, pl.ds(SLOTS, 8), :] for n in range(SLOTS)])
    shares = (
        row_value * (1.0 / LOG2E) - 2.0 * paired,
        (col_value[0:8] + col_value[8:16]) * (1.0 / LOG2E),
    )
    high, low, core = groups[0].highs[0], groups[0].lows[0], groups[0].cores[0]
    who = (2 * lax.rem(high + low, 2) + core, high)
    others = (
        [groups[1].device(1, 0, 1), groups[1].device(*PARTNER), sibling],
        [groups[0].device(*PARTNER)],
    )
    losses = ((image_loss, image_loss_ring), (text_loss, text_loss_ring))

    def loss_near(kind):
        losses[kind][0][who[kind]] = shares[kind]
        return spread(
            losses[kind][0], who[kind], loss_ssem.at[kind, 0], loss_rsem.at[kind, 0], others[kind]
        )

    def loss_ring(kind, near):
        group = groups[1 - kind]
        near.wait_recv()
        ref = losses[kind][0]
        losses[kind][1][group.place] = add_up([ref[n] for n in range(ref.shape[0])])
        return spread(
            losses[kind][1],
            group.place,
            loss_ssem.at[kind, 1],
            loss_rsem.at[kind, 1],
            [group.device(0, n) for n in (2, 1, 3)],
        )

    def loss_sum(kind, ring):
        ring.wait_recv()
        return add_up([losses[kind][1][n] for n in range(RING)])

    parts = (image_part, text_part)
    sends = (image_send, text_send)
    gots = (image_got, text_got)

    def lines(slot, h):
        return pl.ds(PLACE[slot] * block + h * half, half)

    def red_copies(kind):
        way = {(7, 0): RIGHT, (5, 0): RIGHT, (6, 0): LEFT, (3, 0): RIGHT, (3, 1): LEFT}
        way.update({(1, h): RIGHT for h in (0, 1)})
        way.update({(2, h): LEFT for h in (0, 1)})
        way.update({(slot, 1): PARTNER for slot in (4, 5, 6, 7)})
        way[4, 0] = PARTNER
        return {
            key: remote(
                sends[kind].at[lines(*key), :],
                gots[kind].at[n],
                red_ssem.at[kind],
                red_rsem.at[kind, n],
                groups[kind].device(*way[key]),
            )
            for n, key in enumerate(sorted(way))
        }

    reds = [red_copies(kind) for kind in (0, 1)]
    numbers = {key: n for n, key in enumerate(sorted(reds[0]))}

    def total_of(kind, slot, h, *keys):
        value = parts[kind][lines(slot, h), :]
        for key in keys:
            reds[kind][key].wait_recv()
            value = value + gots[kind][numbers[key]].astype(F32)
        return value

    READY = {(7, 0), (7, 1), (6, 0), (6, 1), (3, 0), (5, 1), (2, 0), (4, 1)}

    def pass_on(kind, slot, h, *keys):
        if (slot, h) not in READY:
            sends[kind][lines(slot, h), :] = total_of(kind, slot, h, *keys).astype(BF16)
        reds[kind][slot, h].start()

    def product(kind, g, jobs=()):
        chunks = width // pair
        for n in range(chunks):
            k = pl.ds(n * pair, pair)
            if kind == 0:
                value = add_up(
                    [
                        jnp.dot(
                            jnp.concatenate([w[b, pl.ds(g * pair, pair), :] for b in range(4)], 1),
                            text_rows[c, :, k],
                            preferred_element_type=F32,
                        )
                        for c, w in ((0, w_own), (1, w_other))
                    ]
                )
            else:
                value = add_up(
                    [
                        lax.dot_general(
                            w[g],
                            image_rows[c, :, k],
                            (((0,), (0,)), ((), ())),
                            preferred_element_type=F32,
                        )
                        for c, w in ((0, w_own), (1, w_got))
                    ]
                )
            for job in jobs[n::chunks]:
                job()
            for i in range(4):
                slot, h = PLACE.index(2 * g + i // 2), i % 2
                piece = value[i * half : (i + 1) * half]
                if (slot, h) in READY:
                    sends[kind][lines(slot, h), k] = piece.astype(BF16)
                else:
                    parts[kind][lines(slot, h), k] = piece

    def image(g, beside=None):
        product(0, g, weigh_jobs(beside) if beside is not None else ())
        if beside is not None:
            for c in w_copies[beside]:
                c.start()

    def text(g, beside=None):
        for c in w_copies[g]:
            c.wait_recv()
        product(1, g, weigh_jobs(beside) if beside is not None else ())
        if beside is not None:
            for c in w_copies[beside]:
                c.start()

    for n, job in enumerate(weigh_jobs(3)):
        job()
        if n < 4:
            w_copies[3][n].start()
    product(0, 3, weigh_jobs(2))
    pass_on(0, 7, 1)
    pass_on(0, 7, 0)
    w_copies[2][0].start()
    near_copies = [loss_near(kind) for kind in (0, 1)]
    pass_on(0, 6, 0)
    pass_on(0, 6, 1)
    for c in fwds[0]:
        c.wait_recv()
    text(3, 1)
    pass_on(1, 7, 1)
    pass_on(1, 7, 0)
    image(2, 0)
    pass_on(0, 3, 0)
    pass_on(1, 6, 0)
    text(2)
    ring_copies = [loss_ring(0, near_copies[0])]
    pass_on(0, 5, 1)
    pass_on(1, 3, 0)
    pass_on(1, 5, 1)
    text(1)
    ring_copies.append(loss_ring(1, near_copies[1]))
    pass_on(0, 5, 0, (7, 0))
    pass_on(1, 6, 1)
    image(1)
    pass_on(1, 5, 0, (7, 0))
    pass_on(0, 3, 1, (7, 1))
    pass_on(1, 3, 1, (7, 1))
    image(0)
    pass_on(0, 4, 1)
    pass_on(0, 2, 0)
    text(0)
    pass_on(1, 4, 1)
    pass_on(0, 1, 0, (3, 0))
    pass_on(1, 1, 0, (3, 0))
    pass_on(1, 2, 0)
    pass_on(0, 4, 0, (5, 0), (6, 0))
    pass_on(1, 1, 1, (5, 1))
    pass_on(0, 1, 1, (5, 1))
    pass_on(1, 4, 0, (5, 0), (6, 0))
    pass_on(0, 2, 1, (6, 1), (3, 1))
    pass_on(1, 2, 1, (6, 1), (3, 1))
    loss = loss_sum(0, ring_copies[0]) + loss_sum(1, ring_copies[1])
    loss = jnp.sum(jnp.sum(loss, 0, keepdims=True), 1, keepdims=True)
    total_rows = block * 2 * SLOTS * SLOTS
    loss_ref[...] = jnp.broadcast_to(loss / (2.0 * total_rows), loss_ref.shape)

    for h, keys in ((0, ((1, 0), (2, 0), (4, 0))), (1, ((4, 1), (1, 1), (2, 1)))):
        r = pl.ds(h * half, half)
        for kind, out in ((0, image_out), (1, text_out)):
            out[r, :] = total_of(kind, 0, h, *keys)

    for kind in (0, 1):
        sent = rows[kind].at[0, pl.ds(0, 14 * half), :]
        remote(sent, sent, gather_send.at[kind], gather_recv.at[kind, 0], sibling).wait_send()
        sent = rows[kind].at[0]
        remote(sent, sent, fwd_send.at[kind], fwd_recv.at[kind, 0], sibling).wait_send()
        sent = sends[kind].at[pl.ds(0, 14 * half), :]
        remote(sent, sent, red_ssem.at[kind], red_rsem.at[kind, 0], sibling).wait_send()
    for c in sum(w_copies, []) + near_copies + ring_copies + [row_out, col_out]:
        c.wait_send()


def finish(image_ref, text_ref, loss_ref, image_sum, text_sum, loss_out, image_out, text_out):
    half_scale = 0.5 * image_ref.shape[1] ** (-0.5)
    image_out[...] = half_scale * (image_sum[...] - 2.0 * text_ref[...].astype(F32))
    text_out[...] = half_scale * (text_sum[...] - 2.0 * image_ref[...].astype(F32))
    loss_out[0, 0] = loss_ref[0, 0]


def on_device(image_embed, text_embed):
    block, width = image_embed.shape
    group = SLOTS * block
    dma = pltpu.SemaphoreType.DMA
    shape = jax.ShapeDtypeStruct
    vmem = pl.BlockSpec(memory_space=pltpu.VMEM)
    loss, image_sum, text_sum = pl.pallas_call(
        kernel,
        out_shape=(
            shape((8, 128), F32),
            shape((block, width), F32),
            shape((block, width), F32),
        ),
        in_specs=[pl.BlockSpec(memory_space=pltpu.HBM)] * 2,
        out_specs=(vmem, vmem, vmem),
        scratch_shapes=[
            pltpu.VMEM((2, group, width), BF16),
            pltpu.VMEM((2, group, width), BF16),
            pltpu.VMEM((4, 4, 2 * block, 4 * block), F32),
            pltpu.VMEM((group, 128), F32),
            pltpu.VMEM((group, 128), F32),
            pltpu.VMEM((8, 2 * group), F32),
            pltpu.VMEM((8, 2 * group), F32),
            pltpu.VMEM((SLOTS, 2 * SLOTS, 128), F32),
            pltpu.VMEM((2 * SLOTS, 2 * SLOTS, 128), F32),
            pltpu.VMEM((SLOTS, 128), F32),
            pltpu.VMEM((2 * SLOTS, 128), F32),
            pltpu.VMEM((group, 128), F32),
            pltpu.VMEM((1, 2 * group), F32),
            pltpu.VMEM((4, group, 2 * block), BF16),
            pltpu.VMEM((4, group, 2 * block), BF16),
            pltpu.VMEM((4, group, 2 * block), BF16),
            pltpu.VMEM((group, width), F32),
            pltpu.VMEM((group, width), F32),
            pltpu.VMEM((group, width), BF16),
            pltpu.VMEM((group, width), BF16),
            pltpu.VMEM((14, block // 2, width), BF16),
            pltpu.VMEM((14, block // 2, width), BF16),
            pltpu.VMEM((4, 8, 128), F32),
            pltpu.VMEM((RING, 8, 128), F32),
            pltpu.VMEM((2, 8, 128), F32),
            pltpu.VMEM((RING, 8, 128), F32),
            dma((2,)),
            dma((2, 14)),
            dma((2,)),
            dma((2, 5)),
            dma((1,)),
            dma((1,)),
            dma((1,)),
            dma((1,)),
            dma((2, 2)),
            dma((2, 2)),
            dma((7,)),
            dma((7,)),
            dma((2,)),
            dma((2, 14)),
            dma((2,)),
        ],
        compiler_params=pltpu.CompilerParams(
            collective_id=0, has_side_effects=True, vmem_limit_bytes=56 * 2**20
        ),
    )(image_embed, text_embed)
    loss, image_grad, text_grad = pl.pallas_call(
        finish,
        out_shape=(
            shape((1, 1), F32),
            shape((block, width), F32),
            shape((block, width), F32),
        ),
        in_specs=[vmem] * 5,
        out_specs=(pl.BlockSpec(memory_space=pltpu.SMEM), vmem, vmem),
    )(image_embed, text_embed, loss, image_sum, text_sum)
    return loss.reshape(()), image_grad, text_grad


def solution(mesh):
    return jax.shard_map(
        on_device,
        mesh=mesh,
        in_specs=(P(("inner", "outer"), None), P(("inner", "outer"), None)),
        out_specs=(P(), P(("inner", "outer"), None), P(("inner", "outer"), None)),
        check_vma=False,
    )
```
